32 devices in a mesh: dp: 16 (over z, y, x), tensor: 2 (over core).
Axes of the slice: x: 2, y: 2, z: 4, core: 2. Of those that a mesh axis runs over, the one named last changes fastest.
Arguments:
- tokens: bfloat16 [32768, 768], P(('dp', 'tensor')), may hold values from -6 to 6
- pre_gain: bfloat16 [768], replicated, may hold values from 0.5 to 1.5
- w_zx: bfloat16 [768, 2, 1536], P('dp', None, 'tensor'), may hold values from -0.21875 to 0.21875
- w_bc: bfloat16 [768, 256], P('dp'), may hold values from -0.21875 to 0.21875
- w_dt: bfloat16 [768, 24], P('dp', 'tensor'), may hold values from -0.21875 to 0.21875
- conv_x: bfloat16 [5, 1536], P(None, 'tensor'), may hold values from -3 to 3
- conv_bc: bfloat16 [5, 256], replicated, may hold values from -3 to 3
- a_log: float32 [24], P('tensor'), may hold values from -3 to 1
- dt_bias: float32 [24], P('tensor'), may hold values from -5 to -1
- skip_gain: float32 [24], P('tensor'), may hold values from 0.5 to 1.5
- norm_gain: bfloat16 [1536], P('tensor'), may hold values from 0.5 to 1.5
- w_out: bfloat16 [1536, 768], P('tensor', 'dp'), may hold values from -0.15625 to 0.15625
- cotangent: bfloat16 [32768, 768], P(('dp', 'tensor')), may hold values from -6 to 6
Outputs:
- out: bfloat16 [32768, 768], P(('dp', 'tensor'))
- grad_tokens: bfloat16 [32768, 768], P(('dp', 'tensor'))
- grad_pre_gain: float32 [768], replicated
- grad_w_zx: float32 [768, 2, 1536], P('dp', None, 'tensor')
- grad_w_bc: float32 [768, 256], P('dp')
- grad_w_dt: float32 [768, 24], P('dp', 'tensor')
- grad_conv_x: float32 [5, 1536], P(None, 'tensor')
- grad_conv_bc: float32 [5, 256], replicated
- grad_a_log: float32 [24], P('tensor')
- grad_dt_bias: float32 [24], P('tensor')
- grad_skip_gain: float32 [24], P('tensor')
- grad_norm_gain: float32 [1536], P('tensor')
- grad_w_out: float32 [1536, 768], P('tensor', 'dp')
The draws below stay inside these ranges and needn't reach their ends.
All inputs are finite; a program needn't handle non-finite values.
Results may differ from the reference program's by a relative error of at most 0.014.
Values may be sent and summed in bfloat16 or wider, within the bound.
No kernel may reach another device: no remote copies, remote signals or barrier semaphores. Data moves between devices by JAX's collectives and lax.ppermute only.
A program may use at most 256 MiB of HBM per device.

```python
import jax
import jax.numpy as jnp
from jax import lax

D = 768
HEADS = 24
STATE = 128
CONV = 4
BLOCK = 256
LEN = 1024
INNER = 1536
TOKENS = 32768


def levels(rng, dims, pieces, low, high):
    loudness = 1.0
    for position, parts in pieces:
        steps = jax.random.uniform(jax.random.fold_in(jax.random.fold_in(rng, 6), position), (parts,), jnp.float32, low / len(pieces), high / len(pieces))
        loudness = loudness * jnp.repeat(jnp.exp(steps), dims[position] // parts).reshape((-1,) + (1,) * (len(dims) - 1 - position))
    return loudness


def gaussian(stream_key, dims, spread, limit, cuts=(), kind=jnp.bfloat16):
    entries = spread * jax.random.normal(stream_key, dims, jnp.float32)
    if cuts:
        entries = entries * levels(stream_key, dims, cuts, -0.22, 0.18)
    return jnp.clip(entries, -limit, limit).astype(kind)


def setup_inputs(seed: int = 0) -> dict:
    streams_of = jax.random.split(jax.random.key(seed), 14)
    return {
        "tokens": gaussian(streams_of[0], (TOKENS, D), 1.0, 6.0, ((0, 32),)),
        "pre_gain": jnp.clip(1.0 + 0.1 * jax.random.normal(streams_of[1], (D,), jnp.float32), 0.5, 1.5).astype(jnp.bfloat16),
        "w_zx": gaussian(streams_of[2], (D, 2, INNER), D ** -0.5, 0.21875, ((0, 16), (2, 2))),
        "w_bc": gaussian(streams_of[3], (D, 2 * STATE), D ** -0.5, 0.21875, ((0, 16),)),
        "w_dt": gaussian(streams_of[4], (D, HEADS), D ** -0.5, 0.21875, ((0, 16), (1, 2))),
        "conv_x": gaussian(streams_of[5], (CONV + 1, INNER), 0.5, 3.0, ((1, 2),)),
        "conv_bc": gaussian(streams_of[6], (CONV + 1, 2 * STATE), 0.5, 3.0),
        "a_log": jnp.clip(-3.0 + 4.0 * jax.random.uniform(streams_of[7], (HEADS,), jnp.float32) ** levels(streams_of[7], (HEADS,), ((0, 2),), -0.2, 0.2), -3.0, 1.0),
        "dt_bias": jnp.clip(-5.0 + 4.0 * jax.random.uniform(streams_of[8], (HEADS,), jnp.float32) ** levels(streams_of[8], (HEADS,), ((0, 2),), -0.2, 0.2), -5.0, -1.0),
        "skip_gain": jnp.clip(0.5 + 1.0 * jax.random.uniform(streams_of[9], (HEADS,), jnp.float32) ** levels(streams_of[9], (HEADS,), ((0, 2),), -0.2, 0.2), 0.5, 1.5),
        "norm_gain": jnp.clip(1.0 + 0.1 * jax.random.normal(streams_of[10], (INNER,), jnp.float32), 0.5, 1.5).astype(jnp.bfloat16),
        "w_out": gaussian(streams_of[11], (INNER, D), INNER ** -0.5, 0.15625, ((0, 2), (1, 16))),
        "cotangent": gaussian(streams_of[12], (TOKENS, D), 1.0, 6.0, ((0, 32),)),
    }


epsilon = 1e-05
precise = lax.Precision.HIGHEST
per_group = 4

@jax.custom_vjp
def low(v):
    return lax.optimization_barrier(v.astype(jnp.bfloat16)).astype(jnp.float32)

@jax.custom_vjp
def low_back(v):
    return v

def low_keep(v):
    return (low(v), None)

def low_pass(kept, grad):
    return (grad,)

def back_keep(v):
    return (v, None)

def back_low(kept, grad):
    return (low(grad),)
low.defvjp(low_keep, low_pass)
low_back.defvjp(back_keep, back_low)

def causal_conv(values, kernel):
    tap_count = kernel.shape[0] - 1
    length = values.shape[0]
    padded = jnp.pad(values, ((tap_count - 1, 0), (0, 0)))
    result = kernel[tap_count] + jnp.zeros_like(values)
    for tap_index in range(tap_count):
        result = result + kernel[tap_index] * padded[tap_index:tap_index + length]
    return result

def state_space(x_scaled, decay_rate, b_input, c_input):
    length, head_count, head_dim = x_scaled.shape
    block_count = length // BLOCK
    x_blocks = x_scaled.reshape(block_count, BLOCK, head_count, head_dim)
    b_blocks = b_input.reshape(block_count, BLOCK, -1)
    c_blocks = c_input.reshape(block_count, BLOCK, -1)
    cumulative = jnp.cumsum(decay_rate.reshape(block_count, BLOCK, head_count), axis=1)
    by_head = jnp.swapaxes(cumulative, 1, 2)
    gaps = by_head[:, :, :, None] - by_head[:, :, None, :]
    lower_mask = jnp.arange(BLOCK)[:, None] >= jnp.arange(BLOCK)[None, :]
    decay_matrix = jnp.exp(jnp.where(lower_mask, gaps, -1e+30))
    intersection = jnp.einsum('kin,kjn->kij', c_blocks, b_blocks, precision=precise)
    weighted = decay_matrix * intersection[:, None, :, :]
    local_part = jnp.einsum('khij,kjhp->kihp', weighted, x_blocks, precision=precise)
    tail_decay = jnp.exp(cumulative[:, -1:, :] - cumulative)
    block_states = jnp.einsum('kjhp,kjn->khpn', x_blocks * tail_decay[..., None], b_blocks, precision=precise)

    def carry_step(state, inputs):
        block_state, block_total = inputs
        return (jnp.exp(block_total)[:, None, None] * state + block_state, state)
    zero_state = jnp.zeros(block_states.shape[1:], x_scaled.dtype)
    _, entering = lax.scan(carry_step, zero_state, (block_states, cumulative[:, -1, :]))
    carried = jnp.einsum('kin,khpn->kihp', c_blocks, entering, precision=precise) * jnp.exp(cumulative)[..., None]
    return (local_part + carried).reshape(length, head_count, head_dim)

def mixer_core(zx_seq, bc_seq, dt_seq, conv_x, conv_bc, a_log, dt_bias, skip_gain):
    head_count = dt_seq.shape[1]
    x_conv = jax.nn.silu(causal_conv(zx_seq[:, 1], conv_x))
    b_conv = jax.nn.silu(causal_conv(bc_seq, conv_bc))
    state_width = b_conv.shape[1] // 2
    step_size = jax.nn.softplus(dt_seq + dt_bias)
    decay_rate = -step_size * jnp.exp(a_log)
    x_heads = x_conv.reshape(x_conv.shape[0], head_count, -1)
    scanned = state_space(x_heads * step_size[:, :, None], decay_rate, b_conv[:, :state_width], b_conv[:, state_width:])
    scanned = scanned + skip_gain[:, None] * x_heads
    return scanned.reshape(x_conv.shape) * jax.nn.silu(zx_seq[:, 0])

def mix_group(group_rows, weights):
    pre_gain, w_zx, w_bc, w_dt, conv_x, conv_bc, a_log, dt_bias, skip_gain, norm_gain, w_out = weights
    mean_square = lax.optimization_barrier(jnp.mean(group_rows * group_rows, axis=1, keepdims=True))
    normed = low(group_rows * lax.rsqrt(mean_square + epsilon) * pre_gain)
    inner_width = w_zx.shape[2]
    zx_proj = low_back(jnp.dot(normed, w_zx.reshape(w_zx.shape[0], 2 * inner_width), precision=precise))
    bc_proj = low_back(jnp.dot(normed, w_bc, precision=precise))
    dt_proj = low_back(jnp.dot(normed, w_dt, precision=precise))
    seq_count = group_rows.shape[0] // LEN
    per_seq = jax.vmap(mixer_core, in_axes=(0, 0, 0, None, None, None, None, None))
    gated = per_seq(zx_proj.reshape(seq_count, LEN, 2, inner_width), bc_proj.reshape(seq_count, LEN, -1), dt_proj.reshape(seq_count, LEN, -1), conv_x, conv_bc, a_log, dt_bias, skip_gain)
    gated = gated.reshape(group_rows.shape[0], inner_width)
    inv_rows = lax.rsqrt(lax.optimization_barrier(jnp.mean(gated * gated, axis=1, keepdims=True)) + epsilon)
    mixed = low(gated * inv_rows * norm_gain)
    return jnp.dot(mixed, w_out, precision=precise)

def reference(tokens, pre_gain, w_zx, w_bc, w_dt, conv_x, conv_bc, a_log, dt_bias, skip_gain, norm_gain, w_out, cotangent):
    x_full = tokens.astype(jnp.float32)
    weights = tuple((weight_in.astype(jnp.float32) for weight_in in (pre_gain, w_zx, w_bc, w_dt, conv_x, conv_bc, a_log, dt_bias, skip_gain, norm_gain, w_out)))

    def forward(x_rows, params):
        grouped = x_rows.reshape(-1, per_group * LEN, x_rows.shape[1])

        def one_group(group_rows):
            return mix_group(group_rows, params)
        branch = lax.map(jax.checkpoint(one_group), grouped)
        return x_rows + branch.reshape(x_rows.shape)
    result, pullback = jax.vjp(forward, x_full, weights)
    grad_rows, grad_params = pullback(cotangent.astype(jnp.float32))
    grad_pre, grad_zx, grad_bc, grad_dt, grad_convx, grad_convbc, grad_alog, grad_bias, grad_skip, grad_norm, grad_out = grad_params
    return (result.astype(jnp.bfloat16), grad_rows.astype(jnp.bfloat16), grad_pre, grad_zx, grad_bc, grad_dt, grad_convx, grad_convbc, grad_alog, grad_bias, grad_skip, grad_norm, grad_out)
```

```python
import functools

import jax
import jax.numpy as jnp
from jax import lax
from jax.experimental import pallas as pl
from jax.experimental.pallas import tpu as pltpu
from jax.sharding import PartitionSpec as P

LEN = 1024
Q = 128
HEAD = 64
STATE = 128
epsilon = 1e-05
f32 = jnp.float32
b16 = jnp.bfloat16
exact = lax.Precision.HIGHEST
VMEM = 56 * 1024 * 1024


def nn(a, b, precision=None):
    return lax.dot_general(
        a, b, (((1,), (0,)), ((), ())), preferred_element_type=f32, precision=precision
    )


def nt(a, b, precision=None):
    return lax.dot_general(
        a, b, (((1,), (1,)), ((), ())), preferred_element_type=f32, precision=precision
    )


def tn(a, b):
    return lax.dot_general(a, b, (((0,), (0,)), ((), ())), preferred_element_type=f32)


def sigmoid(v):
    return 0.5 * jnp.tanh(0.5 * v) + 0.5


def softplus(v):
    return jnp.maximum(v, 0.0) + jnp.log1p(jnp.exp(-jnp.abs(v)))


def conv(ref, taps, lanes):
    total = taps[4:5, lanes]
    for k in range(4):
        total = total + taps[k : k + 1, lanes] * ref[5 + k : 5 + k + Q, lanes]
    return total


def iota(axis):
    return lax.broadcasted_iota(jnp.int32, (Q, Q), axis)


def head_rates(dt_raw, heads_ref, low_tri):
    step = softplus(dt_raw + heads_ref[0:1, :])
    decay = -step * heads_ref[1:2, :]
    cum = nn(low_tri, decay, exact)
    return step, decay, cum


def scan_forward_kernel(
    per_seq, pairs,
    xin_ref, xhalo_ref, bd_ref, bdhalo_ref, cx_ref, cb_ref, heads_ref,
    y_ref, state_out_ref,
    state, xs, bs, xt, carried,
):
    first = (pl.program_id(0) % per_seq) == 0

    @pl.when(first)
    def _():
        state[...] = jnp.zeros_like(state)

    keep = jnp.where(first, 0.0, 1.0)
    xs[0:8, :] = xhalo_ref[...].astype(f32)[8:16, :] * keep
    xs[8 : 8 + Q, :] = xin_ref[...].astype(f32)
    bs[0:8, :] = bdhalo_ref[:, : 2 * STATE] * keep
    bs[8 : 8 + Q, :] = bd_ref[:, : 2 * STATE]
    rows, cols = iota(0), iota(1)
    lower = rows >= cols
    low_tri = jnp.where(lower, 1.0, 0.0).astype(f32)
    left = cols < HEAD
    pre_bc = conv(bs, cb_ref, slice(0, 2 * STATE))
    bc = pre_bc * sigmoid(pre_bc)
    b_low, c_low = bc[:, :STATE].astype(b16), bc[:, STATE:].astype(b16)
    gram = jnp.where(lower, nt(c_low, b_low), 0.0)
    step, decay, cum = head_rates(bd_ref[:, 2 * STATE :], heads_ref, low_tri)
    cum_rows = cum.T
    held = state[...].astype(b16)
    state_out_ref[0] = held
    carried[...] = nn(c_low, held)
    for p in range(pairs):
        sl = slice(p * Q, (p + 1) * Q)
        pre = conv(xs, cx_ref, sl)
        x = pre * sigmoid(pre)
        step2 = jnp.where(left, step[:, 2 * p : 2 * p + 1], step[:, 2 * p + 1 : 2 * p + 2])
        scaled = x * step2
        c0 = jnp.broadcast_to(cum[:, 2 * p : 2 * p + 1], (Q, Q))
        c1 = jnp.broadcast_to(cum[:, 2 * p + 1 : 2 * p + 2], (Q, Q))
        w0 = jnp.exp(jnp.minimum(c0 - cum_rows[2 * p : 2 * p + 1, :], 0.0)) * gram
        w1 = jnp.exp(jnp.minimum(c1 - cum_rows[2 * p + 1 : 2 * p + 2, :], 0.0)) * gram
        weights = jnp.concatenate([w0.astype(b16), w1.astype(b16)], axis=1)
        split = jnp.concatenate(
            [jnp.where(left, scaled, 0.0).astype(b16), jnp.where(left, 0.0, scaled).astype(b16)], axis=0
        )
        both = jnp.where(left, c0, c1)
        y = nn(weights, split) + carried[:, sl] * jnp.exp(both) + cx_ref[5:6, sl] * x
        y_ref[:, sl] = y.astype(b16)
        xt[:, sl] = (scaled * jnp.exp(both[Q - 1 : Q, :] - both)).astype(b16)
        state[:, sl] = state[:, sl] * jnp.exp(both[Q - 1 : Q, :])
    state[...] += nn(bc[:, :STATE].T.astype(b16), xt[...])


def scan_forward(xin, bd, cx, cb, heads):
    rows, inner = xin.shape
    blocks, per_seq, pairs = rows // Q, LEN // Q, inner // Q
    wide = bd.shape[1]
    return pl.pallas_call(
        functools.partial(scan_forward_kernel, per_seq, pairs),
        grid=(blocks,),
        in_specs=[
            pl.BlockSpec((Q, inner), lambda k: (k, 0)),
            pl.BlockSpec((16, inner), lambda k: (jnp.maximum(k * (Q // 16) - 1, 0), 0)),
            pl.BlockSpec((Q, wide), lambda k: (k, 0)),
            pl.BlockSpec((8, wide), lambda k: (jnp.maximum(k * (Q // 8) - 1, 0), 0)),
            pl.BlockSpec(cx.shape, lambda k: (0, 0)),
            pl.BlockSpec(cb.shape, lambda k: (0, 0)),
            pl.BlockSpec(heads.shape, lambda k: (0, 0)),
        ],
        out_specs=[
            pl.BlockSpec((Q, inner), lambda k: (k, 0)),
            pl.BlockSpec((1, STATE, inner), lambda k: (k, 0, 0)),
        ],
        out_shape=[
            jax.ShapeDtypeStruct((rows, inner), b16),
            jax.ShapeDtypeStruct((blocks, STATE, inner), b16),
        ],
        scratch_shapes=[
            pltpu.VMEM((STATE, inner), f32),
            pltpu.VMEM((8 + Q, inner), f32),
            pltpu.VMEM((8 + Q, 2 * STATE), f32),
            pltpu.VMEM((Q, inner), b16),
            pltpu.VMEM((Q, inner), f32),
        ],
        compiler_params=pltpu.CompilerParams(vmem_limit_bytes=VMEM),
        cost_estimate=pl.CostEstimate(flops=rows * inner * 1200, bytes_accessed=rows * inner * 8, transcendentals=rows * inner * 8),
        name="scan_forward",
    )(xin, xin, bd, bd, cx, cb, heads)


def scan_backward_kernel(
    per_seq, pairs, blocks,
    dy_ref, xin_ref, xhalo_ref, bd_ref, bdhalo_ref, held_ref, cx_ref, cb_ref, heads_ref, pick_ref,
    dxin_ref, dbd_ref, gx_ref, gb_ref, gh_ref,
    adjoint, xs, bs, dps, dbs, xt, dye, carried, back, p1, p2, p3, row_sums,
):
    step_id = pl.program_id(0)
    block = blocks - 1 - step_id
    first = (block % per_seq) == 0
    last = (block % per_seq) == per_seq - 1

    @pl.when(step_id == 0)
    def _():
        gx_ref[...] = jnp.zeros_like(gx_ref)
        gb_ref[...] = jnp.zeros_like(gb_ref)
        gh_ref[...] = jnp.zeros_like(gh_ref)
        row_sums[...] = jnp.zeros_like(row_sums)

    @pl.when(last)
    def _():
        adjoint[...] = jnp.zeros_like(adjoint)
        dps[...] = jnp.zeros_like(dps)
        dbs[...] = jnp.zeros_like(dbs)

    keep = jnp.where(first, 0.0, 1.0)
    xs[0:8, :] = xhalo_ref[...].astype(f32)[8:16, :] * keep
    xs[8 : 8 + Q, :] = xin_ref[...].astype(f32)
    bs[0:8, :] = bdhalo_ref[:, : 2 * STATE] * keep
    bs[8 : 8 + Q, :] = bd_ref[:, : 2 * STATE]
    dps[Q : Q + 8, :] = dps[0:8, :]
    dbs[Q : Q + 8, :] = dbs[0:8, :]
    rows, cols = iota(0), iota(1)
    lower = rows >= cols
    upper = cols >= rows
    low_tri = jnp.where(lower, 1.0, 0.0).astype(f32)
    left = cols < HEAD
    pre_bc = conv(bs, cb_ref, slice(0, 2 * STATE))
    sig_bc = sigmoid(pre_bc)
    bc = pre_bc * sig_bc
    b_low, c_low = bc[:, :STATE].astype(b16), bc[:, STATE:].astype(b16)
    gram = jnp.where(upper, nt(b_low, c_low), 0.0)
    raw = bd_ref[:, 2 * STATE :]
    step, decay, cum = head_rates(raw, heads_ref, low_tri)
    cum_rows = cum.T
    held = held_ref[0]
    lam = adjoint[...]
    lam_low = lam.astype(b16)
    carried[...] = nn(c_low, held)
    back[...] = nn(b_low, lam_low)
    inner_states = jnp.sum(lam * held.astype(f32), axis=0, keepdims=True)
    dgram = jnp.zeros((Q, Q), f32)
    col_sums = jnp.zeros((Q, Q), f32)
    for p in range(pairs):
        sl = slice(p * Q, (p + 1) * Q)
        pre = conv(xs, cx_ref, sl)
        sig = sigmoid(pre)
        x = pre * sig
        step2 = jnp.where(left, step[:, 2 * p : 2 * p + 1], step[:, 2 * p + 1 : 2 * p + 2])
        scaled = x * step2
        dy = dy_ref[:, sl].astype(f32)
        split = jnp.concatenate(
            [jnp.where(left, dy, 0.0).astype(b16), jnp.where(left, 0.0, dy).astype(b16)], axis=0
        )
        dweights = nt(scaled.astype(b16), split)
        c0 = jnp.broadcast_to(cum[:, 2 * p : 2 * p + 1], (Q, Q))
        c1 = jnp.broadcast_to(cum[:, 2 * p + 1 : 2 * p + 2], (Q, Q))
        weights = []
        for half, column in ((0, c0), (1, c1)):
            head = 2 * p + half
            fade = jnp.exp(jnp.minimum(cum_rows[head : head + 1, :] - column, 0.0))
            weights.append((fade * gram).astype(b16))
            faded = dweights[:, half * Q : (half + 1) * Q] * fade
            dgram = dgram + faded
            cross = faded * gram
            row_sums[head : head + 1, :] = jnp.sum(cross, axis=0, keepdims=True)
            col_sums = jnp.where(cols == head, jnp.sum(cross, axis=1, keepdims=True), col_sums)
        both = jnp.where(left, c0, c1)
        tail = jnp.exp(both[Q - 1 : Q, :] - both)
        rise = jnp.exp(both)
        dx_state = back[:, sl] * tail
        dscaled = nn(jnp.concatenate(weights, axis=1), split) + dx_state
        dye_here = dy * rise
        p1[:, sl] = (dye_here * carried[:, sl]).astype(b16)
        p2[:, sl] = (scaled * dx_state).astype(b16)
        p3[:, sl] = (dscaled * x).astype(b16)
        xt[:, sl] = (scaled * tail).astype(b16)
        dye[:, sl] = dye_here.astype(b16)
        dx = dscaled * step2 + cx_ref[5:6, sl] * dy
        dpre = dx * sig * (1.0 + pre * (1.0 - sig))
        dps[0:Q, sl] = dpre
        dxin = jnp.zeros((Q, Q), f32)
        for k in range(4):
            dxin = dxin + cx_ref[k : k + 1, sl] * dps[3 - k : 3 - k + Q, sl]
            gx_ref[k : k + 1, sl] += jnp.sum(dpre * xs[5 + k : 5 + k + Q, sl], axis=0, keepdims=True)
        dxin_ref[:, sl] = dxin.astype(b16)
        gx_ref[4:5, sl] += jnp.sum(dpre, axis=0, keepdims=True)
        gx_ref[5:6, sl] += jnp.sum(dy * x, axis=0, keepdims=True)
    dgram_low = jnp.where(upper, dgram, 0.0)
    db = nn(dgram_low.astype(b16), c_low) + nt(xt[...], lam_low)
    dc = nn(dgram_low.T.astype(b16), b_low) + nt(dye[...], held)
    total = cum[Q - 1 : Q, :]
    pick = pick_ref[...]
    summed1 = nn(p1[...], pick)
    summed2 = nn(p2[...], pick)
    summed3 = nn(p3[...], pick)
    constant = jnp.exp(total) * nn(jnp.broadcast_to(inner_states, (8, inner_states.shape[1])), pick.astype(f32), exact)[0:1, :]
    up_tri = jnp.where(upper, 1.0, 0.0).astype(f32)
    strict = jnp.where(rows > cols, 1.0, 0.0).astype(f32)
    ddecay = (
        nt(up_tri, row_sums[...], exact)
        + nn(up_tri, summed1 - col_sums, exact)
        + nn(strict, summed2, exact)
        + constant
    )
    dstep = summed3 - ddecay * heads_ref[1:2, :]
    draw = dstep * sigmoid(raw + heads_ref[0:1, :])
    gh_ref[0:1, :] += jnp.sum(ddecay * decay, axis=0, keepdims=True)
    gh_ref[1:2, :] += jnp.sum(draw, axis=0, keepdims=True)
    rises = jnp.exp(jnp.concatenate(
        [jnp.where(left[0:1, :], total[:, 2 * p : 2 * p + 1], total[:, 2 * p + 1 : 2 * p + 2]) for p in range(pairs)], axis=1
    ))
    adjoint[...] = lam * rises + nn(bc[:, STATE:].T.astype(b16), dye[...])
    dbc = jnp.concatenate([db, dc], axis=1)
    dpre_bc = dbc * sig_bc * (1.0 + pre_bc * (1.0 - sig_bc))
    dbs[0:Q, :] = dpre_bc
    dbc_in = jnp.zeros((Q, 2 * STATE), f32)
    for k in range(4):
        dbc_in = dbc_in + cb_ref[k : k + 1, :] * dbs[3 - k : 3 - k + Q, :]
        gb_ref[k : k + 1, :] += jnp.sum(dpre_bc * bs[5 + k : 5 + k + Q, :], axis=0, keepdims=True)
    gb_ref[4:5, :] += jnp.sum(dpre_bc, axis=0, keepdims=True)
    dbd_ref[:, : 2 * STATE] = dbc_in.astype(b16)
    dbd_ref[:, 2 * STATE :] = draw.astype(b16)


def scan_backward(dy, xin, bd, held, cx, cb, heads, pick):
    rows, inner = xin.shape
    blocks, per_seq, pairs = rows // Q, LEN // Q, inner // Q
    wide = bd.shape[1]
    back = lambda k: blocks - 1 - k
    return pl.pallas_call(
        functools.partial(scan_backward_kernel, per_seq, pairs, blocks),
        grid=(blocks,),
        in_specs=[
            pl.BlockSpec((Q, inner), lambda k: (back(k), 0)),
            pl.BlockSpec((Q, inner), lambda k: (back(k), 0)),
            pl.BlockSpec((16, inner), lambda k: (jnp.maximum(back(k) * (Q // 16) - 1, 0), 0)),
            pl.BlockSpec((Q, wide), lambda k: (back(k), 0)),
            pl.BlockSpec((8, wide), lambda k: (jnp.maximum(back(k) * (Q // 8) - 1, 0), 0)),
            pl.BlockSpec((1, STATE, inner), lambda k: (back(k), 0, 0)),
            pl.BlockSpec(cx.shape, lambda k: (0, 0)),
            pl.BlockSpec(cb.shape, lambda k: (0, 0)),
            pl.BlockSpec(heads.shape, lambda k: (0, 0)),
            pl.BlockSpec(pick.shape, lambda k: (0, 0)),
        ],
        out_specs=[
            pl.BlockSpec((Q, inner), lambda k: (back(k), 0)),
            pl.BlockSpec((Q, wide), lambda k: (back(k), 0)),
            pl.BlockSpec((8, inner), lambda k: (0, 0)),
            pl.BlockSpec((8, 2 * STATE), lambda k: (0, 0)),
            pl.BlockSpec((8, Q), lambda k: (0, 0)),
        ],
        out_shape=[
            jax.ShapeDtypeStruct((rows, inner), b16),
            jax.ShapeDtypeStruct((rows, wide), b16),
            jax.ShapeDtypeStruct((8, inner), f32),
            jax.ShapeDtypeStruct((8, 2 * STATE), f32),
            jax.ShapeDtypeStruct((8, Q), f32),
        ],
        scratch_shapes=[
            pltpu.VMEM((STATE, inner), f32),
            pltpu.VMEM((8 + Q, inner), f32),
            pltpu.VMEM((8 + Q, 2 * STATE), f32),
            pltpu.VMEM((8 + Q, inner), f32),
            pltpu.VMEM((8 + Q, 2 * STATE), f32),
            pltpu.VMEM((Q, inner), b16),
            pltpu.VMEM((Q, inner), b16),
            pltpu.VMEM((Q, inner), f32),
            pltpu.VMEM((Q, inner), f32),
            pltpu.VMEM((Q, inner), b16),
            pltpu.VMEM((Q, inner), b16),
            pltpu.VMEM((Q, inner), b16),
            pltpu.VMEM((Q, Q), f32),
        ],
        compiler_params=pltpu.CompilerParams(vmem_limit_bytes=VMEM),
        cost_estimate=pl.CostEstimate(flops=rows * inner * 2400, bytes_accessed=rows * inner * 10, transcendentals=rows * inner * 8),
        name="scan_backward",
    )(dy, xin, xin, bd, bd, held, cx, cb, heads, pick)


def swap(value, bit, axis="dp"):
    count = lax.axis_size(axis)
    return lax.ppermute(value, axis, [(i, i ^ bit) for i in range(count)])


def spread(shard):
    found = {0: shard}
    found[8] = swap(found[0], 8)
    for low in (0, 8):
        found[low | 4] = swap(found[low], 4)
    for z in (0, 4, 8, 12):
        found[z | 1] = swap(found[z], 1)
        found[z | 2] = swap(found[z], 2)
        found[z | 3] = swap(found[z | 2], 1) if z < 8 else swap(found[z | 1], 2)
    return [found[r] for r in range(16)]


def merge_kernel(count, rows, layout, where_ref, *refs):
    mine, other, outs = refs[:count], refs[count : 2 * count], refs[2 * count :]
    me, side = where_ref[0], where_ref[1]
    for r in range(count):
        start = pl.multiple_of((me ^ r) * rows, 16)
        for piece, half in ((mine[r], side), (other[r], 1 - side)):
            for out, (begin, width) in zip(outs, layout):
                lane = pl.multiple_of(half * width, 128)
                out[pl.ds(start, rows), pl.ds(lane, width)] = piece[:, begin : begin + width]


def merge(where, mine, other, layout):
    count, rows = len(mine), mine[0].shape[0]
    whole = pl.BlockSpec(memory_space=pltpu.VMEM)
    return pl.pallas_call(
        functools.partial(merge_kernel, count, rows, layout),
        in_specs=[pl.BlockSpec(memory_space=pltpu.SMEM)] + [whole] * (2 * count),
        out_specs=[whole] * len(layout),
        out_shape=[jax.ShapeDtypeStruct((count * rows, 2 * width), b16) for _, width in layout],
        compiler_params=pltpu.CompilerParams(vmem_limit_bytes=VMEM),
        name="merge_weights",
    )(where, *mine, *other)


def gather(where, shard, layout):
    if lax.axis_size("dp") == 16 and shard.shape[0] % 16 == 0:
        mine = spread(shard)
        other = [swap(piece, 1, "tensor") for piece in mine]
        return merge(where, mine, other, layout)
    full = lax.all_gather(shard, "dp", axis=0, tiled=True)
    return [
        lax.all_gather(full[:, begin : begin + width], "tensor", axis=1, tiled=True)
        for begin, width in layout
    ]


def order():
    first = [(z0 << 2) | (y << 1) | x for y in (0, 1) for x in (0, 1) for z0 in (0, 1)]
    second = [8 | (z0 << 2) | (y << 1) | x for x in (0, 1) for y in (0, 1) for z0 in (0, 1)]
    return first, second


def pack_kernel(rows, parts, where_ref, *refs):
    ins, outs = refs[: len(parts)], refs[len(parts) :]
    me, side = where_ref[0], where_ref[1]
    for position, ranks in enumerate(order()):
        for slot, r in enumerate(ranks):
            start = pl.multiple_of((me ^ r) * rows, 16)
            for half, out in ((side, outs[position]), (1 - side, outs[2 + position])):
                begin = 0
                for ref, (width, shared) in zip(ins, parts):
                    lane = 0 if shared else pl.multiple_of(half * width, 128)
                    out[slot, :, begin : begin + width] = ref[pl.ds(start, rows), pl.ds(lane, width)]
                    begin += width


def pack(where, arrays, parts):
    rows = arrays[0].shape[0] // 16
    width = sum(w for w, _ in parts)
    whole = pl.BlockSpec(memory_space=pltpu.VMEM)
    return pl.pallas_call(
        functools.partial(pack_kernel, rows, parts),
        in_specs=[pl.BlockSpec(memory_space=pltpu.SMEM)] + [whole] * len(arrays),
        out_specs=[whole] * 4,
        out_shape=[jax.ShapeDtypeStruct((8, rows, width), b16)] * 4,
        compiler_params=pltpu.CompilerParams(vmem_limit_bytes=VMEM),
        name="pack_gradients",
    )(where, *arrays)


def plus(a, b):
    return (a.astype(f32) + b.astype(f32)).astype(b16)


def scatter_sum(where, arrays, parts):
    side = where[1]
    if lax.axis_size("dp") == 16 and arrays[0].shape[0] % 256 == 0:
        keep_a, keep_b, send_a, send_b = pack(where, arrays, parts)
        a = plus(keep_a, swap(send_a, 1, "tensor"))
        b = plus(keep_b, swap(send_b, 1, "tensor"))
        a, b = plus(a[:4], swap(a[4:], 2)), plus(b[:4], swap(b[4:], 1))
        a, b = plus(a[:2], swap(a[2:], 1)), plus(b[:2], swap(b[2:], 2))
        moved_a, moved_b = swap(a[1], 4), swap(b[1], 4)
        b = plus(b[0], moved_b)
        return (a[0].astype(f32) + moved_a.astype(f32)) + swap(b, 8).astype(f32)
    halves = []
    for array, (width, shared) in zip(arrays, parts):
        if shared:
            array = lax.psum(array, "tensor")
        else:
            array = lax.psum_scatter(array, "tensor", scatter_dimension=1, tiled=True)
        halves.append(array)
    return lax.psum_scatter(
        jnp.concatenate(halves, axis=1).astype(f32), "dp", scatter_dimension=0, tiled=True
    )


def total_sum(value):
    if lax.axis_size("dp") == 16:
        value = value + swap(value, 1, "tensor")
        for bit in (1, 2, 4, 8):
            value = value + swap(value, bit)
        return value
    return lax.psum(value, ("dp", "tensor"))


def both_sides(value, side, axis):
    other = swap(value, 1, "tensor")
    return jnp.where(
        side == 0, jnp.concatenate([value, other], axis), jnp.concatenate([other, value], axis)
    )


def body(
    tokens, pre_gain, w_zx, w_bc, w_dt, conv_x, conv_bc, a_log, dt_bias, skip_gain, norm_gain, w_out, cotangent,
):
    side = lax.axis_index("tensor")
    where = jnp.stack([lax.axis_index("dp"), side]).astype(jnp.int32)
    model, half = tokens.shape[1], conv_x.shape[1]
    inner = 2 * half
    half_heads = a_log.shape[0]
    heads_count = 2 * half_heads
    shard_rows = w_zx.shape[0]

    dt_pad = lax.dynamic_update_slice(
        jnp.zeros((shard_rows, 128), b16), w_dt, (0, side * half_heads)
    )
    bc_half = lax.dynamic_slice(w_bc, (0, side * STATE), (shard_rows, STATE))
    first = jnp.concatenate([w_zx[:, 1], bc_half, dt_pad], axis=1)
    w_x, full_bc, full_dt = gather(where, first, ((0, half), (half, STATE), (half + STATE, 128)))
    (w_z,) = gather(where, w_zx[:, 0], ((0, half),))
    (w_out_t,) = gather(where, w_out.T, ((0, half),))
    w_s = jnp.concatenate([full_bc, full_dt[:, :128] + full_dt[:, 128:]], axis=1)

    small = jnp.concatenate(
        [
            conv_x.astype(f32),
            norm_gain.astype(f32)[None],
            jnp.pad(jnp.concatenate([a_log, dt_bias, skip_gain]), (0, half - 3 * half_heads))[None],
            jnp.zeros((1, half), f32),
        ],
        axis=0,
    )
    small = both_sides(small[None], side, 0)
    wide = jnp.concatenate([small[0, :6], small[1, :6]], axis=1)
    gain_norm = wide[5:6]
    per_head = small[:, 6, : 3 * half_heads].reshape(2, 3, half_heads).transpose(1, 0, 2)
    per_head = per_head.reshape(3, heads_count)
    cx = jnp.concatenate(
        [wide[:5], jnp.repeat(per_head[2], HEAD)[None], jnp.zeros((2, inner), f32)], axis=0
    )
    cb = jnp.pad(conv_bc.astype(f32), ((0, 3), (0, 0)))
    heads = jnp.pad(
        jnp.stack([per_head[1], jnp.exp(per_head[0])]), ((0, 6), (0, Q - heads_count))
    )
    pick = (jnp.arange(inner)[:, None] // HEAD == jnp.arange(Q)[None, :]).astype(b16)

    x = tokens.astype(f32)
    gain_pre = pre_gain.astype(f32)
    scale = lax.rsqrt(jnp.mean(x * x, axis=1, keepdims=True) + epsilon)
    normed = (x * scale * gain_pre).astype(b16)
    xin = nn(normed, w_x).astype(b16)
    bd = nn(normed, w_s)
    ssd, held = scan_forward(xin, bd, cx, cb, heads)
    z = nn(normed, w_z).astype(b16)

    zf = z.astype(f32)
    yf = ssd.astype(f32)
    sig = sigmoid(zf)
    gated = yf * zf * sig
    inv = lax.rsqrt(jnp.mean(gated * gated, axis=1, keepdims=True) + epsilon)
    mixed = (gated * inv * gain_norm).astype(b16)
    grad_out = tn(cotangent, mixed).astype(b16)
    out_part = scatter_sum(where, [grad_out], ((half, False),))
    out = (x + nt(mixed, w_out_t)).astype(b16)
    dmixed = nn(cotangent, w_out_t)
    grad_norm = jnp.sum(dmixed * gated * inv, axis=0)
    dhat = dmixed * gain_norm
    cross = jnp.mean(dhat * gated, axis=1, keepdims=True)
    dgated = inv * dhat - gated * (inv * inv * inv) * cross
    dz = (dgated * yf * sig * (1.0 + zf * (1.0 - sig))).astype(b16)
    dssd = (dgated * zf * sig).astype(b16)
    grad_z = tn(normed, dz).astype(b16)
    z_part = scatter_sum(where, [grad_z], ((half, False),))

    dxin, dbd, gx, gb, gh = scan_backward(dssd, xin, bd, held, cx, cb, heads, pick)
    grad_x = tn(normed, dxin).astype(b16)
    grad_s = tn(normed, dbd).astype(b16)
    x_part = scatter_sum(
        where,
        [grad_x, grad_s[:, : 2 * STATE], grad_s[:, 2 * STATE :]],
        ((half, False), (STATE, False), (128, True)),
    )
    dnormed = nt(dz, w_z) + nt(dxin, w_x) + nt(dbd, w_s)
    grad_pre = jnp.sum(dnormed * x * scale, axis=0)
    dn = dnormed * gain_pre
    grad_tokens = cotangent.astype(f32) + scale * dn
    grad_tokens = grad_tokens - x * (scale * scale * scale) * jnp.mean(dn * x, axis=1, keepdims=True)

    flat = jnp.concatenate(
        [gx[:6].reshape(-1), grad_norm, gb[:5].reshape(-1), gh[0], gh[1], grad_pre]
    )
    flat = jnp.pad(flat, (0, -flat.shape[0] % 1024)).reshape(-1, 128)
    summed = total_sum(flat).reshape(-1)
    sizes = [5 * inner, inner, inner, 10 * STATE, Q, Q, model]
    pieces, begin = [], 0
    for size in sizes:
        pieces.append(summed[begin : begin + size])
        begin += size
    convx_sum, skip_lanes, norm_sum, convbc_sum, alog_sum, bias_sum, pre_sum = pieces

    def mine(vector, width):
        return lax.dynamic_slice_in_dim(vector, side * width, width, vector.ndim - 1)

    skip_sum = jnp.sum(skip_lanes.reshape(heads_count, HEAD), axis=1)
    z_out = jnp.stack([z_part, x_part[:, :half]], axis=1)
    bc_part = both_sides(x_part[:, half : half + STATE].astype(b16), side, 1).astype(f32)
    dt_part = mine(x_part[:, half + STATE :], half_heads)
    return (
        out,
        grad_tokens.astype(b16),
        pre_sum,
        z_out,
        bc_part,
        dt_part,
        mine(convx_sum.reshape(5, inner), half),
        convbc_sum.reshape(5, 2 * STATE),
        mine(alog_sum, half_heads),
        mine(bias_sum, half_heads),
        mine(skip_sum, half_heads),
        mine(norm_sum, half),
        out_part.T,
    )


def solution(mesh):
    placed = (
        P(("dp", "tensor"), None),
        P(),
        P("dp", None, "tensor"),
        P("dp", None),
        P("dp", "tensor"),
        P(None, "tensor"),
        P(),
        P("tensor"),
        P("tensor"),
        P("tensor"),
        P("tensor"),
        P("tensor", "dp"),
        P(("dp", "tensor"), None),
    )
    return jax.shard_map(
        body,
        mesh=mesh,
        in_specs=placed,
        out_specs=(
            P(("dp", "tensor"), None),
            P(("dp", "tensor"), None),
            P(),
            P("dp", None, "tensor"),
            P("dp", None),
            P("dp", "tensor"),
            P(None, "tensor"),
            P(),
            P("tensor"),
            P("tensor"),
            P("tensor"),
            P("tensor"),
            P("tensor", "dp"),
        ),
        check_vma=False,
    )
```

```python
import functools

import jax
import jax.numpy as jnp
from jax import lax
from jax.experimental import pallas as pl
from jax.experimental.pallas import tpu as pltpu
from jax.sharding import PartitionSpec as P

LEN = 1024
Q = 128
HEAD = 64
STATE = 128
epsilon = 1e-05
f32 = jnp.float32
b16 = jnp.bfloat16
exact = lax.Precision.HIGHEST
VMEM = 56 * 1024 * 1024


def nn(a, b, precision=None):
    return lax.dot_general(
        a, b, (((1,), (0,)), ((), ())), preferred_element_type=f32, precision=precision
    )


def nt(a, b, precision=None):
    return lax.dot_general(
        a, b, (((1,), (1,)), ((), ())), preferred_element_type=f32, precision=precision
    )


def tn(a, b):
    return lax.dot_general(a, b, (((0,), (0,)), ((), ())), preferred_element_type=f32)


def sigmoid(v):
    return 0.5 * jnp.tanh(0.5 * v) + 0.5


def softplus(v):
    return jnp.maximum(v, 0.0) + jnp.log1p(jnp.exp(-jnp.abs(v)))


def iota(axis):
    return lax.broadcasted_iota(jnp.int32, (Q, Q), axis)


def token(row):
    return ((row & 7) << 4) | (row >> 3)


def sublane(width):
    return lax.broadcasted_iota(jnp.int32, (24, width), 0) & 7


def with_past(here, past):
    mixed = jnp.where(
        sublane(here.shape[1]) == 0, pltpu.roll(past, 17, 0), pltpu.roll(here[Q - 24 :], 1, 0)
    )
    return jnp.concatenate([mixed, here], axis=0)


def with_future(here, future):
    mixed = jnp.where(
        sublane(here.shape[1]) == 7, pltpu.roll(future, 7, 0), pltpu.roll(here[:24], 23, 0)
    )
    return jnp.concatenate([here, mixed], axis=0)


def conv(padded, taps, lanes):
    total = taps[4:5, lanes]
    for k in range(4):
        total = total + taps[k : k + 1, lanes] * padded[8 * k : 8 * k + Q]
    return total


def fold(value):
    return jnp.sum(value.reshape(Q // 8, 8, value.shape[1]), axis=0)


def split_low(value, count):
    pieces = []
    for _ in range(count):
        piece = value.astype(b16)
        pieces.append(piece)
        value = value - piece.astype(f32)
    return jnp.concatenate(pieces, axis=1)


def head_rates(dt_raw, heads_ref, low_tri):
    step = softplus(dt_raw + heads_ref[0:1, :])
    decay = -step * heads_ref[1:2, :]
    sums = nn(low_tri, split_low(decay, 3))
    cum = sums[:, :Q] + sums[:, Q : 2 * Q] + sums[:, 2 * Q :]
    return step, decay, cum


def scan_forward_kernel(
    per_seq, pairs, base, resumed, *refs
):
    xin_ref, xhalo_ref, bd_ref, bdhalo_ref, cx_ref, cb_ref, heads_ref = refs[:7]
    y_ref, state_out_ref, pre_ref, state, xt, carried = refs[-6:]
    first = ((base + pl.program_id(0)) % per_seq) == 0

    if resumed:

        @pl.when(pl.program_id(0) == 0)
        def _():
            state[...] = refs[7][...]

    @pl.when(first)
    def _():
        state[...] = jnp.zeros_like(state)

    keep = jnp.where(first, 0.0, 1.0)
    rows, cols = token(iota(0)), token(iota(1))
    lower = rows >= cols
    low_tri = jnp.where(lower, 1.0, 0.0).astype(b16)
    left = iota(1) < HEAD
    bs = with_past(bd_ref[:, : 2 * STATE], bdhalo_ref[8:32, : 2 * STATE] * keep)
    pre_bc = conv(bs, cb_ref, slice(0, 2 * STATE))
    bc = pre_bc * sigmoid(pre_bc)
    b_low, c_low = bc[:, :STATE].astype(b16), bc[:, STATE:].astype(b16)
    gram = jnp.where(lower, nt(c_low, b_low), 0.0)
    step, decay, cum = head_rates(bd_ref[:, 2 * STATE :], heads_ref, low_tri)
    cum_rows = cum.T
    held = state[...].astype(b16)
    state_out_ref[0] = held
    carried[...] = nn(c_low, held)
    for p in range(pairs):
        sl = slice(p * Q, (p + 1) * Q)
        past = xhalo_ref[:, sl].astype(f32)[8:32] * keep
        pre = conv(with_past(xin_ref[:, sl].astype(f32), past), cx_ref, sl)
        pre_ref[:, sl] = pre.astype(b16)
        x = pre * sigmoid(pre)
        step2 = jnp.where(left, step[:, 2 * p : 2 * p + 1], step[:, 2 * p + 1 : 2 * p + 2])
        scaled = x * step2
        c0 = jnp.broadcast_to(cum[:, 2 * p : 2 * p + 1], (Q, Q))
        c1 = jnp.broadcast_to(cum[:, 2 * p + 1 : 2 * p + 2], (Q, Q))
        w0 = jnp.exp(jnp.minimum(c0 - cum_rows[2 * p : 2 * p + 1, :], 0.0)) * gram
        w1 = jnp.exp(jnp.minimum(c1 - cum_rows[2 * p + 1 : 2 * p + 2, :], 0.0)) * gram
        weights = jnp.concatenate([w0.astype(b16), w1.astype(b16)], axis=1)
        split = jnp.concatenate(
            [jnp.where(left, scaled, 0.0).astype(b16), jnp.where(left, 0.0, scaled).astype(b16)], axis=0
        )
        both = jnp.where(left, c0, c1)
        y = nn(weights, split) + carried[:, sl] * jnp.exp(both) + cx_ref[5:6, sl] * x
        y_ref[:, sl] = y.astype(b16)
        xt[:, sl] = (scaled * jnp.exp(both[Q - 1 : Q, :] - both)).astype(b16)
        state[:, sl] = state[:, sl] * jnp.exp(both[Q - 1 : Q, :])
    state[...] += nn(bc[:, :STATE].T.astype(b16), xt[...])


def scan_forward(xin, bd, cx, cb, heads, base, count, before):
    rows, inner = xin.shape
    blocks, per_seq, pairs = rows // Q, LEN // Q, inner // Q
    wide = bd.shape[1]
    kept = [] if before is None else [before[3], *before[:3]]
    return pl.pallas_call(
        functools.partial(scan_forward_kernel, per_seq, pairs, base, before is not None),
        grid=(count,),
        in_specs=[
            pl.BlockSpec((Q, inner), lambda k: (base + k, 0)),
            pl.BlockSpec((32, inner), lambda k: (jnp.maximum((base + k) * (Q // 32) - 1, 0), 0)),
            pl.BlockSpec((Q, wide), lambda k: (base + k, 0)),
            pl.BlockSpec((32, wide), lambda k: (jnp.maximum((base + k) * (Q // 32) - 1, 0), 0)),
            pl.BlockSpec(cx.shape, lambda k: (0, 0)),
            pl.BlockSpec(cb.shape, lambda k: (0, 0)),
            pl.BlockSpec(heads.shape, lambda k: (0, 0)),
        ]
        + ([pl.BlockSpec((STATE, inner), lambda k: (0, 0))] + [pl.BlockSpec(memory_space=pl.ANY)] * 3 if kept else []),
        out_specs=[
            pl.BlockSpec((Q, inner), lambda k: (base + k, 0)),
            pl.BlockSpec((1, STATE, inner), lambda k: (base + k, 0, 0)),
            pl.BlockSpec((Q, inner), lambda k: (base + k, 0)),
            pl.BlockSpec((STATE, inner), lambda k: (0, 0)),
        ],
        out_shape=[
            jax.ShapeDtypeStruct((rows, inner), b16),
            jax.ShapeDtypeStruct((blocks, STATE, inner), b16),
            jax.ShapeDtypeStruct((rows, inner), b16),
            jax.ShapeDtypeStruct((STATE, inner), f32),
        ],
        input_output_aliases={8: 0, 9: 1, 10: 2} if kept else {},
        scratch_shapes=[
            pltpu.VMEM((Q, inner), b16),
            pltpu.VMEM((Q, inner), f32),
        ],
        compiler_params=pltpu.CompilerParams(vmem_limit_bytes=VMEM),
        cost_estimate=pl.CostEstimate(flops=count * Q * inner * 6000, bytes_accessed=count * Q * inner * 8, transcendentals=count * Q * inner * 8),
        name="scan_forward",
    )(xin, xin, bd, bd, cx, cb, heads, *kept)


def scan_backward_kernel(
    per_seq, pairs, base, count, resumed, *refs
):
    (dy_ref, xin_ref, pre_ref, bd_ref, bdhalo_ref, held_ref, cx_ref, cb_ref, heads_ref, pick_ref) = refs[:10]
    (
        dxin_ref, dbd_ref, adjoint, xnext, bnext, gx_ref, gb_ref, gh_ref,
        xt, dye, carried, back, products, row_sums,
    ) = refs[-14:]
    step_id = pl.program_id(0)
    block = base + count - 1 - step_id
    first = (block % per_seq) == 0
    last = (block % per_seq) == per_seq - 1

    @pl.when(step_id == 0)
    def _():
        row_sums[...] = jnp.zeros_like(row_sums)
        for here, ref in enumerate((adjoint, xnext, bnext, gx_ref, gb_ref, gh_ref)):
            ref[...] = refs[10 + here][...] if resumed else jnp.zeros_like(ref)

    @pl.when(last)
    def _():
        adjoint[...] = jnp.zeros_like(adjoint)
        xnext[...] = jnp.zeros_like(xnext)
        bnext[...] = jnp.zeros_like(bnext)

    keep = jnp.where(first, 0.0, 1.0)
    rows, cols = token(iota(0)), token(iota(1))
    upper = cols >= rows
    low_tri = jnp.where(rows >= cols, 1.0, 0.0).astype(b16)
    left = iota(1) < HEAD
    left_low = jnp.where(left, 1.0, 0.0).astype(b16)
    right_low = jnp.where(left, 0.0, 1.0).astype(b16)
    ones_low = jnp.ones((8, Q), b16)
    lane_of = lax.broadcasted_iota(jnp.int32, (2 * Q, Q), 1)
    half_of = lax.broadcasted_iota(jnp.int32, (2 * Q, Q), 0) // Q
    bs = with_past(bd_ref[:, : 2 * STATE], bdhalo_ref[8:32, : 2 * STATE] * keep)
    pre_bc = conv(bs, cb_ref, slice(0, 2 * STATE))
    sig_bc = sigmoid(pre_bc)
    bc = pre_bc * sig_bc
    b_low, c_low = bc[:, :STATE].astype(b16), bc[:, STATE:].astype(b16)
    gram = jnp.where(upper, nt(b_low, c_low), 0.0)
    raw = bd_ref[:, 2 * STATE :]
    step, decay, cum = head_rates(raw, heads_ref, low_tri)
    cum_rows = cum.T
    held = held_ref[0]
    lam = adjoint[...]
    lam_low = lam.astype(b16)
    carried[...] = nn(c_low, held)
    back[...] = nn(b_low, lam_low)
    inner_states = jnp.sum(lam * held.astype(f32), axis=0, keepdims=True)
    dgram = jnp.zeros((Q, Q), f32)
    col_sums = jnp.zeros((Q, Q), f32)
    for p in range(pairs):
        sl = slice(p * Q, (p + 1) * Q)
        pre = pre_ref[:, sl].astype(f32)
        sig = sigmoid(pre)
        x = pre * sig
        step2 = jnp.where(left, step[:, 2 * p : 2 * p + 1], step[:, 2 * p + 1 : 2 * p + 2])
        scaled = x * step2
        dy_low = dy_ref[:, sl]
        dy = dy_low.astype(f32)
        split = jnp.concatenate([dy_low * left_low, dy_low * right_low], axis=0)
        dweights = nt(scaled.astype(b16), split)
        c0 = jnp.broadcast_to(cum[:, 2 * p : 2 * p + 1], (Q, Q))
        c1 = jnp.broadcast_to(cum[:, 2 * p + 1 : 2 * p + 2], (Q, Q))
        weights, crossing = [], []
        for half, column in ((0, c0), (1, c1)):
            head = 2 * p + half
            fade = jnp.exp(jnp.minimum(cum_rows[head : head + 1, :] - column, 0.0))
            weights.append((fade * gram).astype(b16))
            faded = dweights[:, half * Q : (half + 1) * Q] * fade
            dgram = dgram + faded
            crossing.append((faded * gram).astype(b16))
        crossing = jnp.concatenate(crossing, axis=1)
        over_rows = nn(ones_low, crossing)
        row_sums[2 * p : 2 * p + 1, :] = over_rows[0:1, :Q]
        row_sums[2 * p + 1 : 2 * p + 2, :] = over_rows[0:1, Q:]
        col_sums = col_sums + nn(crossing, jnp.where(lane_of == 2 * p + half_of, 1.0, 0.0).astype(b16))
        both = jnp.where(left, c0, c1)
        tail = jnp.exp(both[Q - 1 : Q, :] - both)
        rise = jnp.exp(both)
        dx_state = back[:, sl] * tail
        dscaled = nn(jnp.concatenate(weights, axis=1), split) + dx_state
        dye_here = dy * rise
        products[0:Q, sl] = (dye_here * carried[:, sl]).astype(b16)
        products[Q : 2 * Q, sl] = (scaled * dx_state).astype(b16)
        products[2 * Q :, sl] = (dscaled * x).astype(b16)
        xt[:, sl] = (scaled * tail).astype(b16)
        dye[:, sl] = dye_here.astype(b16)
        dx = dscaled * step2 + cx_ref[5:6, sl] * dy
        dpre = dx * (sig + x * (1.0 - sig))
        padded = with_future(dpre, xnext[:, sl])
        xnext[:, sl] = dpre[:24]
        dxin = jnp.zeros((Q, Q), f32)
        xin = xin_ref[:, sl].astype(f32)
        for k in range(4):
            ahead = padded[24 - 8 * k : 24 - 8 * k + Q]
            dxin = dxin + cx_ref[k : k + 1, sl] * ahead
            gx_ref[8 * k : 8 * k + 8, sl] += fold(ahead * xin)
        dxin_ref[:, sl] = dxin.astype(b16)
        gx_ref[32:40, sl] += fold(dpre)
        gx_ref[40:48, sl] += fold(dy * x)
    dgram_low = jnp.where(upper, dgram, 0.0)
    db = nn(dgram_low.astype(b16), c_low) + nt(xt[...], lam_low)
    dc = nn(dgram_low.T.astype(b16), b_low) + nt(dye[...], held)
    total = cum[Q - 1 : Q, :]
    pick = pick_ref[...]
    summed = nn(products[...], pick)
    high = inner_states.astype(b16)
    low = (inner_states - high.astype(f32)).astype(b16)
    both_states = jnp.concatenate([jnp.broadcast_to(high, (8, high.shape[1])), jnp.broadcast_to(low, (8, low.shape[1]))], axis=0)
    state_sums = nn(both_states, pick)
    constant = jnp.exp(total) * (state_sums[0:1, :] + state_sums[8:9, :])
    up_tri = jnp.where(upper, 1.0, 0.0).astype(b16)
    strict = jnp.where(rows > cols, 1.0, 0.0).astype(b16)
    moved = jnp.concatenate([summed[:Q] - col_sums + row_sums[...].T, summed[Q : 2 * Q]], axis=0)
    crossed = nn(jnp.concatenate([up_tri, strict], axis=1), split_low(moved, 3))
    ddecay = crossed[:, :Q] + crossed[:, Q : 2 * Q] + crossed[:, 2 * Q :] + constant
    summed3 = summed[2 * Q :]
    dstep = summed3 - ddecay * heads_ref[1:2, :]
    draw = dstep * sigmoid(raw + heads_ref[0:1, :])
    gh_ref[0:1, :] += jnp.sum(ddecay * decay, axis=0, keepdims=True)
    gh_ref[1:2, :] += jnp.sum(draw, axis=0, keepdims=True)
    rises = jnp.exp(jnp.concatenate(
        [jnp.where(left[0:1, :], total[:, 2 * p : 2 * p + 1], total[:, 2 * p + 1 : 2 * p + 2]) for p in range(pairs)], axis=1
    ))
    adjoint[...] = lam * rises + nn(bc[:, STATE:].T.astype(b16), dye[...])
    dbc = jnp.concatenate([db, dc], axis=1)
    dpre_bc = dbc * sig_bc * (1.0 + pre_bc * (1.0 - sig_bc))
    padded = with_future(dpre_bc, bnext[...])
    bnext[...] = dpre_bc[:24]
    dbc_in = jnp.zeros((Q, 2 * STATE), f32)
    for k in range(4):
        ahead = padded[24 - 8 * k : 24 - 8 * k + Q]
        dbc_in = dbc_in + cb_ref[k : k + 1, :] * ahead
        gb_ref[8 * k : 8 * k + 8, :] += fold(ahead * bd_ref[:, : 2 * STATE])
    gb_ref[32:40, :] += fold(dpre_bc)
    dbd_ref[:, : 2 * STATE] = dbc_in.astype(b16)
    dbd_ref[:, 2 * STATE :] = draw.astype(b16)


def scan_backward(dy, xin, pre, bd, held, cx, cb, heads, pick, base, count, before):
    rows, inner = xin.shape
    blocks, per_seq, pairs = rows // Q, LEN // Q, inner // Q
    wide = bd.shape[1]
    back = lambda k: base + count - 1 - k
    fixed = lambda shape: pl.BlockSpec(shape, lambda k: (0, 0))
    carry = [(STATE, inner), (24, inner), (24, 2 * STATE), (48, inner), (40, 2 * STATE), (8, Q)]
    kept = [] if before is None else [*before[2:], before[0], before[1]]
    return pl.pallas_call(
        functools.partial(scan_backward_kernel, per_seq, pairs, base, count, before is not None),
        grid=(count,),
        in_specs=[
            pl.BlockSpec((Q, inner), lambda k: (back(k), 0)),
            pl.BlockSpec((Q, inner), lambda k: (back(k), 0)),
            pl.BlockSpec((Q, inner), lambda k: (back(k), 0)),
            pl.BlockSpec((Q, wide), lambda k: (back(k), 0)),
            pl.BlockSpec((32, wide), lambda k: (jnp.maximum(back(k) * (Q // 32) - 1, 0), 0)),
            pl.BlockSpec((1, STATE, inner), lambda k: (back(k), 0, 0)),
            fixed(cx.shape),
            fixed(cb.shape),
            fixed(heads.shape),
            fixed(pick.shape),
        ]
        + ([fixed(shape) for shape in carry] + [pl.BlockSpec(memory_space=pl.ANY)] * 2 if kept else []),
        out_specs=[
            pl.BlockSpec((Q, inner), lambda k: (back(k), 0)),
            pl.BlockSpec((Q, wide), lambda k: (back(k), 0)),
        ]
        + [fixed(shape) for shape in carry],
        out_shape=[
            jax.ShapeDtypeStruct((rows, inner), b16),
            jax.ShapeDtypeStruct((rows, wide), b16),
        ]
        + [jax.ShapeDtypeStruct(shape, f32) for shape in carry],
        input_output_aliases={16: 0, 17: 1} if kept else {},
        scratch_shapes=[
            pltpu.VMEM((Q, inner), b16),
            pltpu.VMEM((Q, inner), b16),
            pltpu.VMEM((Q, inner), f32),
            pltpu.VMEM((Q, inner), f32),
            pltpu.VMEM((3 * Q, inner), b16),
            pltpu.VMEM((Q, Q), f32),
        ],
        compiler_params=pltpu.CompilerParams(vmem_limit_bytes=VMEM),
        cost_estimate=pl.CostEstimate(flops=count * Q * inner * 12000, bytes_accessed=count * Q * inner * 10, transcendentals=count * Q * inner * 8),
        name="scan_backward",
    )(dy, xin, pre, bd, bd, held, cx, cb, heads, pick, *kept)


def swap(value, bit, axis="dp"):
    count = lax.axis_size(axis)
    return lax.ppermute(value, axis, [(i, i ^ bit) for i in range(count)])


def tie(value, *others):
    return lax.optimization_barrier((value, *others))[0]


def fast(rows):
    return lax.axis_size("dp") == 16 and rows % 16 == 0


def along_z(shard):
    return jnp.stack([shard] + [swap(shard, z << 2) for z in (1, 2, 3)])


def around(column):
    return [column] + [swap(column, q) for q in (1, 2, 3)]


def merge_kernel(rows, layout, where_ref, *refs):
    mine, other, outs = refs[:4], refs[4:8], refs[8:]
    me, side = where_ref[0], where_ref[1]
    for q in range(4):
        for z in range(4):
            start = pl.multiple_of((me ^ (4 * z + q)) * rows, 16)
            for piece, half in ((mine[q], side), (other[q], 1 - side)):
                for out, (begin, width) in zip(outs, layout):
                    lane = pl.multiple_of(half * width, 128)
                    out[pl.ds(start, rows), pl.ds(lane, width)] = piece[z, :, begin : begin + width]


def merge(where, mine, other, layout):
    rows = mine[0].shape[1]
    whole = pl.BlockSpec(memory_space=pltpu.VMEM)
    return pl.pallas_call(
        functools.partial(merge_kernel, rows, layout),
        in_specs=[pl.BlockSpec(memory_space=pltpu.SMEM)] + [whole] * 8,
        out_specs=[whole] * len(layout),
        out_shape=[jax.ShapeDtypeStruct((16 * rows, 2 * width), b16) for _, width in layout],
        compiler_params=pltpu.CompilerParams(vmem_limit_bytes=VMEM),
        name="merge_weights",
    )(where, *mine, *other)


def gather_plain(shard, layout):
    full = lax.all_gather(shard, "dp", axis=0, tiled=True)
    return [
        lax.all_gather(full[:, begin : begin + width], "tensor", axis=1, tiled=True)
        for begin, width in layout
    ]


def pack_kernel(rows, parts, where_ref, *refs):
    ins, (keep, send) = refs[:-2], refs[-2:]
    me, side = where_ref[0], where_ref[1]
    for q in range(4):
        for z in range(4):
            start = pl.multiple_of((me ^ (4 * z + q)) * rows, 16)
            for half, out in ((side, keep), (1 - side, send)):
                begin = 0
                for which, base, width, shared in parts:
                    ref = ins[which]
                    lane = base if shared else pl.multiple_of(base + half * width, 128)
                    out[q, z, :, begin : begin + width] = ref[pl.ds(start, rows), pl.ds(lane, width)]
                    begin += width


def pack(where, arrays, parts):
    rows = arrays[0].shape[0] // 16
    width = sum(part[2] for part in parts)
    whole = pl.BlockSpec(memory_space=pltpu.VMEM)
    return pl.pallas_call(
        functools.partial(pack_kernel, rows, parts),
        in_specs=[pl.BlockSpec(memory_space=pltpu.SMEM)] + [whole] * len(arrays),
        out_specs=[whole] * 2,
        out_shape=[jax.ShapeDtypeStruct((4, 4, rows, width), b16)] * 2,
        compiler_params=pltpu.CompilerParams(vmem_limit_bytes=VMEM),
        name="pack_gradients",
    )(where, *arrays)


def sum_tensor(keep, send):
    got = swap(send, 1, "tensor")
    return (keep.astype(f32) + got.astype(f32)).astype(b16)


def sum_around(parts):
    got = [swap(parts[q], q) for q in (1, 2, 3)]
    total = parts[0].astype(f32)
    for value in got:
        total = total + value.astype(f32)
    return total.astype(b16)


def sum_along_z(parts):
    got = [swap(parts[z], z << 2) for z in (1, 2, 3)]
    total = parts[0].astype(f32)
    for value in got:
        total = total + value.astype(f32)
    return total


def scatter_plain(arrays, parts):
    halves = []
    for which, base, width, shared in parts:
        array = arrays[which][:, base : base + (width if shared else 2 * width)]
        if shared:
            array = lax.psum(array, "tensor")
        else:
            array = lax.psum_scatter(array, "tensor", scatter_dimension=1, tiled=True)
        halves.append(array)
    return lax.psum_scatter(
        jnp.concatenate(halves, axis=1).astype(f32), "dp", scatter_dimension=0, tiled=True
    )


def shuffle(value):
    rows, width = value.shape
    return value.reshape(-1, 8, 16, width).swapaxes(1, 2).reshape(rows, width)


def unshuffle(value):
    rows, width = value.shape
    return value.reshape(-1, 16, 8, width).swapaxes(1, 2).reshape(rows, width)


def both_sides(value, side, axis):
    other = swap(value, 1, "tensor")
    return jnp.where(
        side == 0, jnp.concatenate([value, other], axis), jnp.concatenate([other, value], axis)
    )


def body(
    tokens, pre_gain, w_zx, w_bc, w_dt, conv_x, conv_bc, a_log, dt_bias, skip_gain, norm_gain, w_out, cotangent,
):
    side = lax.axis_index("tensor")
    where = jnp.stack([lax.axis_index("dp"), side]).astype(jnp.int32)
    model, half = tokens.shape[1], conv_x.shape[1]
    inner = 2 * half
    half_heads = a_log.shape[0]
    heads_count = 2 * half_heads
    shard_rows = w_zx.shape[0]

    dt_pad = lax.dynamic_update_slice(
        jnp.zeros((shard_rows, 128), b16), w_dt, (0, side * half_heads)
    )
    bc_half = lax.dynamic_slice(w_bc, (0, side * STATE), (shard_rows, STATE))
    quick = fast(shard_rows)
    first = jnp.concatenate([w_zx[:, 1], bc_half, dt_pad], axis=1)
    second = jnp.concatenate([w_zx[:, 0], w_out.T], axis=1)
    first_layout = ((0, half), (half, STATE), (half + STATE, 128))
    second_layout = ((0, half), (half, half))
    if quick:
        column = along_z(first)
        later = along_z(tie(second, column))
        mine_first = around(column)
        other_first = [swap(part, 1, "tensor") for part in mine_first]
        mine_second = around(tie(later, *mine_first))
        w_x, full_bc, full_dt = merge(where, mine_first, other_first, first_layout)
    else:
        w_x, full_bc, full_dt = gather_plain(first, first_layout)
        w_z, w_out_t = gather_plain(second, second_layout)
    small = jnp.concatenate(
        [
            conv_x.astype(f32),
            norm_gain.astype(f32)[None],
            jnp.pad(jnp.concatenate([a_log, dt_bias, skip_gain]), (0, half - 3 * half_heads))[None],
            jnp.zeros((1, half), f32),
        ],
        axis=0,
    )
    small = both_sides(small[None], side, 0)
    wide = jnp.concatenate([small[0, :6], small[1, :6]], axis=1)
    gain_norm = wide[5:6]
    per_head = small[:, 6, : 3 * half_heads].reshape(2, 3, half_heads).transpose(1, 0, 2)
    per_head = per_head.reshape(3, heads_count)
    cx = jnp.concatenate(
        [wide[:5], jnp.repeat(per_head[2], HEAD)[None], jnp.zeros((2, inner), f32)], axis=0
    )
    cb = jnp.pad(conv_bc.astype(f32), ((0, 3), (0, 0)))
    heads = jnp.pad(
        jnp.stack([per_head[1], jnp.exp(per_head[0])]), ((0, 6), (0, Q - heads_count))
    )
    pick = (jnp.arange(inner)[:, None] // HEAD == jnp.arange(Q)[None, :]).astype(b16)

    w_s = jnp.concatenate([full_bc, full_dt[:, :128] + full_dt[:, 128:]], axis=1)
    tokens, cotangent = lax.optimization_barrier((shuffle(tokens), shuffle(cotangent)))
    x = tokens.astype(f32)
    gain_pre = pre_gain.astype(f32)
    scale = lax.rsqrt(jnp.mean(x * x, axis=1, keepdims=True) + epsilon)
    normed = (x * scale * gain_pre).astype(b16)
    normed_t, cot_t = lax.optimization_barrier((normed.T, cotangent.T))
    xin = nn(normed, w_x).astype(b16)
    bd = nn(normed, w_s)
    blocks = tokens.shape[0] // Q
    started = list(scan_forward(xin, bd, cx, cb, heads, 0, blocks // 2, None))
    if quick:
        started[3], *mine_second = lax.optimization_barrier((started[3], *mine_second))
        other_second = [swap(part, 1, "tensor") for part in mine_second]
    ssd, held, pre, ended = scan_forward(
        xin, bd, cx, cb, heads, blocks // 2, blocks - blocks // 2, started
    )
    if quick:
        other_second = lax.optimization_barrier((ended, *other_second))[1:]
        w_z, w_out_t = merge(where, mine_second, other_second, second_layout)
    z = nn(normed, w_z).astype(b16)

    zf = z.astype(f32)
    yf = ssd.astype(f32)
    sig = sigmoid(zf)
    gated = yf * zf * sig
    inv = lax.rsqrt(jnp.mean(gated * gated, axis=1, keepdims=True) + epsilon)
    mixed = (gated * inv * gain_norm).astype(b16)
    grad_out = nn(cot_t, mixed).astype(b16)
    dmixed = nn(cotangent, w_out_t)
    grad_norm = jnp.sum(dmixed * gated * inv, axis=0)
    dhat = dmixed * gain_norm
    cross = jnp.mean(dhat * gated, axis=1, keepdims=True)
    dgated = inv * dhat - gated * (inv * inv * inv) * cross
    dz = (dgated * yf * sig * (1.0 + zf * (1.0 - sig))).astype(b16)
    dssd = (dgated * zf * sig).astype(b16)
    grad_z = nn(normed_t, dz).astype(b16)

    early, early_parts = [grad_z, grad_out], ((0, 0, half, False), (1, 0, half, False))
    scan = lambda base, count, before: list(
        scan_backward(dssd, xin, pre, bd, held, cx, cb, heads, pick, base, count, before)
    )
    if quick:
        keep, send = pack(where, early, early_parts)
        dssd, keep, send = lax.optimization_barrier((dssd, keep, send))
        parts = sum_tensor(keep, send)
        carry = scan(blocks * 7 // 8, blocks // 8, None)
        carry[2], parts = lax.optimization_barrier((carry[2], parts))
        parts = sum_around(parts)
        carry = scan(blocks // 4, blocks * 5 // 8, carry)
        carry[2], parts = lax.optimization_barrier((carry[2], parts))
        early_part = sum_along_z(parts)
        carry = scan(0, blocks // 4, carry)
    else:
        early_part = scatter_plain(early, early_parts)
        carry = scan(0, blocks, None)
    dxin, dbd, _, _, _, gx, gb, gh = carry
    grad_x = nn(normed_t, dxin).astype(b16)
    grad_s = nn(normed_t, dbd).astype(b16)
    late = [grad_x, grad_s]
    late_parts = ((0, 0, half, False), (1, 0, STATE, False), (1, 2 * STATE, 128, True))
    if quick:
        late[0], early_part = lax.optimization_barrier((late[0], early_part))
        keep, send = pack(where, late, late_parts)
        dxin, dz, keep, send = lax.optimization_barrier((dxin, dz, keep, send))
        late_part = sum_tensor(keep, send)
    dnormed = nt(dz, w_z) + nt(dxin, w_x) + nt(dbd, w_s)
    if quick:
        dnormed, mixed, late_part = lax.optimization_barrier((dnormed, mixed, late_part))
    grad_pre = jnp.sum(dnormed * x * scale, axis=0)
    flat = jnp.concatenate(
        [
            jnp.sum(gx.reshape(6, 8, inner), axis=1).reshape(-1),
            grad_norm,
            jnp.sum(gb.reshape(5, 8, 2 * STATE), axis=1).reshape(-1),
            gh[0],
            gh[1],
            grad_pre,
        ]
    )
    flat = jnp.pad(flat, (0, -flat.shape[0] % 1024)).reshape(-1, 128)
    if quick:
        late_part = sum_around(late_part)
        flat = flat + swap(flat, 1, "tensor")
        flat = flat + swap(flat, 1) + swap(flat, 2) + swap(flat, 3)
    dn = dnormed * gain_pre
    grad_tokens = cotangent.astype(f32) + scale * dn
    grad_tokens = grad_tokens - x * (scale * scale * scale) * jnp.mean(dn * x, axis=1, keepdims=True)
    out = (x + nt(mixed, w_out_t)).astype(b16)
    if quick:
        flat, late_part = lax.optimization_barrier((flat, late_part))
        late_part = sum_along_z(late_part)
        summed = flat + swap(flat, 4) + swap(flat, 8) + swap(flat, 12)
    else:
        late_part = scatter_plain(late, late_parts)
        summed = lax.psum(flat, ("dp", "tensor"))
    summed = summed.reshape(-1)
    sizes = [5 * inner, inner, inner, 10 * STATE, Q, Q, model]
    pieces, begin = [], 0
    for size in sizes:
        pieces.append(summed[begin : begin + size])
        begin += size
    convx_sum, skip_lanes, norm_sum, convbc_sum, alog_sum, bias_sum, pre_sum = pieces

    def mine(vector, width):
        return lax.dynamic_slice_in_dim(vector, side * width, width, vector.ndim - 1)

    skip_sum = jnp.sum(skip_lanes.reshape(heads_count, HEAD), axis=1)
    z_out = jnp.stack([early_part[:, :half], late_part[:, :half]], axis=1)
    bc_part = both_sides(late_part[:, half : half + STATE].astype(b16), side, 1).astype(f32)
    dt_part = mine(late_part[:, half + STATE :], half_heads)
    return (
        unshuffle(out),
        unshuffle(grad_tokens.astype(b16)),
        pre_sum,
        z_out,
        bc_part,
        dt_part,
        mine(convx_sum.reshape(5, inner), half),
        convbc_sum.reshape(5, 2 * STATE),
        mine(alog_sum, half_heads),
        mine(bias_sum, half_heads),
        mine(skip_sum, half_heads),
        mine(norm_sum, half),
        early_part[:, half:].T,
    )


def solution(mesh):
    placed = (
        P(("dp", "tensor"), None),
        P(),
        P("dp", None, "tensor"),
        P("dp", None),
        P("dp", "tensor"),
        P(None, "tensor"),
        P(),
        P("tensor"),
        P("tensor"),
        P("tensor"),
        P("tensor"),
        P("tensor", "dp"),
        P(("dp", "tensor"), None),
    )
    return jax.shard_map(
        body,
        mesh=mesh,
        in_specs=placed,
        out_specs=(
            P(("dp", "tensor"), None),
            P(("dp", "tensor"), None),
            P(),
            P("dp", None, "tensor"),
            P("dp", None),
            P("dp", "tensor"),
            P(None, "tensor"),
            P(),
            P("tensor"),
            P("tensor"),
            P("tensor"),
            P("tensor"),
            P("tensor", "dp"),
        ),
        check_vma=False,
    )
```

```python
import functools

import jax
import jax.numpy as jnp
from jax import lax
from jax.experimental import pallas as pl
from jax.experimental.pallas import tpu as pltpu
from jax.sharding import PartitionSpec as P

LEN = 1024
Q = 128
HEAD = 64
STATE = 128
epsilon = 1e-05
f32 = jnp.float32
b16 = jnp.bfloat16
exact = lax.Precision.HIGHEST
MIB = 1024 * 1024


def nn(a, b, precision=None):
    return lax.dot_general(
        a, b, (((1,), (0,)), ((), ())), preferred_element_type=f32, precision=precision
    )


def nt(a, b, precision=None):
    return lax.dot_general(
        a, b, (((1,), (1,)), ((), ())), preferred_element_type=f32, precision=precision
    )


def tn(a, b):
    return lax.dot_general(a, b, (((0,), (0,)), ((), ())), preferred_element_type=f32)


def sigmoid(v):
    return 0.5 * jnp.tanh(0.5 * v) + 0.5


def softplus(v):
    return jnp.maximum(v, 0.0) + jnp.log1p(jnp.exp(-jnp.abs(v)))


def iota(axis):
    return lax.broadcasted_iota(jnp.int32, (Q, Q), axis)


def token(row):
    return ((row & 7) << 4) | (row >> 3)


def sublane(width):
    return lax.broadcasted_iota(jnp.int32, (24, width), 0) & 7


def with_past(here, past):
    mixed = jnp.where(
        sublane(here.shape[1]) == 0, pltpu.roll(past, 17, 0), pltpu.roll(here[Q - 24 :], 1, 0)
    )
    return jnp.concatenate([mixed, here], axis=0)


def with_future(here, future):
    mixed = jnp.where(
        sublane(here.shape[1]) == 7, pltpu.roll(future, 7, 0), pltpu.roll(here[:24], 23, 0)
    )
    return jnp.concatenate([here, mixed], axis=0)


def conv(padded, taps, lanes):
    total = taps[4:5, lanes]
    for k in range(4):
        total = total + taps[k : k + 1, lanes] * padded[8 * k : 8 * k + Q]
    return total


def fold(value):
    return jnp.sum(value.reshape(Q // 8, 8, value.shape[1]), axis=0)


def split_low(value, count):
    pieces = []
    for _ in range(count):
        piece = value.astype(b16)
        pieces.append(piece)
        value = value - piece.astype(f32)
    return jnp.concatenate(pieces, axis=1)


def head_rates(dt_raw, heads_ref, low_tri):
    step = softplus(dt_raw + heads_ref[0:1, :])
    decay = -step * heads_ref[1:2, :]
    sums = nn(low_tri, split_low(decay, 3))
    cum = sums[:, :Q] + sums[:, Q : 2 * Q] + sums[:, 2 * Q :]
    return step, decay, cum


def scan_forward_kernel(
    per_seq, pairs, base, resumed, *refs
):
    xin_ref, xhalo_ref, bd_ref, bdhalo_ref, cx_ref, cb_ref, heads_ref = refs[:7]
    y_ref, state_out_ref, pre_ref, rates_ref, state = refs[-5:]
    first = ((base + pl.program_id(0)) % per_seq) == 0

    if resumed:

        @pl.when(pl.program_id(0) == 0)
        def _():
            state[...] = refs[7][...]

    @pl.when(first)
    def _():
        state[...] = jnp.zeros_like(state)

    keep = jnp.where(first, 0.0, 1.0)
    rows, cols = token(iota(0)), token(iota(1))
    lower = rows >= cols
    low_tri = jnp.where(lower, 1.0, 0.0).astype(b16)
    left = iota(1) < HEAD
    bs = with_past(bd_ref[:, : 2 * STATE], bdhalo_ref[8:32, : 2 * STATE] * keep)
    pre_bc = conv(bs, cb_ref, slice(0, 2 * STATE))
    bc = pre_bc * sigmoid(pre_bc)
    b_low, c_low = bc[:, :STATE].astype(b16), bc[:, STATE:].astype(b16)
    gram = jnp.where(lower, nt(c_low, b_low), 0.0)
    step, decay, cum = head_rates(bd_ref[:, 2 * STATE :], heads_ref, low_tri)
    cum_rows = cum.T
    rates_ref[:, :Q] = step
    rates_ref[:, Q:] = cum
    b_turned = bc[:, :STATE].T.astype(b16)
    for p in range(pairs):
        sl = slice(p * Q, (p + 1) * Q)
        past = xhalo_ref[:, sl].astype(f32)[8:32] * keep
        pre = conv(with_past(xin_ref[:, sl].astype(f32), past), cx_ref, sl)
        pre_ref[:, sl] = pre.astype(b16)
        x = pre * sigmoid(pre)
        step2 = jnp.where(left, step[:, 2 * p : 2 * p + 1], step[:, 2 * p + 1 : 2 * p + 2])
        scaled = x * step2
        c0 = jnp.broadcast_to(cum[:, 2 * p : 2 * p + 1], (Q, Q))
        c1 = jnp.broadcast_to(cum[:, 2 * p + 1 : 2 * p + 2], (Q, Q))
        w0 = jnp.exp(jnp.minimum(c0 - cum_rows[2 * p : 2 * p + 1, :], 0.0)) * gram
        w1 = jnp.exp(jnp.minimum(c1 - cum_rows[2 * p + 1 : 2 * p + 2, :], 0.0)) * gram
        weights = jnp.concatenate([w0.astype(b16), w1.astype(b16)], axis=1)
        split = jnp.concatenate(
            [jnp.where(left, scaled, 0.0).astype(b16), jnp.where(left, 0.0, scaled).astype(b16)], axis=0
        )
        both = jnp.where(left, c0, c1)
        entering = state[:, sl]
        held = entering.astype(b16)
        state_out_ref[0, :, sl] = held
        y = nn(weights, split) + nn(c_low, held) * jnp.exp(both) + cx_ref[5:6, sl] * x
        y_ref[:, sl] = y.astype(b16)
        leaving = (scaled * jnp.exp(both[Q - 1 : Q, :] - both)).astype(b16)
        state[:, sl] = entering * jnp.exp(both[Q - 1 : Q, :]) + nn(b_turned, leaving)


def scan_forward(xin, bd, cx, cb, heads, base, count, before):
    rows, inner = xin.shape
    blocks, per_seq, pairs = rows // Q, LEN // Q, inner // Q
    wide = bd.shape[1]
    kept = [] if before is None else [before[4], *before[:4]]
    return pl.pallas_call(
        functools.partial(scan_forward_kernel, per_seq, pairs, base, before is not None),
        grid=(count,),
        in_specs=[
            pl.BlockSpec((Q, inner), lambda k: (base + k, 0)),
            pl.BlockSpec((32, inner), lambda k: (jnp.maximum((base + k) * (Q // 32) - 1, 0), 0)),
            pl.BlockSpec((Q, wide), lambda k: (base + k, 0)),
            pl.BlockSpec((32, wide), lambda k: (jnp.maximum((base + k) * (Q // 32) - 1, 0), 0)),
            pl.BlockSpec(cx.shape, lambda k: (0, 0)),
            pl.BlockSpec(cb.shape, lambda k: (0, 0)),
            pl.BlockSpec(heads.shape, lambda k: (0, 0)),
        ]
        + ([pl.BlockSpec((STATE, inner), lambda k: (0, 0))] + [pl.BlockSpec(memory_space=pl.ANY)] * 4 if kept else []),
        out_specs=[
            pl.BlockSpec((Q, inner), lambda k: (base + k, 0)),
            pl.BlockSpec((1, STATE, inner), lambda k: (base + k, 0, 0)),
            pl.BlockSpec((Q, inner), lambda k: (base + k, 0)),
            pl.BlockSpec((Q, 2 * Q), lambda k: (base + k, 0)),
            pl.BlockSpec((STATE, inner), lambda k: (0, 0)),
        ],
        out_shape=[
            jax.ShapeDtypeStruct((rows, inner), b16),
            jax.ShapeDtypeStruct((blocks, STATE, inner), b16),
            jax.ShapeDtypeStruct((rows, inner), b16),
            jax.ShapeDtypeStruct((rows, 2 * Q), f32),
            jax.ShapeDtypeStruct((STATE, inner), f32),
        ],
        input_output_aliases={8: 0, 9: 1, 10: 2, 11: 3} if kept else {},
        compiler_params=pltpu.CompilerParams(vmem_limit_bytes=56 * MIB),
        cost_estimate=pl.CostEstimate(flops=count * Q * inner * 6000, bytes_accessed=count * Q * inner * 8, transcendentals=count * Q * inner * 8),
        name="scan_forward",
    )(xin, xin, bd, bd, cx, cb, heads, *kept)


def scan_backward_kernel(
    per_seq, pairs, base, count, resumed, *refs
):
    (dy_ref, xin_ref, pre_ref, bd_ref, bdhalo_ref, held_ref, rates_ref, cx_ref, cb_ref, heads_ref, pick_ref) = refs[:11]
    (
        dxin_ref, dbd_ref, adjoint, xnext, bnext, gx_ref, gb_ref, gh_ref,
        xt, dye, lam_low, products, row_sums,
    ) = refs[-13:]
    step_id = pl.program_id(0)
    block = base + count - 1 - step_id
    first = (block % per_seq) == 0
    last = (block % per_seq) == per_seq - 1

    @pl.when(step_id == 0)
    def _():
        row_sums[...] = jnp.zeros_like(row_sums)
        for here, ref in enumerate((adjoint, xnext, bnext, gx_ref, gb_ref, gh_ref)):
            ref[...] = refs[11 + here][...] if resumed else jnp.zeros_like(ref)

    @pl.when(last)
    def _():
        adjoint[...] = jnp.zeros_like(adjoint)
        xnext[...] = jnp.zeros_like(xnext)
        bnext[...] = jnp.zeros_like(bnext)

    keep = jnp.where(first, 0.0, 1.0)
    rows, cols = token(iota(0)), token(iota(1))
    upper = cols >= rows
    left = iota(1) < HEAD
    left_low = jnp.where(left, 1.0, 0.0).astype(b16)
    right_low = jnp.where(left, 0.0, 1.0).astype(b16)
    ones_low = jnp.ones((8, Q), b16)
    lane_of = lax.broadcasted_iota(jnp.int32, (2 * Q, Q), 1)
    half_of = lax.broadcasted_iota(jnp.int32, (2 * Q, Q), 0) // Q
    bs = with_past(bd_ref[:, : 2 * STATE], bdhalo_ref[8:32, : 2 * STATE] * keep)
    pre_bc = conv(bs, cb_ref, slice(0, 2 * STATE))
    sig_bc = sigmoid(pre_bc)
    bc = pre_bc * sig_bc
    b_low, c_low = bc[:, :STATE].astype(b16), bc[:, STATE:].astype(b16)
    gram = jnp.where(upper, nt(b_low, c_low), 0.0)
    raw = bd_ref[:, 2 * STATE :]
    step, cum = rates_ref[:, :Q], rates_ref[:, Q:]
    cum_rows = cum.T
    c_turned = bc[:, STATE:].T.astype(b16)
    inner_states = []
    dgram = jnp.zeros((Q, Q), f32)
    col_sums = jnp.zeros((Q, Q), f32)
    for p in range(pairs):
        sl = slice(p * Q, (p + 1) * Q)
        pre = pre_ref[:, sl].astype(f32)
        sig = sigmoid(pre)
        x = pre * sig
        step2 = jnp.where(left, step[:, 2 * p : 2 * p + 1], step[:, 2 * p + 1 : 2 * p + 2])
        scaled = x * step2
        dy_low = dy_ref[:, sl]
        dy = dy_low.astype(f32)
        split = jnp.concatenate([dy_low * left_low, dy_low * right_low], axis=0)
        dweights = nt(scaled.astype(b16), split)
        c0 = jnp.broadcast_to(cum[:, 2 * p : 2 * p + 1], (Q, Q))
        c1 = jnp.broadcast_to(cum[:, 2 * p + 1 : 2 * p + 2], (Q, Q))
        weights, crossing = [], []
        for half, column in ((0, c0), (1, c1)):
            head = 2 * p + half
            fade = jnp.exp(jnp.minimum(cum_rows[head : head + 1, :] - column, 0.0))
            weights.append((fade * gram).astype(b16))
            faded = dweights[:, half * Q : (half + 1) * Q] * fade
            dgram = dgram + faded
            crossing.append((faded * gram).astype(b16))
        crossing = jnp.concatenate(crossing, axis=1)
        over_rows = nn(ones_low, crossing)
        row_sums[2 * p : 2 * p + 1, :] = over_rows[0:1, :Q]
        row_sums[2 * p + 1 : 2 * p + 2, :] = over_rows[0:1, Q:]
        col_sums = col_sums + nn(crossing, jnp.where(lane_of == 2 * p + half_of, 1.0, 0.0).astype(b16))
        both = jnp.where(left, c0, c1)
        tail = jnp.exp(both[Q - 1 : Q, :] - both)
        rise = jnp.exp(both)
        held = held_ref[0, :, sl]
        lam = adjoint[:, sl]
        lam_here = lam.astype(b16)
        lam_low[:, sl] = lam_here
        inner_states.append(jnp.sum(lam * held.astype(f32), axis=0, keepdims=True))
        dx_state = nn(b_low, lam_here) * tail
        dscaled = nn(jnp.concatenate(weights, axis=1), split) + dx_state
        dye_here = dy * rise
        products[0:Q, sl] = (dye_here * nn(c_low, held)).astype(b16)
        products[Q : 2 * Q, sl] = (scaled * dx_state).astype(b16)
        products[2 * Q :, sl] = (dscaled * x).astype(b16)
        xt[:, sl] = (scaled * tail).astype(b16)
        dye_low = dye_here.astype(b16)
        dye[:, sl] = dye_low
        adjoint[:, sl] = lam * rise[Q - 1 : Q, :] + nn(c_turned, dye_low)
        dx = dscaled * step2 + cx_ref[5:6, sl] * dy
        dpre = dx * (sig + x * (1.0 - sig))
        padded = with_future(dpre, xnext[:, sl])
        xnext[:, sl] = dpre[:24]
        dxin = jnp.zeros((Q, Q), f32)
        xin = xin_ref[:, sl].astype(f32)
        for k in range(4):
            ahead = padded[24 - 8 * k : 24 - 8 * k + Q]
            dxin = dxin + cx_ref[k : k + 1, sl] * ahead
            gx_ref[8 * k : 8 * k + 8, sl] += fold(ahead * xin)
        dxin_ref[:, sl] = dxin.astype(b16)
        gx_ref[32:40, sl] += fold(dpre)
        gx_ref[40:48, sl] += fold(dy * x)
    dgram_low = jnp.where(upper, dgram, 0.0)
    db = nn(dgram_low.astype(b16), c_low) + nt(xt[...], lam_low[...])
    dc = nn(dgram_low.T.astype(b16), b_low) + nt(dye[...], held_ref[0])
    total = cum[Q - 1 : Q, :]
    inner_states = jnp.concatenate(inner_states, axis=1)
    pick = pick_ref[...]
    summed = nn(products[...], pick)
    high = inner_states.astype(b16)
    low = (inner_states - high.astype(f32)).astype(b16)
    both_states = jnp.concatenate([jnp.broadcast_to(high, (8, high.shape[1])), jnp.broadcast_to(low, (8, low.shape[1]))], axis=0)
    state_sums = nn(both_states, pick)
    constant = jnp.exp(total) * (state_sums[0:1, :] + state_sums[8:9, :])
    up_tri = jnp.where(upper, 1.0, 0.0).astype(b16)
    strict = jnp.where(rows > cols, 1.0, 0.0).astype(b16)
    moved = jnp.concatenate([summed[:Q] - col_sums + row_sums[...].T, summed[Q : 2 * Q]], axis=0)
    crossed = nn(jnp.concatenate([up_tri, strict], axis=1), split_low(moved, 3))
    ddecay = crossed[:, :Q] + crossed[:, Q : 2 * Q] + crossed[:, 2 * Q :] + constant
    summed3 = summed[2 * Q :]
    dstep = summed3 - ddecay * heads_ref[1:2, :]
    draw = dstep * sigmoid(raw + heads_ref[0:1, :])
    gh_ref[0:1, :] += jnp.sum(ddecay * step, axis=0, keepdims=True) * -heads_ref[1:2, :]
    gh_ref[1:2, :] += jnp.sum(draw, axis=0, keepdims=True)
    dbc = jnp.concatenate([db, dc], axis=1)
    dpre_bc = dbc * sig_bc * (1.0 + pre_bc * (1.0 - sig_bc))
    padded = with_future(dpre_bc, bnext[...])
    bnext[...] = dpre_bc[:24]
    dbc_in = jnp.zeros((Q, 2 * STATE), f32)
    for k in range(4):
        ahead = padded[24 - 8 * k : 24 - 8 * k + Q]
        dbc_in = dbc_in + cb_ref[k : k + 1, :] * ahead
        gb_ref[8 * k : 8 * k + 8, :] += fold(ahead * bd_ref[:, : 2 * STATE])
    gb_ref[32:40, :] += fold(dpre_bc)
    dbd_ref[:, : 2 * STATE] = dbc_in.astype(b16)
    dbd_ref[:, 2 * STATE :] = draw.astype(b16)


def scan_backward(dy, xin, pre, bd, held, rates, cx, cb, heads, pick, base, count, before):
    rows, inner = xin.shape
    blocks, per_seq, pairs = rows // Q, LEN // Q, inner // Q
    wide = bd.shape[1]
    back = lambda k: base + count - 1 - k
    fixed = lambda shape: pl.BlockSpec(shape, lambda k: (0, 0))
    carry = [(STATE, inner), (24, inner), (24, 2 * STATE), (48, inner), (40, 2 * STATE), (8, Q)]
    kept = [] if before is None else [*before[2:], before[0], before[1]]
    return pl.pallas_call(
        functools.partial(scan_backward_kernel, per_seq, pairs, base, count, before is not None),
        grid=(count,),
        in_specs=[
            pl.BlockSpec((Q, inner), lambda k: (back(k), 0)),
            pl.BlockSpec((Q, inner), lambda k: (back(k), 0)),
            pl.BlockSpec((Q, inner), lambda k: (back(k), 0)),
            pl.BlockSpec((Q, wide), lambda k: (back(k), 0)),
            pl.BlockSpec((32, wide), lambda k: (jnp.maximum(back(k) * (Q // 32) - 1, 0), 0)),
            pl.BlockSpec((1, STATE, inner), lambda k: (back(k), 0, 0)),
            pl.BlockSpec((Q, 2 * Q), lambda k: (back(k), 0)),
            fixed(cx.shape),
            fixed(cb.shape),
            fixed(heads.shape),
            fixed(pick.shape),
        ]
        + ([fixed(shape) for shape in carry] + [pl.BlockSpec(memory_space=pl.ANY)] * 2 if kept else []),
        out_specs=[
            pl.BlockSpec((Q, inner), lambda k: (back(k), 0)),
            pl.BlockSpec((Q, wide), lambda k: (back(k), 0)),
        ]
        + [fixed(shape) for shape in carry],
        out_shape=[
            jax.ShapeDtypeStruct((rows, inner), b16),
            jax.ShapeDtypeStruct((rows, wide), b16),
        ]
        + [jax.ShapeDtypeStruct(shape, f32) for shape in carry],
        input_output_aliases={17: 0, 18: 1} if kept else {},
        scratch_shapes=[
            pltpu.VMEM((Q, inner), b16),
            pltpu.VMEM((Q, inner), b16),
            pltpu.VMEM((STATE, inner), b16),
            pltpu.VMEM((3 * Q, inner), b16),
            pltpu.VMEM((Q, Q), f32),
        ],
        compiler_params=pltpu.CompilerParams(vmem_limit_bytes=56 * MIB),
        cost_estimate=pl.CostEstimate(flops=count * Q * inner * 12000, bytes_accessed=count * Q * inner * 10, transcendentals=count * Q * inner * 8),
        name="scan_backward",
    )(dy, xin, pre, bd, bd, held, rates, cx, cb, heads, pick, *kept)


def gate_kernel(y, normed, cot, w_z, w_out_t, gain, mixed, dz, dssd, grad_norm, zs, hats, dhats):
    @pl.when(pl.program_id(0) == 0)
    def _():
        grad_norm[...] = jnp.zeros_like(grad_norm)

    rows, inner = y.shape
    chunks = [slice(begin, begin + 256) for begin in range(0, inner, 256)]
    squares = jnp.zeros((rows, 128), f32)
    for sl in chunks:
        z = nn(normed[...], w_z[:, sl])
        zs[:, sl] = z
        gated = y[:, sl].astype(f32) * (z * sigmoid(z))
        hats[:, sl] = gated
        square = gated * gated
        squares = squares + square[:, :128] + square[:, 128:]
    inv = lax.rsqrt(jnp.sum(squares, axis=1, keepdims=True) / inner + epsilon)
    crosses = jnp.zeros((rows, 128), f32)
    for sl in chunks:
        hat = hats[:, sl] * inv
        hats[:, sl] = hat
        mixed[:, sl] = (hat * gain[:, sl]).astype(b16)
        dmixed = nn(cot[...], w_out_t[:, sl])
        dhat = dmixed * gain[:, sl]
        dhats[:, sl] = dhat
        product = dmixed * hat
        grad_norm[:, sl] += jnp.sum(product.reshape(rows // 8, 8, 256), axis=0)
        product = dhat * hat
        crosses = crosses + product[:, :128] + product[:, 128:]
    cross = jnp.sum(crosses, axis=1, keepdims=True) / inner
    for sl in chunks:
        dgated = inv * (dhats[:, sl] - hats[:, sl] * cross)
        z = zs[:, sl]
        sig = sigmoid(z)
        gate = z * sig
        dz[:, sl] = (dgated * y[:, sl].astype(f32) * (sig + gate * (1.0 - sig))).astype(b16)
        dssd[:, sl] = (dgated * gate).astype(b16)


def gate_both(y, normed, cot, w_z, w_out_t, gain):
    rows, inner = y.shape
    model = normed.shape[1]
    size = 256
    tall = lambda width: pl.BlockSpec((size, width), lambda k: (k, 0))
    fixed = lambda shape: pl.BlockSpec(shape, lambda k: (0, 0))
    return pl.pallas_call(
        gate_kernel,
        grid=(rows // size,),
        in_specs=[tall(inner), tall(model), tall(model), fixed(w_z.shape), fixed(w_out_t.shape), fixed(gain.shape)],
        out_specs=[tall(inner)] * 3 + [fixed((8, inner))],
        out_shape=[jax.ShapeDtypeStruct((rows, inner), b16)] * 3 + [jax.ShapeDtypeStruct((8, inner), f32)],
        scratch_shapes=[pltpu.VMEM((size, inner), f32)] * 3,
        compiler_params=pltpu.CompilerParams(vmem_limit_bytes=56 * MIB),
        cost_estimate=pl.CostEstimate(flops=rows * inner * 8000, bytes_accessed=rows * inner * 10, transcendentals=rows * inner * 2),
        name="gate_both",
    )(y, normed, cot, w_z, w_out_t, gain)


def swap(value, bit, axis="dp"):
    count = lax.axis_size(axis)
    return lax.ppermute(value, axis, [(i, i ^ bit) for i in range(count)])


def tie(value, *others):
    return lax.optimization_barrier((value, *others))[0]


def fast(rows):
    return lax.axis_size("dp") == 16 and rows % 16 == 0


def along_z(shard):
    return jnp.stack([shard] + [swap(shard, z << 2) for z in (1, 2, 3)])


def around(column):
    return [column] + [swap(column, q) for q in (1, 2, 3)]


def merge_kernel(rows, layout, where_ref, *refs):
    mine, other, outs = refs[:4], refs[4:8], refs[8:]
    me, side = where_ref[0], where_ref[1]
    for q in range(4):
        for z in range(4):
            start = pl.multiple_of((me ^ (4 * z + q)) * rows, 16)
            for piece, half in ((mine[q], side), (other[q], 1 - side)):
                for out, (begin, width) in zip(outs, layout):
                    lane = pl.multiple_of(half * width, 128)
                    out[pl.ds(start, rows), pl.ds(lane, width)] = piece[z, :, begin : begin + width]


def merge(where, mine, other, layout):
    rows = mine[0].shape[1]
    whole = pl.BlockSpec(memory_space=pltpu.VMEM)
    return pl.pallas_call(
        functools.partial(merge_kernel, rows, layout),
        in_specs=[pl.BlockSpec(memory_space=pltpu.SMEM)] + [whole] * 8,
        out_specs=[whole] * len(layout),
        out_shape=[jax.ShapeDtypeStruct((16 * rows, 2 * width), b16) for _, width in layout],
        compiler_params=pltpu.CompilerParams(vmem_limit_bytes=16 * MIB),
        name="merge_weights",
    )(where, *mine, *other)


def gather_plain(shard, layout):
    full = lax.all_gather(shard, "dp", axis=0, tiled=True)
    return [
        lax.all_gather(full[:, begin : begin + width], "tensor", axis=1, tiled=True)
        for begin, width in layout
    ]


def put(where_ref, rows, piece, keep, send, lane, width, owner):
    me, side = where_ref[0], where_ref[1]

    def store(out):
        for q in range(4):
            for z in range(4):
                start = pl.multiple_of((me ^ (4 * z + q)) * rows, 16)
                out[q, z * rows : (z + 1) * rows, pl.ds(lane, width)] = piece[pl.ds(start, rows), :width]

    if owner is None:
        store(keep)
        store(send)
    else:
        pl.when(side == owner)(lambda: store(keep))
        pl.when(side != owner)(lambda: store(send))


def product_sums(weight, grad):
    total = jnp.zeros((weight.shape[0], 128), f32)
    for begin in range(0, weight.shape[1], 128):
        lanes = slice(begin, begin + 128)
        total = total + weight[:, lanes].astype(f32) * grad[:, lanes]
    return total


TILE = 256


def pack_early_kernel(rows, where_ref, normed_t, cot_t, dz, mixed, w_z, keep, send, sums, piece):
    step = pl.program_id(0)
    width = piece.shape[1]

    @pl.when(step == 0)
    def _():
        sums[...] = jnp.zeros_like(sums)

    @pl.when(step < 2)
    def _():
        grad = nn(normed_t[...], dz[...])
        sums[...] += product_sums(w_z, grad)
        piece[...] = grad.astype(b16)

    @pl.when(step >= 2)
    def _():
        piece[...] = nn(cot_t[...], mixed[...]).astype(b16)

    put(where_ref, rows, piece, keep, send, pl.multiple_of((step // 2) * width, 128), width, step % 2)


def pack_early(where, normed_t, cot_t, dz, mixed, w_z):
    model, tokens = normed_t.shape
    rows = model // 16
    inner = dz.shape[1]
    half = inner // 2
    fixed = lambda shape: pl.BlockSpec(shape, lambda t: (0,) * len(shape))
    first = lambda t: (0, jnp.minimum(t, 1))
    second = lambda t: (0, jnp.maximum(t - 2, 0))
    packed = (4, 4 * rows, inner)
    return pl.pallas_call(
        functools.partial(pack_early_kernel, rows),
        grid=(4,),
        in_specs=[
            pl.BlockSpec(memory_space=pltpu.SMEM),
            fixed((model, tokens)),
            fixed((model, tokens)),
            pl.BlockSpec((tokens, half), first),
            pl.BlockSpec((tokens, half), second),
            pl.BlockSpec((model, half), first),
        ],
        out_specs=[fixed(packed), fixed(packed), fixed((model, 128))],
        out_shape=[jax.ShapeDtypeStruct(packed, b16)] * 2 + [jax.ShapeDtypeStruct((model, 128), f32)],
        scratch_shapes=[pltpu.VMEM((model, half), b16)],
        compiler_params=pltpu.CompilerParams(vmem_limit_bytes=56 * MIB),
        cost_estimate=pl.CostEstimate(flops=4 * model * tokens * inner, bytes_accessed=4 * tokens * inner, transcendentals=0),
        name="pack_early",
    )(where, normed_t, cot_t, dz, mixed, w_z)


def pack_first_kernel(rows, where_ref, normed_t, dxin, dbd, w_x, w_s, sums_in, keep, send, sums, piece):
    step = pl.program_id(0)

    @pl.when(step == 0)
    def _():
        sums[...] = sums_in[...]

    @pl.when(step < 2)
    def _():
        grad = nn(normed_t[...], dxin[...])
        sums[...] += product_sums(w_x, grad)
        piece[:, :TILE] = grad.astype(b16)
        put(where_ref, rows, piece, keep, send, 0, TILE, step)

    @pl.when(step == 2)
    def _():
        grad = nn(normed_t[...], dbd[...])
        sums[...] += product_sums(w_s, grad)
        piece[...] = grad.astype(b16)
        put(where_ref, rows, piece, keep, send, TILE, piece.shape[1], None)


def pack_first(where, normed_t, dxin, dbd, w_x, w_s, sums):
    model, tokens = normed_t.shape
    rows = model // 16
    tiles = dxin.shape[1] // TILE
    shared = dbd.shape[1]
    fixed = lambda shape: pl.BlockSpec(shape, lambda t: (0,) * len(shape))
    chosen = lambda t: (0, jnp.minimum(t, 1) * (tiles // 2))
    packed = (4, 4 * rows, TILE + shared)
    return pl.pallas_call(
        functools.partial(pack_first_kernel, rows),
        grid=(3,),
        in_specs=[
            pl.BlockSpec(memory_space=pltpu.SMEM),
            fixed((model, tokens)),
            pl.BlockSpec((tokens, TILE), chosen),
            fixed(dbd.shape),
            pl.BlockSpec((model, TILE), chosen),
            fixed(w_s.shape),
            fixed((model, 128)),
        ],
        out_specs=[fixed(packed), fixed(packed), fixed((model, 128))],
        out_shape=[jax.ShapeDtypeStruct(packed, b16)] * 2 + [jax.ShapeDtypeStruct((model, 128), f32)],
        scratch_shapes=[pltpu.VMEM((model, shared), b16)],
        compiler_params=pltpu.CompilerParams(vmem_limit_bytes=20 * MIB),
        cost_estimate=pl.CostEstimate(flops=2 * model * tokens * (2 * TILE + shared), bytes_accessed=4 * tokens * TILE, transcendentals=0),
        name="pack_first",
    )(where, normed_t, dxin, dbd, w_x, w_s, sums)


def pack_second_kernel(
    rows, each, where_ref, normed_t, dxin, w_x, sums_in, gx, gb, gh, grad_norm, gain_pre, keep, send, sums, piece, flat
):
    step = pl.program_id(0)

    @pl.when(step == 0)
    def _():
        sums[...] = sums_in[...]

    grad = nn(normed_t[...], dxin[...])
    sums[...] += product_sums(w_x, grad)
    piece[...] = grad.astype(b16)
    put(where_ref, rows, piece, keep, send, pl.multiple_of((step % each) * TILE, 128), TILE, step // each)

    @pl.when(step == 2 * each - 1)
    def _():
        model = piece.shape[0]
        width = each * TILE
        lines = gx.shape[1] // width
        flat[...] = jnp.zeros_like(flat)
        for r in range(7):
            source = gx[8 * r : 8 * r + 8, :] if r < 6 else grad_norm[...]
            line = jnp.sum(source, axis=0, keepdims=True)
            for k in range(lines):
                flat[lines * r + k : lines * r + k + 1, :] = line[:, k * width : (k + 1) * width]
        for k in range(5):
            row, lane = 7 * lines + k // 2, 2 * STATE * (k % 2)
            flat[row : row + 1, lane : lane + 2 * STATE] = jnp.sum(
                gb[8 * k : 8 * k + 8, :], axis=0, keepdims=True
            )
        row = 7 * lines + 2
        flat[row : row + 1, 256:384] = gh[0:1, :]
        flat[row : row + 1, 384:512] = gh[1:2, :]
        total = sums[...]
        high = total.astype(b16)
        low = (total - high.astype(f32)).astype(b16)
        ones = jnp.ones((8, 128), b16)
        over = (nt(ones, high) + nt(ones, low))[0:1, :] / gain_pre[...]
        flat[row + 1 : row + 2, :] = over[:, :width]
        flat[row + 2 : row + 3, : model - width] = over[:, width:]
        flat_low = flat[...].astype(b16)
        for q in range(4):
            keep[q, 4 * rows :, :] = flat_low
            send[q, 4 * rows :, :] = flat_low


def pack_second(where, normed_t, dxin, w_x, sums, gx, gb, gh, grad_norm, gain_pre):
    model, tokens = normed_t.shape
    rows = model // 16
    half = dxin.shape[1] // TILE // 2
    each = half - 1
    fixed = lambda shape: pl.BlockSpec(shape, lambda t: (0,) * len(shape))
    chosen = lambda t: (0, (t // each) * half + 1 + t % each)
    packed = (4, 4 * rows + 32, each * TILE)
    return pl.pallas_call(
        functools.partial(pack_second_kernel, rows, each),
        grid=(2 * each,),
        in_specs=[
            pl.BlockSpec(memory_space=pltpu.SMEM),
            fixed((model, tokens)),
            pl.BlockSpec((tokens, TILE), chosen),
            pl.BlockSpec((model, TILE), chosen),
            fixed((model, 128)),
            fixed(gx.shape),
            fixed(gb.shape),
            fixed(gh.shape),
            fixed(grad_norm.shape),
            fixed(gain_pre.shape),
        ],
        out_specs=[fixed(packed), fixed(packed)],
        out_shape=[jax.ShapeDtypeStruct(packed, b16)] * 2,
        scratch_shapes=[
            pltpu.VMEM((model, 128), f32),
            pltpu.VMEM((model, TILE), b16),
            pltpu.VMEM((32, each * TILE), f32),
        ],
        compiler_params=pltpu.CompilerParams(vmem_limit_bytes=20 * MIB),
        cost_estimate=pl.CostEstimate(flops=4 * model * tokens * each * TILE, bytes_accessed=4 * tokens * each * TILE, transcendentals=0),
        name="pack_second",
    )(where, normed_t, dxin, w_x, sums, gx, gb, gh, grad_norm, gain_pre)


def finish_kernel(half, side_ref, *refs):
    early, first, second, pick = refs[:4], refs[4:8], refs[8:12], refs[12]
    (z_out, bc_out, dt_out, cx_out, cb_out, alog_out, bias_out, skip_out, norm_out, pre_out, w_out, lines) = refs[13:]
    side = side_ref[1]
    rows = early[0].shape[0]

    def total(parts):
        value = parts[0][...].astype(f32)
        for k in range(1, 4):
            value = value + parts[k][...].astype(f32)
        return value

    one, two, three = total(early), total(first), total(second)
    width = three.shape[1]
    z_out[:, 0, :] = one[:, :half]
    z_out[:, 1, :TILE] = two[:, :TILE]
    z_out[:, 1, TILE:] = three[:rows]
    w_out[...] = one[:, half:]
    bc_out[...] = two[:, TILE : TILE + 2 * STATE]
    heads = half // HEAD

    def own(value):
        return jnp.where(side == 0, value[:, :heads], value[:, heads : 2 * heads])

    dt_out[...] = own(two[:, TILE + 2 * STATE :]).T
    flat = three[rows:]
    count = 2 * half // width
    for r in range(7):
        for k in range(count):
            lines[r : r + 1, k * width : (k + 1) * width] = flat[count * r + k : count * r + k + 1, :]
    mine = lines[:, pl.ds(pl.multiple_of(side * half, 128), half)]
    cx_out[...] = mine[:5]
    high = mine[5:6].astype(b16)
    low = (mine[5:6] - high.astype(f32)).astype(b16)
    pair = jnp.concatenate([jnp.broadcast_to(high, (8, half)), jnp.broadcast_to(low, (8, half))], axis=0)
    sums = nn(pair, pick[...])
    skip_out[...] = (sums[0:1] + sums[8:9])[:, :heads]
    norm_out[...] = mine[6]
    row = 7 * count
    for k in range(5):
        lane = 2 * STATE * (k % 2)
        cb_out[k : k + 1, :] = flat[row + k // 2 : row + k // 2 + 1, lane : lane + 2 * STATE]
    alog_out[...] = own(flat[row + 2 : row + 3, 256:384])
    bias_out[...] = own(flat[row + 2 : row + 3, 384:512])
    model = pre_out.shape[0]
    pre_out[...] = jnp.concatenate([flat[row + 3], flat[row + 4, : model - width]])


def finish(where, early, first, second, pick, model, half):
    rows = early[0].shape[0]
    heads = half // HEAD
    whole = pl.BlockSpec(memory_space=pltpu.VMEM)
    shapes = [
        (rows, 2, half), (rows, 2 * STATE), (heads, rows), (5, half), (5, 2 * STATE),
        (1, heads), (1, heads), (1, heads), (half,), (model,), (rows, half),
    ]
    return pl.pallas_call(
        functools.partial(finish_kernel, half),
        in_specs=[pl.BlockSpec(memory_space=pltpu.SMEM)] + [whole] * 13,
        out_specs=[whole] * len(shapes),
        out_shape=[jax.ShapeDtypeStruct(shape, f32) for shape in shapes],
        scratch_shapes=[pltpu.VMEM((8, 2 * half), f32)],
        compiler_params=pltpu.CompilerParams(vmem_limit_bytes=16 * MIB),
        name="finish",
    )(where, *early, *first, *second, pick)


def sum_tensor(keep, send):
    got = swap(send, 1, "tensor")
    return (keep.astype(f32) + got.astype(f32)).astype(b16)


def sum_around(parts, rows):
    total = parts[0].astype(f32)
    for value in [swap(parts[q], q) for q in (1, 2, 3)]:
        total = total + value.astype(f32)
    split = total[: 4 * rows].reshape(4, rows, total.shape[1])
    if total.shape[0] > 4 * rows:
        shared = jnp.broadcast_to(total[None, 4 * rows :], (4, *total[4 * rows :].shape))
        split = jnp.concatenate([split, shared], axis=1)
    return split.astype(b16)


def along_z_parts(parts):
    return [parts[0]] + [swap(parts[z], z << 2) for z in (1, 2, 3)]


def scatter_plain(arrays, parts):
    halves = []
    for which, base, width, shared in parts:
        array = arrays[which][:, base : base + (width if shared else 2 * width)]
        if shared:
            array = lax.psum(array, "tensor")
        else:
            array = lax.psum_scatter(array, "tensor", scatter_dimension=1, tiled=True)
        halves.append(array)
    return lax.psum_scatter(
        jnp.concatenate(halves, axis=1).astype(f32), "dp", scatter_dimension=0, tiled=True
    )


def prepare_kernel(tokens, cot, gain, x_out, cot_out, normed_out, normed_t, cot_t):
    order = jnp.where(iota(1) == token(iota(0)), 1.0, 0.0).astype(b16)
    x = nn(order, tokens[...])
    x_out[...] = x.astype(b16)
    moved = nn(order, cot[...])
    cot_out[...] = moved.astype(b16)
    cot_t[...] = moved.T.astype(b16)
    normed = x * lax.rsqrt(jnp.mean(x * x, axis=1, keepdims=True) + epsilon) * gain[...]
    normed_out[...] = normed.astype(b16)
    normed_t[...] = normed.T.astype(b16)


def prepare(tokens, cot, gain):
    rows, model = tokens.shape
    tall = pl.BlockSpec((Q, model), lambda k: (k, 0))
    flat = pl.BlockSpec((model, Q), lambda k: (0, k))
    return pl.pallas_call(
        prepare_kernel,
        grid=(rows // Q,),
        in_specs=[tall, tall, pl.BlockSpec((1, model), lambda k: (0, 0))],
        out_specs=[tall, tall, tall, flat, flat],
        out_shape=[jax.ShapeDtypeStruct((rows, model), b16)] * 3 + [jax.ShapeDtypeStruct((model, rows), b16)] * 2,
        compiler_params=pltpu.CompilerParams(vmem_limit_bytes=56 * MIB),
        name="prepare",
    )(tokens, cot, gain)


def restore(value, out):
    order = jnp.where(iota(0) == token(iota(1)), 1.0, 0.0).astype(b16)
    value = value.astype(b16)
    for begin in range(0, value.shape[0], Q):
        out[begin : begin + Q, :] = nn(order, value[begin : begin + Q]).astype(b16)


def token_grads_kernel(dz, dxin, dbd, x, cot, w_z, w_x, w_s, gain, out):
    dn = nt(dz[...], w_z[...]) + nt(dxin[...], w_x[...]) + nt(dbd[...], w_s[...])
    dn = dn * gain[...]
    value = x[...].astype(f32)
    scale = lax.rsqrt(jnp.mean(value * value, axis=1, keepdims=True) + epsilon)
    inner = jnp.mean(dn * value, axis=1, keepdims=True)
    grad = cot[...].astype(f32) + scale * dn - value * (scale * scale * scale * inner)
    restore(grad, out)


def token_grads(dz, dxin, dbd, x, cot, w_z, w_x, w_s, gain):
    rows, model = x.shape
    tall = lambda value: pl.BlockSpec((256, value.shape[1]), lambda k: (k, 0))
    fixed = lambda value: pl.BlockSpec(value.shape, lambda k: (0, 0))
    return pl.pallas_call(
        token_grads_kernel,
        grid=(rows // 256,),
        in_specs=[tall(v) for v in (dz, dxin, dbd, x, cot)] + [fixed(v) for v in (w_z, w_x, w_s, gain)],
        out_specs=tall(x),
        out_shape=jax.ShapeDtypeStruct(x.shape, b16),
        compiler_params=pltpu.CompilerParams(vmem_limit_bytes=32 * MIB),
        cost_estimate=pl.CostEstimate(flops=rows * model * 8000, bytes_accessed=rows * model * 20, transcendentals=0),
        name="token_grads",
    )(dz, dxin, dbd, x, cot, w_z, w_x, w_s, gain)


def add_branch_kernel(mixed, x, w_out_t, out):
    restore(x[...].astype(f32) + nt(mixed[...], w_out_t[...]), out)


def add_branch(mixed, x, w_out_t):
    rows, model = x.shape
    tall = lambda value: pl.BlockSpec((256, value.shape[1]), lambda k: (k, 0))
    return pl.pallas_call(
        add_branch_kernel,
        grid=(rows // 256,),
        in_specs=[tall(mixed), tall(x), pl.BlockSpec(w_out_t.shape, lambda k: (0, 0))],
        out_specs=tall(x),
        out_shape=jax.ShapeDtypeStruct(x.shape, b16),
        compiler_params=pltpu.CompilerParams(vmem_limit_bytes=24 * MIB),
        cost_estimate=pl.CostEstimate(flops=rows * model * 4000, bytes_accessed=rows * model * 10, transcendentals=0),
        name="add_branch",
    )(mixed, x, w_out_t)


def both_sides(value, side, axis):
    other = swap(value, 1, "tensor")
    return jnp.where(
        side == 0, jnp.concatenate([value, other], axis), jnp.concatenate([other, value], axis)
    )


def body(
    tokens, pre_gain, w_zx, w_bc, w_dt, conv_x, conv_bc, a_log, dt_bias, skip_gain, norm_gain, w_out, cotangent,
):
    side = lax.axis_index("tensor")
    where = jnp.stack([lax.axis_index("dp"), side]).astype(jnp.int32)
    model, half = tokens.shape[1], conv_x.shape[1]
    inner = 2 * half
    half_heads = a_log.shape[0]
    heads_count = 2 * half_heads
    shard_rows = w_zx.shape[0]

    dt_pad = lax.dynamic_update_slice(
        jnp.zeros((shard_rows, 128), b16), w_dt, (0, side * half_heads)
    )
    bc_half = lax.dynamic_slice(w_bc, (0, side * STATE), (shard_rows, STATE))
    quick = fast(shard_rows)
    first = jnp.concatenate([w_zx[:, 1], bc_half, dt_pad], axis=1)
    second = jnp.concatenate([w_zx[:, 0], w_out.T], axis=1)
    first_layout = ((0, half), (half, STATE), (half + STATE, 128))
    second_layout = ((0, half), (half, half))
    gain_row = pre_gain.astype(f32)[None]
    if quick:
        column = along_z(first)
        tokens, cotangent, _ = lax.optimization_barrier((tokens, cotangent, column))
    ready = prepare(tokens, cotangent, gain_row)
    if quick:
        mine_first = around(column)
        later = along_z(tie(second, column))
        mine_first[3], *ready = lax.optimization_barrier((mine_first[3], *ready))
        other_first = [swap(part, 1, "tensor") for part in mine_first]
        mine_second = around(tie(later, *mine_first))
        w_x, full_bc, full_dt = merge(where, mine_first, other_first, first_layout)
    else:
        w_x, full_bc, full_dt = gather_plain(first, first_layout)
        w_z, w_out_t = gather_plain(second, second_layout)
    small = jnp.concatenate(
        [
            conv_x.astype(f32),
            norm_gain.astype(f32)[None],
            jnp.pad(jnp.concatenate([a_log, dt_bias, skip_gain]), (0, half - 3 * half_heads))[None],
            jnp.zeros((1, half), f32),
        ],
        axis=0,
    )
    small = both_sides(small[None], side, 0)
    wide = jnp.concatenate([small[0, :6], small[1, :6]], axis=1)
    gain_norm = wide[5:6]
    per_head = small[:, 6, : 3 * half_heads].reshape(2, 3, half_heads).transpose(1, 0, 2)
    per_head = per_head.reshape(3, heads_count)
    cx = jnp.concatenate(
        [wide[:5], jnp.repeat(per_head[2], HEAD)[None], jnp.zeros((2, inner), f32)], axis=0
    )
    cb = jnp.pad(conv_bc.astype(f32), ((0, 3), (0, 0)))
    heads = jnp.pad(
        jnp.stack([per_head[1], jnp.exp(per_head[0])]), ((0, 6), (0, Q - heads_count))
    )
    pick = (jnp.arange(inner)[:, None] // HEAD == jnp.arange(Q)[None, :]).astype(b16)

    w_s = jnp.concatenate([full_bc, full_dt[:, :128] + full_dt[:, 128:]], axis=1)
    x, cotangent, normed, normed_t, cot_t = ready
    xin = nn(normed, w_x).astype(b16)
    bd = nn(normed, w_s)
    blocks = tokens.shape[0] // Q
    started = list(scan_forward(xin, bd, cx, cb, heads, 0, blocks // 2, None))
    if quick:
        started[4], *mine_second = lax.optimization_barrier((started[4], *mine_second))
        other_second = [swap(part, 1, "tensor") for part in mine_second]
    ssd, held, pre, rates, ended = scan_forward(
        xin, bd, cx, cb, heads, blocks // 2, blocks - blocks // 2, started
    )
    if quick:
        other_second = lax.optimization_barrier((ended, *other_second))[1:]
        w_z, w_out_t = merge(where, mine_second, other_second, second_layout)
    mixed, dz, dssd, grad_norm = gate_both(ssd, normed, cotangent, w_z, w_out_t, gain_norm)
    scan = lambda base, count, before: list(
        scan_backward(dssd, xin, pre, bd, held, rates, cx, cb, heads, pick, base, count, before)
    )
    if quick:
        keep, send, sums = pack_early(where, normed_t, cot_t, dz, mixed, w_z)
        dssd, keep, send = lax.optimization_barrier((dssd, keep, send))
        parts = sum_tensor(keep, send)
        carry = scan(blocks * 7 // 8, blocks // 8, None)
        carry[2], parts = lax.optimization_barrier((carry[2], parts))
        parts = sum_around(parts, shard_rows)
        carry = scan(blocks // 4, blocks * 5 // 8, carry)
        carry[2], parts = lax.optimization_barrier((carry[2], parts))
        early = along_z_parts(parts)
        carry = scan(0, blocks // 4, carry)
        carry[0], carry[1], *early = lax.optimization_barrier((carry[0], carry[1], *early))
    else:
        early = scatter_plain(
            [nn(normed_t, dz).astype(b16), nn(cot_t, mixed).astype(b16)],
            ((0, 0, half, False), (1, 0, half, False)),
        )
        carry = scan(0, blocks, None)
    dxin, dbd, _, _, _, gx, gb, gh = carry
    if quick:
        keep, send, sums = pack_first(where, normed_t, dxin, dbd, w_x, w_s, sums)
        sums, keep, send = lax.optimization_barrier((sums, keep, send))
        parts_first = sum_tensor(keep, send)
        keep, send = pack_second(where, normed_t, dxin, w_x, sums, gx, gb, gh, grad_norm, gain_row)
        dxin, dz, mixed, keep, send, parts_first = lax.optimization_barrier(
            (dxin, dz, mixed, keep, send, parts_first)
        )
        parts_second = sum_tensor(keep, send)
        parts_first = sum_around(parts_first, shard_rows)
    grad_tokens = token_grads(dz, dxin, dbd, x, cotangent, w_z, w_x, w_s, gain_row)
    if quick:
        grad_tokens, mixed, parts_first, parts_second = lax.optimization_barrier(
            (grad_tokens, mixed, parts_first, parts_second)
        )
        second = sum_around(parts_second, shard_rows)
        first = along_z_parts(parts_first)
    out = add_branch(mixed, x, w_out_t)
    if quick:
        out, second, *first = lax.optimization_barrier((out, second, *first))
        second = along_z_parts(second)
        z_out, bc_out, dt_out, cx_out, cb_out, alog, bias, skip, norm, pre_sum, w_out_grad = finish(
            where, early, first, second, pick[:half], model, half
        )
        return (
            out, grad_tokens, pre_sum, z_out, bc_out, dt_out.T,
            cx_out, cb_out, alog[0], bias[0], skip[0], norm, w_out_grad.T,
        )
    late = scatter_plain(
        [nn(normed_t, dxin).astype(b16), nn(normed_t, dbd).astype(b16)],
        ((0, 0, half, False), (1, 0, 2 * STATE + 128, True)),
    )
    dnormed = nt(dz, w_z) + nt(dxin, w_x) + nt(dbd, w_s)
    wide_x = x.astype(f32)
    scale = lax.rsqrt(jnp.mean(wide_x * wide_x, axis=1, keepdims=True) + epsilon)
    grad_pre = jnp.sum(dnormed * wide_x * scale, axis=0)
    lines = jnp.sum(gx.reshape(6, 8, inner), axis=1)
    lines, norm, convbc, rates, grad_pre = lax.psum(
        (lines, jnp.sum(grad_norm, axis=0), jnp.sum(gb.reshape(5, 8, 2 * STATE), axis=1), gh[:2], grad_pre), ("dp", "tensor")
    )

    def mine(vector, width):
        return lax.dynamic_slice_in_dim(vector, side * width, width, vector.ndim - 1)

    skip = jnp.sum(lines[5].reshape(heads_count, HEAD), axis=1)
    return (
        out,
        grad_tokens,
        grad_pre,
        jnp.stack([early[:, :half], late[:, :half]], axis=1),
        late[:, half : half + 2 * STATE],
        mine(late[:, half + 2 * STATE :], half_heads),
        mine(lines[:5], half),
        convbc,
        mine(rates[0], half_heads),
        mine(rates[1], half_heads),
        mine(skip, half_heads),
        mine(norm, half),
        early[:, half:].T,
    )


def solution(mesh):
    placed = (
        P(("dp", "tensor"), None),
        P(),
        P("dp", None, "tensor"),
        P("dp", None),
        P("dp", "tensor"),
        P(None, "tensor"),
        P(),
        P("tensor"),
        P("tensor"),
        P("tensor"),
        P("tensor"),
        P("tensor", "dp"),
        P(("dp", "tensor"), None),
    )
    return jax.shard_map(
        body,
        mesh=mesh,
        in_specs=placed,
        out_specs=(
            P(("dp", "tensor"), None),
            P(("dp", "tensor"), None),
            P(),
            P("dp", None, "tensor"),
            P("dp", None),
            P("dp", "tensor"),
            P(None, "tensor"),
            P(),
            P("tensor"),
            P("tensor"),
            P("tensor"),
            P("tensor"),
            P("tensor", "dp"),
        ),
        check_vma=False,
    )
```

```python
import functools

import jax
import jax.numpy as jnp
from jax import lax
from jax.experimental import pallas as pl
from jax.experimental.pallas import tpu as pltpu
from jax.sharding import PartitionSpec as P

LEN = 1024
Q = 128
HEAD = 64
STATE = 128
epsilon = 1e-05
f32 = jnp.float32
b16 = jnp.bfloat16
exact = lax.Precision.HIGHEST
MIB = 1024 * 1024


def nn(a, b, precision=None):
    return lax.dot_general(
        a, b, (((1,), (0,)), ((), ())), preferred_element_type=f32, precision=precision
    )


def nt(a, b, precision=None):
    return lax.dot_general(
        a, b, (((1,), (1,)), ((), ())), preferred_element_type=f32, precision=precision
    )


def tn(a, b):
    return lax.dot_general(a, b, (((0,), (0,)), ((), ())), preferred_element_type=f32)


def sigmoid(v):
    return 0.5 * jnp.tanh(0.5 * v) + 0.5


def softplus(v):
    return jnp.maximum(v, 0.0) + jnp.log1p(jnp.exp(-jnp.abs(v)))


def iota(axis):
    return lax.broadcasted_iota(jnp.int32, (Q, Q), axis)


def token(row):
    return ((row & 7) << 4) | (row >> 3)


def sublane(width):
    return lax.broadcasted_iota(jnp.int32, (24, width), 0) & 7


def with_past(here, past):
    mixed = jnp.where(
        sublane(here.shape[1]) == 0, pltpu.roll(past, 17, 0), pltpu.roll(here[Q - 24 :], 1, 0)
    )
    return jnp.concatenate([mixed, here], axis=0)


def with_future(here, future):
    mixed = jnp.where(
        sublane(here.shape[1]) == 7, pltpu.roll(future, 7, 0), pltpu.roll(here[:24], 23, 0)
    )
    return jnp.concatenate([here, mixed], axis=0)


def conv(padded, taps, lanes):
    total = taps[4:5, lanes]
    for k in range(4):
        total = total + taps[k : k + 1, lanes] * padded[8 * k : 8 * k + Q]
    return total


def fold(value):
    return jnp.sum(value.reshape(Q // 8, 8, value.shape[1]), axis=0)


def split_low(value, count):
    pieces = []
    for _ in range(count):
        piece = value.astype(b16)
        pieces.append(piece)
        value = value - piece.astype(f32)
    return jnp.concatenate(pieces, axis=1)


def head_rates(dt_raw, heads_ref, low_tri):
    step = softplus(dt_raw + heads_ref[0:1, :])
    decay = -step * heads_ref[1:2, :]
    sums = nn(low_tri, split_low(decay, 3))
    cum = sums[:, :Q] + sums[:, Q : 2 * Q] + sums[:, 2 * Q :]
    return step, decay, cum


def scan_forward_kernel(
    per_seq, pairs, base, resumed, *refs
):
    xin_ref, xhalo_ref, bd_ref, bdhalo_ref, cx_ref, cb_ref, heads_ref = refs[:7]
    y_ref, state_out_ref, pre_ref, rates_ref, state = refs[-5:]
    first = ((base + pl.program_id(0)) % per_seq) == 0

    if resumed:

        @pl.when(pl.program_id(0) == 0)
        def _():
            state[...] = refs[7][...]

    @pl.when(first)
    def _():
        state[...] = jnp.zeros_like(state)

    keep = jnp.where(first, 0.0, 1.0)
    rows, cols = token(iota(0)), token(iota(1))
    lower = rows >= cols
    low_tri = jnp.where(lower, 1.0, 0.0).astype(b16)
    left = iota(1) < HEAD
    bs = with_past(bd_ref[:, : 2 * STATE], bdhalo_ref[8:32, : 2 * STATE] * keep)
    pre_bc = conv(bs, cb_ref, slice(0, 2 * STATE))
    bc = pre_bc * sigmoid(pre_bc)
    b_low, c_low = bc[:, :STATE].astype(b16), bc[:, STATE:].astype(b16)
    gram = jnp.where(lower, nt(c_low, b_low), 0.0)
    step, decay, cum = head_rates(bd_ref[:, 2 * STATE :], heads_ref, low_tri)
    cum_rows = cum.T
    rates_ref[:, :Q] = step
    rates_ref[:, Q:] = cum
    b_turned = bc[:, :STATE].T.astype(b16)
    leaving = []
    for p in range(pairs):
        sl = slice(p * Q, (p + 1) * Q)
        if p % 2 == 0:
            two = slice(p * Q, (p + 2) * Q)
            entering = state[:, two]
            held = entering.astype(b16)
            state_out_ref[0, :, two] = held
            carried = nn(c_low, held)
            rises = []
        past = xhalo_ref[:, sl].astype(f32)[8:32] * keep
        pre = conv(with_past(xin_ref[:, sl].astype(f32), past), cx_ref, sl)
        pre_ref[:, sl] = pre.astype(b16)
        x = pre * sigmoid(pre)
        step2 = jnp.where(left, step[:, 2 * p : 2 * p + 1], step[:, 2 * p + 1 : 2 * p + 2])
        scaled = x * step2
        c0 = jnp.broadcast_to(cum[:, 2 * p : 2 * p + 1], (Q, Q))
        c1 = jnp.broadcast_to(cum[:, 2 * p + 1 : 2 * p + 2], (Q, Q))
        w0 = jnp.exp(jnp.minimum(c0 - cum_rows[2 * p : 2 * p + 1, :], 0.0)) * gram
        w1 = jnp.exp(jnp.minimum(c1 - cum_rows[2 * p + 1 : 2 * p + 2, :], 0.0)) * gram
        weights = jnp.concatenate([w0.astype(b16), w1.astype(b16)], axis=1)
        split = jnp.concatenate(
            [jnp.where(left, scaled, 0.0).astype(b16), jnp.where(left, 0.0, scaled).astype(b16)], axis=0
        )
        both = jnp.where(left, c0, c1)
        rise = jnp.exp(both)
        here = carried[:, (p % 2) * Q : (p % 2 + 1) * Q]
        y = nn(weights, split) + here * rise + cx_ref[5:6, sl] * x
        y_ref[:, sl] = y.astype(b16)
        leaving.append((scaled * jnp.exp(both[Q - 1 : Q, :] - both)).astype(b16))
        rises.append(rise[Q - 1 : Q, :])
        if p % 2 == 1:
            added = nn(b_turned, jnp.concatenate(leaving[-2:], axis=1))
            state[:, two] = entering * jnp.concatenate(rises, axis=1) + added


def scan_forward(xin, bd, cx, cb, heads, base, count, before):
    rows, inner = xin.shape
    blocks, per_seq, pairs = rows // Q, LEN // Q, inner // Q
    wide = bd.shape[1]
    kept = [] if before is None else [before[4], *before[:4]]
    return pl.pallas_call(
        functools.partial(scan_forward_kernel, per_seq, pairs, base, before is not None),
        grid=(count,),
        in_specs=[
            pl.BlockSpec((Q, inner), lambda k: (base + k, 0)),
            pl.BlockSpec((32, inner), lambda k: (jnp.maximum((base + k) * (Q // 32) - 1, 0), 0)),
            pl.BlockSpec((Q, wide), lambda k: (base + k, 0)),
            pl.BlockSpec((32, wide), lambda k: (jnp.maximum((base + k) * (Q // 32) - 1, 0), 0)),
            pl.BlockSpec(cx.shape, lambda k: (0, 0)),
            pl.BlockSpec(cb.shape, lambda k: (0, 0)),
            pl.BlockSpec(heads.shape, lambda k: (0, 0)),
        ]
        + ([pl.BlockSpec((STATE, inner), lambda k: (0, 0))] + [pl.BlockSpec(memory_space=pl.ANY)] * 4 if kept else []),
        out_specs=[
            pl.BlockSpec((Q, inner), lambda k: (base + k, 0)),
            pl.BlockSpec((1, STATE, inner), lambda k: (base + k, 0, 0)),
            pl.BlockSpec((Q, inner), lambda k: (base + k, 0)),
            pl.BlockSpec((Q, 2 * Q), lambda k: (base + k, 0)),
            pl.BlockSpec((STATE, inner), lambda k: (0, 0)),
        ],
        out_shape=[
            jax.ShapeDtypeStruct((rows, inner), b16),
            jax.ShapeDtypeStruct((blocks, STATE, inner), b16),
            jax.ShapeDtypeStruct((rows, inner), b16),
            jax.ShapeDtypeStruct((rows, 2 * Q), f32),
            jax.ShapeDtypeStruct((STATE, inner), f32),
        ],
        input_output_aliases={8: 0, 9: 1, 10: 2, 11: 3} if kept else {},
        compiler_params=pltpu.CompilerParams(vmem_limit_bytes=56 * MIB),
        cost_estimate=pl.CostEstimate(flops=count * Q * inner * 6000, bytes_accessed=count * Q * inner * 8, transcendentals=count * Q * inner * 8),
        name="scan_forward",
    )(xin, xin, bd, bd, cx, cb, heads, *kept)


def scan_backward_kernel(
    per_seq, pairs, base, count, resumed, *refs
):
    (dy_ref, xin_ref, pre_ref, bd_ref, bdhalo_ref, held_ref, rates_ref, cx_ref, cb_ref, heads_ref, pick_ref) = refs[:11]
    (
        dxin_ref, dbd_ref, adjoint, xnext, bnext, gx_ref, gb_ref, gh_ref,
        xt, dye, lam_low, products, row_sums,
    ) = refs[-13:]
    step_id = pl.program_id(0)
    block = base + count - 1 - step_id
    first = (block % per_seq) == 0
    last = (block % per_seq) == per_seq - 1

    @pl.when(step_id == 0)
    def _():
        row_sums[...] = jnp.zeros_like(row_sums)
        for here, ref in enumerate((adjoint, xnext, bnext, gx_ref, gb_ref, gh_ref)):
            ref[...] = refs[11 + here][...] if resumed else jnp.zeros_like(ref)

    @pl.when(last)
    def _():
        adjoint[...] = jnp.zeros_like(adjoint)
        xnext[...] = jnp.zeros_like(xnext)
        bnext[...] = jnp.zeros_like(bnext)

    keep = jnp.where(first, 0.0, 1.0)
    rows, cols = token(iota(0)), token(iota(1))
    upper = cols >= rows
    left = iota(1) < HEAD
    left_low = jnp.where(left, 1.0, 0.0).astype(b16)
    right_low = jnp.where(left, 0.0, 1.0).astype(b16)
    ones_low = jnp.ones((8, Q), b16)
    lane_of = lax.broadcasted_iota(jnp.int32, (2 * Q, Q), 1)
    half_of = lax.broadcasted_iota(jnp.int32, (2 * Q, Q), 0) // Q
    bs = with_past(bd_ref[:, : 2 * STATE], bdhalo_ref[8:32, : 2 * STATE] * keep)
    pre_bc = conv(bs, cb_ref, slice(0, 2 * STATE))
    sig_bc = sigmoid(pre_bc)
    bc = pre_bc * sig_bc
    b_low, c_low = bc[:, :STATE].astype(b16), bc[:, STATE:].astype(b16)
    gram = jnp.where(upper, nt(b_low, c_low), 0.0)
    raw = bd_ref[:, 2 * STATE :]
    step, cum = rates_ref[:, :Q], rates_ref[:, Q:]
    cum_rows = cum.T
    c_turned = bc[:, STATE:].T.astype(b16)
    inner_states = []
    dgram = jnp.zeros((Q, Q), f32)
    col_sums = jnp.zeros((Q, Q), f32)
    for p in range(pairs):
        sl = slice(p * Q, (p + 1) * Q)
        if p % 2 == 0:
            two = slice(p * Q, (p + 2) * Q)
            held = held_ref[0, :, two]
            lam = adjoint[:, two]
            lam_here = lam.astype(b16)
            lam_low[:, two] = lam_here
            inner_states.append(jnp.sum(lam * held.astype(f32), axis=0, keepdims=True))
            carried_two = nn(c_low, held)
            back_two = nn(b_low, lam_here)
            rises = []
        half_lanes = slice((p % 2) * Q, (p % 2 + 1) * Q)
        pre = pre_ref[:, sl].astype(f32)
        sig = sigmoid(pre)
        x = pre * sig
        step2 = jnp.where(left, step[:, 2 * p : 2 * p + 1], step[:, 2 * p + 1 : 2 * p + 2])
        scaled = x * step2
        dy_low = dy_ref[:, sl]
        dy = dy_low.astype(f32)
        split = jnp.concatenate([dy_low * left_low, dy_low * right_low], axis=0)
        dweights = nt(scaled.astype(b16), split)
        c0 = jnp.broadcast_to(cum[:, 2 * p : 2 * p + 1], (Q, Q))
        c1 = jnp.broadcast_to(cum[:, 2 * p + 1 : 2 * p + 2], (Q, Q))
        weights, crossing = [], []
        for half, column in ((0, c0), (1, c1)):
            head = 2 * p + half
            fade = jnp.exp(jnp.minimum(cum_rows[head : head + 1, :] - column, 0.0))
            weights.append((fade * gram).astype(b16))
            faded = dweights[:, half * Q : (half + 1) * Q] * fade
            dgram = dgram + faded
            crossing.append((faded * gram).astype(b16))
        crossing = jnp.concatenate(crossing, axis=1)
        over_rows = nn(ones_low, crossing)
        row_sums[2 * p : 2 * p + 1, :] = over_rows[0:1, :Q]
        row_sums[2 * p + 1 : 2 * p + 2, :] = over_rows[0:1, Q:]
        col_sums = col_sums + nn(crossing, jnp.where(lane_of == 2 * p + half_of, 1.0, 0.0).astype(b16))
        both = jnp.where(left, c0, c1)
        tail = jnp.exp(both[Q - 1 : Q, :] - both)
        rise = jnp.exp(both)
        dx_state = back_two[:, half_lanes] * tail
        dscaled = nn(jnp.concatenate(weights, axis=1), split) + dx_state
        dye_here = dy * rise
        products[0:Q, sl] = (dye_here * carried_two[:, half_lanes]).astype(b16)
        products[Q : 2 * Q, sl] = (scaled * dx_state).astype(b16)
        products[2 * Q :, sl] = (dscaled * x).astype(b16)
        xt[:, sl] = (scaled * tail).astype(b16)
        dye[:, sl] = dye_here.astype(b16)
        rises.append(rise[Q - 1 : Q, :])
        if p % 2 == 1:
            adjoint[:, two] = lam * jnp.concatenate(rises, axis=1) + nn(c_turned, dye[:, two])
        dx = dscaled * step2 + cx_ref[5:6, sl] * dy
        dpre = dx * (sig + x * (1.0 - sig))
        padded = with_future(dpre, xnext[:, sl])
        xnext[:, sl] = dpre[:24]
        dxin = jnp.zeros((Q, Q), f32)
        xin = xin_ref[:, sl].astype(f32)
        for k in range(4):
            ahead = padded[24 - 8 * k : 24 - 8 * k + Q]
            dxin = dxin + cx_ref[k : k + 1, sl] * ahead
            gx_ref[8 * k : 8 * k + 8, sl] += fold(ahead * xin)
        dxin_ref[:, sl] = dxin.astype(b16)
        gx_ref[32:40, sl] += fold(dpre)
        gx_ref[40:48, sl] += fold(dy * x)
    dgram_low = jnp.where(upper, dgram, 0.0)
    db = nn(dgram_low.astype(b16), c_low) + nt(xt[...], lam_low[...])
    dc = nn(dgram_low.T.astype(b16), b_low) + nt(dye[...], held_ref[0])
    total = cum[Q - 1 : Q, :]
    inner_states = jnp.concatenate(inner_states, axis=1)
    pick = pick_ref[...]
    summed = nn(products[...], pick)
    high = inner_states.astype(b16)
    low = (inner_states - high.astype(f32)).astype(b16)
    both_states = jnp.concatenate([jnp.broadcast_to(high, (8, high.shape[1])), jnp.broadcast_to(low, (8, low.shape[1]))], axis=0)
    state_sums = nn(both_states, pick)
    constant = jnp.exp(total) * (state_sums[0:1, :] + state_sums[8:9, :])
    up_tri = jnp.where(upper, 1.0, 0.0).astype(b16)
    strict = jnp.where(rows > cols, 1.0, 0.0).astype(b16)
    moved = jnp.concatenate([summed[:Q] - col_sums + row_sums[...].T, summed[Q : 2 * Q]], axis=0)
    crossed = nn(jnp.concatenate([up_tri, strict], axis=1), split_low(moved, 3))
    ddecay = crossed[:, :Q] + crossed[:, Q : 2 * Q] + crossed[:, 2 * Q :] + constant
    summed3 = summed[2 * Q :]
    dstep = summed3 - ddecay * heads_ref[1:2, :]
    draw = dstep * sigmoid(raw + heads_ref[0:1, :])
    gh_ref[0:1, :] += jnp.sum(ddecay * step, axis=0, keepdims=True) * -heads_ref[1:2, :]
    gh_ref[1:2, :] += jnp.sum(draw, axis=0, keepdims=True)
    dbc = jnp.concatenate([db, dc], axis=1)
    dpre_bc = dbc * sig_bc * (1.0 + pre_bc * (1.0 - sig_bc))
    padded = with_future(dpre_bc, bnext[...])
    bnext[...] = dpre_bc[:24]
    dbc_in = jnp.zeros((Q, 2 * STATE), f32)
    for k in range(4):
        ahead = padded[24 - 8 * k : 24 - 8 * k + Q]
        dbc_in = dbc_in + cb_ref[k : k + 1, :] * ahead
        gb_ref[8 * k : 8 * k + 8, :] += fold(ahead * bd_ref[:, : 2 * STATE])
    gb_ref[32:40, :] += fold(dpre_bc)
    dbd_ref[:, : 2 * STATE] = dbc_in.astype(b16)
    dbd_ref[:, 2 * STATE :] = draw.astype(b16)


def scan_backward(dy, xin, pre, bd, held, rates, cx, cb, heads, pick, base, count, before):
    rows, inner = xin.shape
    blocks, per_seq, pairs = rows // Q, LEN // Q, inner // Q
    wide = bd.shape[1]
    back = lambda k: base + count - 1 - k
    fixed = lambda shape: pl.BlockSpec(shape, lambda k: (0, 0))
    carry = [(STATE, inner), (24, inner), (24, 2 * STATE), (48, inner), (40, 2 * STATE), (8, Q)]
    kept = [] if before is None else [*before[2:], before[0], before[1]]
    return pl.pallas_call(
        functools.partial(scan_backward_kernel, per_seq, pairs, base, count, before is not None),
        grid=(count,),
        in_specs=[
            pl.BlockSpec((Q, inner), lambda k: (back(k), 0)),
            pl.BlockSpec((Q, inner), lambda k: (back(k), 0)),
            pl.BlockSpec((Q, inner), lambda k: (back(k), 0)),
            pl.BlockSpec((Q, wide), lambda k: (back(k), 0)),
            pl.BlockSpec((32, wide), lambda k: (jnp.maximum(back(k) * (Q // 32) - 1, 0), 0)),
            pl.BlockSpec((1, STATE, inner), lambda k: (back(k), 0, 0)),
            pl.BlockSpec((Q, 2 * Q), lambda k: (back(k), 0)),
            fixed(cx.shape),
            fixed(cb.shape),
            fixed(heads.shape),
            fixed(pick.shape),
        ]
        + ([fixed(shape) for shape in carry] + [pl.BlockSpec(memory_space=pl.ANY)] * 2 if kept else []),
        out_specs=[
            pl.BlockSpec((Q, inner), lambda k: (back(k), 0)),
            pl.BlockSpec((Q, wide), lambda k: (back(k), 0)),
        ]
        + [fixed(shape) for shape in carry],
        out_shape=[
            jax.ShapeDtypeStruct((rows, inner), b16),
            jax.ShapeDtypeStruct((rows, wide), b16),
        ]
        + [jax.ShapeDtypeStruct(shape, f32) for shape in carry],
        input_output_aliases={17: 0, 18: 1} if kept else {},
        scratch_shapes=[
            pltpu.VMEM((Q, inner), b16),
            pltpu.VMEM((Q, inner), b16),
            pltpu.VMEM((STATE, inner), b16),
            pltpu.VMEM((3 * Q, inner), b16),
            pltpu.VMEM((Q, Q), f32),
        ],
        compiler_params=pltpu.CompilerParams(vmem_limit_bytes=56 * MIB),
        cost_estimate=pl.CostEstimate(flops=count * Q * inner * 12000, bytes_accessed=count * Q * inner * 10, transcendentals=count * Q * inner * 8),
        name="scan_backward",
    )(dy, xin, pre, bd, bd, held, rates, cx, cb, heads, pick, *kept)


def gate_kernel(y, normed, cot, w_z, w_out_t, gain, mixed, dz, dssd, grad_norm, zs, hats, dhats):
    @pl.when(pl.program_id(0) == 0)
    def _():
        grad_norm[...] = jnp.zeros_like(grad_norm)

    rows, inner = y.shape
    chunks = [slice(begin, begin + 256) for begin in range(0, inner, 256)]
    squares = jnp.zeros((rows, 128), f32)
    for sl in chunks:
        z = nn(normed[...], w_z[:, sl])
        zs[:, sl] = z
        gated = y[:, sl].astype(f32) * (z * sigmoid(z))
        hats[:, sl] = gated
        square = gated * gated
        squares = squares + square[:, :128] + square[:, 128:]
    inv = lax.rsqrt(jnp.sum(squares, axis=1, keepdims=True) / inner + epsilon)
    crosses = jnp.zeros((rows, 128), f32)
    for sl in chunks:
        hat = hats[:, sl] * inv
        hats[:, sl] = hat
        mixed[:, sl] = (hat * gain[:, sl]).astype(b16)
        dmixed = nn(cot[...], w_out_t[:, sl])
        dhat = dmixed * gain[:, sl]
        dhats[:, sl] = dhat
        product = dmixed * hat
        grad_norm[:, sl] += jnp.sum(product.reshape(rows // 8, 8, 256), axis=0)
        product = dhat * hat
        crosses = crosses + product[:, :128] + product[:, 128:]
    cross = jnp.sum(crosses, axis=1, keepdims=True) / inner
    for sl in chunks:
        dgated = inv * (dhats[:, sl] - hats[:, sl] * cross)
        z = zs[:, sl]
        sig = sigmoid(z)
        gate = z * sig
        dz[:, sl] = (dgated * y[:, sl].astype(f32) * (sig + gate * (1.0 - sig))).astype(b16)
        dssd[:, sl] = (dgated * gate).astype(b16)


def gate_both(y, normed, cot, w_z, w_out_t, gain):
    rows, inner = y.shape
    model = normed.shape[1]
    size = 256
    tall = lambda width: pl.BlockSpec((size, width), lambda k: (k, 0))
    fixed = lambda shape: pl.BlockSpec(shape, lambda k: (0, 0))
    return pl.pallas_call(
        gate_kernel,
        grid=(rows // size,),
        in_specs=[tall(inner), tall(model), tall(model), fixed(w_z.shape), fixed(w_out_t.shape), fixed(gain.shape)],
        out_specs=[tall(inner)] * 3 + [fixed((8, inner))],
        out_shape=[jax.ShapeDtypeStruct((rows, inner), b16)] * 3 + [jax.ShapeDtypeStruct((8, inner), f32)],
        scratch_shapes=[pltpu.VMEM((size, inner), f32)] * 3,
        compiler_params=pltpu.CompilerParams(vmem_limit_bytes=56 * MIB),
        cost_estimate=pl.CostEstimate(flops=rows * inner * 8000, bytes_accessed=rows * inner * 10, transcendentals=rows * inner * 2),
        name="gate_both",
    )(y, normed, cot, w_z, w_out_t, gain)


def swap(value, bit, axis="dp"):
    count = lax.axis_size(axis)
    return lax.ppermute(value, axis, [(i, i ^ bit) for i in range(count)])


def tie(value, *others):
    return lax.optimization_barrier((value, *others))[0]


def fast(rows):
    return lax.axis_size("dp") == 16 and rows % 16 == 0


def along_z(shard):
    return jnp.stack([shard] + [swap(shard, z << 2) for z in (1, 2, 3)])


def around(column):
    return [column] + [swap(column, q) for q in (1, 2, 3)]


def merge_kernel(rows, layout, where_ref, *refs):
    mine, other, outs = refs[:4], refs[4:8], refs[8:]
    me, side = where_ref[0], where_ref[1]
    for q in range(4):
        for z in range(4):
            start = pl.multiple_of((me ^ (4 * z + q)) * rows, 16)
            for piece, half in ((mine[q], side), (other[q], 1 - side)):
                for out, (begin, width) in zip(outs, layout):
                    lane = pl.multiple_of(half * width, 128)
                    out[pl.ds(start, rows), pl.ds(lane, width)] = piece[z, :, begin : begin + width]


def merge(where, mine, other, layout):
    rows = mine[0].shape[1]
    whole = pl.BlockSpec(memory_space=pltpu.VMEM)
    return pl.pallas_call(
        functools.partial(merge_kernel, rows, layout),
        in_specs=[pl.BlockSpec(memory_space=pltpu.SMEM)] + [whole] * 8,
        out_specs=[whole] * len(layout),
        out_shape=[jax.ShapeDtypeStruct((16 * rows, 2 * width), b16) for _, width in layout],
        compiler_params=pltpu.CompilerParams(vmem_limit_bytes=16 * MIB),
        name="merge_weights",
    )(where, *mine, *other)


def gather_plain(shard, layout):
    full = lax.all_gather(shard, "dp", axis=0, tiled=True)
    return [
        lax.all_gather(full[:, begin : begin + width], "tensor", axis=1, tiled=True)
        for begin, width in layout
    ]


def put(where_ref, rows, piece, keep, send, lane, width, owner):
    me, side = where_ref[0], where_ref[1]

    def store(out):
        for q in range(4):
            for z in range(4):
                start = pl.multiple_of((me ^ (4 * z + q)) * rows, 16)
                out[q, z * rows : (z + 1) * rows, pl.ds(lane, width)] = piece[pl.ds(start, rows), :width]

    if owner is None:
        store(keep)
        store(send)
    else:
        pl.when(side == owner)(lambda: store(keep))
        pl.when(side != owner)(lambda: store(send))


def product_sums(weight, grad):
    total = jnp.zeros((weight.shape[0], 128), f32)
    for begin in range(0, weight.shape[1], 128):
        lanes = slice(begin, begin + 128)
        total = total + weight[:, lanes].astype(f32) * grad[:, lanes]
    return total


TILE = 256


def pack_whole_kernel(rows, weighted, where_ref, left, right, *refs):
    step = pl.program_id(0)
    grad = nn(left[...], right[...])
    if weighted:
        weight, keep, send, sums, piece = refs

        @pl.when(step == 0)
        def _():
            sums[...] = jnp.zeros_like(sums)

        sums[...] += product_sums(weight, grad)
    else:
        keep, send, piece = refs
    piece[...] = grad.astype(b16)
    put(where_ref, rows, piece, keep, send, 0, piece.shape[1], step)


def pack_whole(where, left, right, weight=None):
    model, tokens = left.shape
    rows = model // 16
    half = right.shape[1] // 2
    fixed = lambda shape: pl.BlockSpec(shape, lambda t: (0,) * len(shape))
    packed = (4, 4 * rows, half)
    weights = [] if weight is None else [weight]
    extra = [(model, 128)] * len(weights)
    return pl.pallas_call(
        functools.partial(pack_whole_kernel, rows, bool(weights)),
        grid=(2,),
        in_specs=[
            pl.BlockSpec(memory_space=pltpu.SMEM),
            fixed((model, tokens)),
            pl.BlockSpec((tokens, half), lambda t: (0, t)),
        ]
        + [pl.BlockSpec((model, half), lambda t: (0, t))] * len(weights),
        out_specs=[fixed(packed), fixed(packed)] + [fixed(shape) for shape in extra],
        out_shape=[jax.ShapeDtypeStruct(packed, b16)] * 2 + [jax.ShapeDtypeStruct(shape, f32) for shape in extra],
        scratch_shapes=[pltpu.VMEM((model, half), b16)],
        compiler_params=pltpu.CompilerParams(vmem_limit_bytes=30 * MIB),
        cost_estimate=pl.CostEstimate(flops=8 * model * tokens * half, bytes_accessed=8 * tokens * half, transcendentals=0),
        name="pack_whole",
    )(where, left, right, *weights)


def pack_first_kernel(rows, where_ref, normed_t, dxin, dbd, w_x, w_s, sums_in, keep, send, sums, piece):
    step = pl.program_id(0)

    @pl.when(step == 0)
    def _():
        sums[...] = sums_in[...]

    @pl.when(step < 2)
    def _():
        grad = nn(normed_t[...], dxin[...])
        sums[...] += product_sums(w_x, grad)
        piece[:, :TILE] = grad.astype(b16)
        put(where_ref, rows, piece, keep, send, 0, TILE, step)

    @pl.when(step == 2)
    def _():
        grad = nn(normed_t[...], dbd[...])
        sums[...] += product_sums(w_s, grad)
        piece[...] = grad.astype(b16)
        put(where_ref, rows, piece, keep, send, TILE, piece.shape[1], None)


def pack_first(where, normed_t, dxin, dbd, w_x, w_s, sums):
    model, tokens = normed_t.shape
    rows = model // 16
    tiles = dxin.shape[1] // TILE
    shared = dbd.shape[1]
    fixed = lambda shape: pl.BlockSpec(shape, lambda t: (0,) * len(shape))
    chosen = lambda t: (0, jnp.minimum(t, 1) * (tiles // 2))
    packed = (4, 4 * rows, TILE + shared)
    return pl.pallas_call(
        functools.partial(pack_first_kernel, rows),
        grid=(3,),
        in_specs=[
            pl.BlockSpec(memory_space=pltpu.SMEM),
            fixed((model, tokens)),
            pl.BlockSpec((tokens, TILE), chosen),
            fixed(dbd.shape),
            pl.BlockSpec((model, TILE), chosen),
            fixed(w_s.shape),
            fixed((model, 128)),
        ],
        out_specs=[fixed(packed), fixed(packed), fixed((model, 128))],
        out_shape=[jax.ShapeDtypeStruct(packed, b16)] * 2 + [jax.ShapeDtypeStruct((model, 128), f32)],
        scratch_shapes=[pltpu.VMEM((model, shared), b16)],
        compiler_params=pltpu.CompilerParams(vmem_limit_bytes=20 * MIB),
        cost_estimate=pl.CostEstimate(flops=2 * model * tokens * (2 * TILE + shared), bytes_accessed=4 * tokens * TILE, transcendentals=0),
        name="pack_first",
    )(where, normed_t, dxin, dbd, w_x, w_s, sums)


def pack_second_kernel(
    rows, each, where_ref, normed_t, dxin, w_x, sums_in, gx, gb, gh, grad_norm, gain_pre, keep, send, sums, piece, flat
):
    step = pl.program_id(0)

    @pl.when(step == 0)
    def _():
        sums[...] = sums_in[...]

    grad = nn(normed_t[...], dxin[...])
    sums[...] += product_sums(w_x, grad)
    piece[...] = grad.astype(b16)
    put(where_ref, rows, piece, keep, send, pl.multiple_of((step % each) * TILE, 128), TILE, step // each)

    @pl.when(step == 2 * each - 1)
    def _():
        model = piece.shape[0]
        width = each * TILE
        lines = gx.shape[1] // width
        flat[...] = jnp.zeros_like(flat)
        for r in range(7):
            source = gx[8 * r : 8 * r + 8, :] if r < 6 else grad_norm[...]
            line = jnp.sum(source, axis=0, keepdims=True)
            for k in range(lines):
                flat[lines * r + k : lines * r + k + 1, :] = line[:, k * width : (k + 1) * width]
        for k in range(5):
            row, lane = 7 * lines + k // 2, 2 * STATE * (k % 2)
            flat[row : row + 1, lane : lane + 2 * STATE] = jnp.sum(
                gb[8 * k : 8 * k + 8, :], axis=0, keepdims=True
            )
        row = 7 * lines + 2
        flat[row : row + 1, 256:384] = gh[0:1, :]
        flat[row : row + 1, 384:512] = gh[1:2, :]
        total = sums[...]
        high = total.astype(b16)
        low = (total - high.astype(f32)).astype(b16)
        ones = jnp.ones((8, 128), b16)
        over = (nt(ones, high) + nt(ones, low))[0:1, :] / gain_pre[...]
        flat[row + 1 : row + 2, :] = over[:, :width]
        flat[row + 2 : row + 3, : model - width] = over[:, width:]
        flat_low = flat[...].astype(b16)
        for q in range(4):
            keep[q, 4 * rows :, :] = flat_low
            send[q, 4 * rows :, :] = flat_low


def pack_second(where, normed_t, dxin, w_x, sums, gx, gb, gh, grad_norm, gain_pre):
    model, tokens = normed_t.shape
    rows = model // 16
    half = dxin.shape[1] // TILE // 2
    each = half - 1
    fixed = lambda shape: pl.BlockSpec(shape, lambda t: (0,) * len(shape))
    chosen = lambda t: (0, (t // each) * half + 1 + t % each)
    packed = (4, 4 * rows + 32, each * TILE)
    return pl.pallas_call(
        functools.partial(pack_second_kernel, rows, each),
        grid=(2 * each,),
        in_specs=[
            pl.BlockSpec(memory_space=pltpu.SMEM),
            fixed((model, tokens)),
            pl.BlockSpec((tokens, TILE), chosen),
            pl.BlockSpec((model, TILE), chosen),
            fixed((model, 128)),
            fixed(gx.shape),
            fixed(gb.shape),
            fixed(gh.shape),
            fixed(grad_norm.shape),
            fixed(gain_pre.shape),
        ],
        out_specs=[fixed(packed), fixed(packed)],
        out_shape=[jax.ShapeDtypeStruct(packed, b16)] * 2,
        scratch_shapes=[
            pltpu.VMEM((model, 128), f32),
            pltpu.VMEM((model, TILE), b16),
            pltpu.VMEM((32, each * TILE), f32),
        ],
        compiler_params=pltpu.CompilerParams(vmem_limit_bytes=20 * MIB),
        cost_estimate=pl.CostEstimate(flops=4 * model * tokens * each * TILE, bytes_accessed=4 * tokens * each * TILE, transcendentals=0),
        name="pack_second",
    )(where, normed_t, dxin, w_x, sums, gx, gb, gh, grad_norm, gain_pre)


def finish_kernel(half, side_ref, *refs):
    early, first, second, pick = refs[:2], refs[2:4], refs[4:8], refs[8]
    (z_out, bc_out, dt_out, cx_out, cb_out, alog_out, bias_out, skip_out, norm_out, pre_out, w_out, lines) = refs[9:]
    side = side_ref[1]
    rows = first[0].shape[0]

    def total(parts):
        value = parts[0][...].astype(f32)
        for k in range(1, len(parts)):
            value = value + parts[k][...].astype(f32)
        return value

    one, two, three = total(early), total(first), total(second)
    width = three.shape[1]
    z_out[:, 0, :] = one[:, :half]
    z_out[:, 1, :TILE] = two[:, :TILE]
    z_out[:, 1, TILE:] = three[:rows]
    w_out[...] = one[:, half:]
    bc_out[...] = two[:, TILE : TILE + 2 * STATE]
    heads = half // HEAD

    def own(value):
        return jnp.where(side == 0, value[:, :heads], value[:, heads : 2 * heads])

    dt_out[...] = own(two[:, TILE + 2 * STATE :]).T
    flat = three[rows:]
    count = 2 * half // width
    for r in range(7):
        for k in range(count):
            lines[r : r + 1, k * width : (k + 1) * width] = flat[count * r + k : count * r + k + 1, :]
    mine = lines[:, pl.ds(pl.multiple_of(side * half, 128), half)]
    cx_out[...] = mine[:5]
    high = mine[5:6].astype(b16)
    low = (mine[5:6] - high.astype(f32)).astype(b16)
    pair = jnp.concatenate([jnp.broadcast_to(high, (8, half)), jnp.broadcast_to(low, (8, half))], axis=0)
    sums = nn(pair, pick[...])
    skip_out[...] = (sums[0:1] + sums[8:9])[:, :heads]
    norm_out[...] = mine[6]
    row = 7 * count
    for k in range(5):
        lane = 2 * STATE * (k % 2)
        cb_out[k : k + 1, :] = flat[row + k // 2 : row + k // 2 + 1, lane : lane + 2 * STATE]
    alog_out[...] = own(flat[row + 2 : row + 3, 256:384])
    bias_out[...] = own(flat[row + 2 : row + 3, 384:512])
    model = pre_out.shape[0]
    pre_out[...] = jnp.concatenate([flat[row + 3], flat[row + 4, : model - width]])


def finish(where, early, first, second, pick, model, half):
    rows = first[0].shape[0]
    heads = half // HEAD
    whole = pl.BlockSpec(memory_space=pltpu.VMEM)
    shapes = [
        (rows, 2, half), (rows, 2 * STATE), (heads, rows), (5, half), (5, 2 * STATE),
        (1, heads), (1, heads), (1, heads), (half,), (model,), (rows, half),
    ]
    return pl.pallas_call(
        functools.partial(finish_kernel, half),
        in_specs=[pl.BlockSpec(memory_space=pltpu.SMEM)] + [whole] * 9,
        out_specs=[whole] * len(shapes),
        out_shape=[jax.ShapeDtypeStruct(shape, f32) for shape in shapes],
        scratch_shapes=[pltpu.VMEM((8, 2 * half), f32)],
        compiler_params=pltpu.CompilerParams(vmem_limit_bytes=16 * MIB),
        name="finish",
    )(where, *early, *first, *second, pick)


def sum_tensor(keep, send):
    got = swap(send, 1, "tensor")
    return (keep.astype(f32) + got.astype(f32)).astype(b16)


def sum_around(parts, rows):
    total = parts[0].astype(f32)
    for value in [swap(parts[q], q) for q in (1, 2, 3)]:
        total = total + value.astype(f32)
    split = total[: 4 * rows].reshape(4, rows, total.shape[1])
    if total.shape[0] > 4 * rows:
        shared = jnp.broadcast_to(total[None, 4 * rows :], (4, *total[4 * rows :].shape))
        split = jnp.concatenate([split, shared], axis=1)
    return split.astype(b16)


def plus(a, b):
    return (a.astype(f32) + b.astype(f32)).astype(b16)


def along_z_parts(parts):
    return [parts[0]] + [swap(parts[z], z << 2) for z in (1, 2, 3)]


def scatter_plain(arrays, parts):
    halves = []
    for which, base, width, shared in parts:
        array = arrays[which][:, base : base + (width if shared else 2 * width)]
        if shared:
            array = lax.psum(array, "tensor")
        else:
            array = lax.psum_scatter(array, "tensor", scatter_dimension=1, tiled=True)
        halves.append(array)
    return lax.psum_scatter(
        jnp.concatenate(halves, axis=1).astype(f32), "dp", scatter_dimension=0, tiled=True
    )


def prepare_kernel(tokens, cot, gain, x_out, cot_out, normed_out, normed_t, cot_t):
    order = jnp.where(iota(1) == token(iota(0)), 1.0, 0.0).astype(b16)
    x = nn(order, tokens[...])
    x_out[...] = x.astype(b16)
    moved = nn(order, cot[...])
    cot_out[...] = moved.astype(b16)
    cot_t[...] = moved.T.astype(b16)
    normed = x * lax.rsqrt(jnp.mean(x * x, axis=1, keepdims=True) + epsilon) * gain[...]
    normed_out[...] = normed.astype(b16)
    normed_t[...] = normed.T.astype(b16)


def prepare(tokens, cot, gain):
    rows, model = tokens.shape
    tall = pl.BlockSpec((Q, model), lambda k: (k, 0))
    flat = pl.BlockSpec((model, Q), lambda k: (0, k))
    return pl.pallas_call(
        prepare_kernel,
        grid=(rows // Q,),
        in_specs=[tall, tall, pl.BlockSpec((1, model), lambda k: (0, 0))],
        out_specs=[tall, tall, tall, flat, flat],
        out_shape=[jax.ShapeDtypeStruct((rows, model), b16)] * 3 + [jax.ShapeDtypeStruct((model, rows), b16)] * 2,
        compiler_params=pltpu.CompilerParams(vmem_limit_bytes=56 * MIB),
        name="prepare",
    )(tokens, cot, gain)


def restore(value, out):
    order = jnp.where(iota(0) == token(iota(1)), 1.0, 0.0).astype(b16)
    value = value.astype(b16)
    for begin in range(0, value.shape[0], Q):
        out[begin : begin + Q, :] = nn(order, value[begin : begin + Q]).astype(b16)


def token_grads_kernel(dz, dxin, dbd, x, cot, w_z, w_x, w_s, gain, out):
    dn = nt(dz[...], w_z[...]) + nt(dxin[...], w_x[...]) + nt(dbd[...], w_s[...])
    dn = dn * gain[...]
    value = x[...].astype(f32)
    scale = lax.rsqrt(jnp.mean(value * value, axis=1, keepdims=True) + epsilon)
    inner = jnp.mean(dn * value, axis=1, keepdims=True)
    grad = cot[...].astype(f32) + scale * dn - value * (scale * scale * scale * inner)
    restore(grad, out)


def token_grads(dz, dxin, dbd, x, cot, w_z, w_x, w_s, gain):
    rows, model = x.shape
    tall = lambda value: pl.BlockSpec((256, value.shape[1]), lambda k: (k, 0))
    fixed = lambda value: pl.BlockSpec(value.shape, lambda k: (0, 0))
    return pl.pallas_call(
        token_grads_kernel,
        grid=(rows // 256,),
        in_specs=[tall(v) for v in (dz, dxin, dbd, x, cot)] + [fixed(v) for v in (w_z, w_x, w_s, gain)],
        out_specs=tall(x),
        out_shape=jax.ShapeDtypeStruct(x.shape, b16),
        compiler_params=pltpu.CompilerParams(vmem_limit_bytes=32 * MIB),
        cost_estimate=pl.CostEstimate(flops=rows * model * 8000, bytes_accessed=rows * model * 20, transcendentals=0),
        name="token_grads",
    )(dz, dxin, dbd, x, cot, w_z, w_x, w_s, gain)


def add_branch_kernel(mixed, x, w_out_t, out):
    restore(x[...].astype(f32) + nt(mixed[...], w_out_t[...]), out)


def add_branch(mixed, x, w_out_t):
    rows, model = x.shape
    tall = lambda value: pl.BlockSpec((256, value.shape[1]), lambda k: (k, 0))
    return pl.pallas_call(
        add_branch_kernel,
        grid=(rows // 256,),
        in_specs=[tall(mixed), tall(x), pl.BlockSpec(w_out_t.shape, lambda k: (0, 0))],
        out_specs=tall(x),
        out_shape=jax.ShapeDtypeStruct(x.shape, b16),
        compiler_params=pltpu.CompilerParams(vmem_limit_bytes=24 * MIB),
        cost_estimate=pl.CostEstimate(flops=rows * model * 4000, bytes_accessed=rows * model * 10, transcendentals=0),
        name="add_branch",
    )(mixed, x, w_out_t)


def both_sides(value, side, axis):
    other = swap(value, 1, "tensor")
    return jnp.where(
        side == 0, jnp.concatenate([value, other], axis), jnp.concatenate([other, value], axis)
    )


def body(
    tokens, pre_gain, w_zx, w_bc, w_dt, conv_x, conv_bc, a_log, dt_bias, skip_gain, norm_gain, w_out, cotangent,
):
    side = lax.axis_index("tensor")
    where = jnp.stack([lax.axis_index("dp"), side]).astype(jnp.int32)
    model, half = tokens.shape[1], conv_x.shape[1]
    inner = 2 * half
    half_heads = a_log.shape[0]
    heads_count = 2 * half_heads
    shard_rows = w_zx.shape[0]

    dt_pad = lax.dynamic_update_slice(
        jnp.zeros((shard_rows, 128), b16), w_dt, (0, side * half_heads)
    )
    bc_half = lax.dynamic_slice(w_bc, (0, side * STATE), (shard_rows, STATE))
    quick = fast(shard_rows)
    first = jnp.concatenate([w_zx[:, 1], bc_half, dt_pad], axis=1)
    second = jnp.concatenate([w_zx[:, 0], w_out.T], axis=1)
    first_layout = ((0, half), (half, STATE), (half + STATE, 128))
    second_layout = ((0, half), (half, half))
    gain_row = pre_gain.astype(f32)[None]
    if quick:
        column = along_z(first)
        tokens, cotangent, _ = lax.optimization_barrier((tokens, cotangent, column))
    ready = prepare(tokens, cotangent, gain_row)
    if quick:
        mine_first = around(column)
        later = along_z(tie(second, column))
        mine_first[3], *ready = lax.optimization_barrier((mine_first[3], *ready))
        other_first = [swap(part, 1, "tensor") for part in mine_first]
        mine_second = around(tie(later, *mine_first))
        w_x, full_bc, full_dt = merge(where, mine_first, other_first, first_layout)
    else:
        w_x, full_bc, full_dt = gather_plain(first, first_layout)
        w_z, w_out_t = gather_plain(second, second_layout)
    small = jnp.concatenate(
        [
            conv_x.astype(f32),
            norm_gain.astype(f32)[None],
            jnp.pad(jnp.concatenate([a_log, dt_bias, skip_gain]), (0, half - 3 * half_heads))[None],
            jnp.zeros((1, half), f32),
        ],
        axis=0,
    )
    small = both_sides(small[None], side, 0)
    wide = jnp.concatenate([small[0, :6], small[1, :6]], axis=1)
    gain_norm = wide[5:6]
    per_head = small[:, 6, : 3 * half_heads].reshape(2, 3, half_heads).transpose(1, 0, 2)
    per_head = per_head.reshape(3, heads_count)
    cx = jnp.concatenate(
        [wide[:5], jnp.repeat(per_head[2], HEAD)[None], jnp.zeros((2, inner), f32)], axis=0
    )
    cb = jnp.pad(conv_bc.astype(f32), ((0, 3), (0, 0)))
    heads = jnp.pad(
        jnp.stack([per_head[1], jnp.exp(per_head[0])]), ((0, 6), (0, Q - heads_count))
    )
    pick = (jnp.arange(inner)[:, None] // HEAD == jnp.arange(Q)[None, :]).astype(b16)

    w_s = jnp.concatenate([full_bc, full_dt[:, :128] + full_dt[:, 128:]], axis=1)
    x, cotangent, normed, normed_t, cot_t = ready
    xin = nn(normed, w_x).astype(b16)
    bd = nn(normed, w_s)
    blocks = tokens.shape[0] // Q
    started = list(scan_forward(xin, bd, cx, cb, heads, 0, blocks * 3 // 4, None))
    if quick:
        started[4], *mine_second = lax.optimization_barrier((started[4], *mine_second))
        other_second = [swap(part, 1, "tensor") for part in mine_second]
    ssd, held, pre, rates, ended = scan_forward(
        xin, bd, cx, cb, heads, blocks * 3 // 4, blocks - blocks * 3 // 4, started
    )
    if quick:
        other_second = lax.optimization_barrier((ended, *other_second))[1:]
        w_z, w_out_t = merge(where, mine_second, other_second, second_layout)
    mixed, dz, dssd, grad_norm = gate_both(ssd, normed, cotangent, w_z, w_out_t, gain_norm)
    scan = lambda base, count, before: list(
        scan_backward(dssd, xin, pre, bd, held, rates, cx, cb, heads, pick, base, count, before)
    )
    if quick:
        keep_out, send_out = pack_whole(where, cot_t, mixed)
        dz, keep_out, send_out = lax.optimization_barrier((dz, keep_out, send_out))
        parts_out = sum_tensor(keep_out, send_out)
        keep, send, sums = pack_whole(where, normed_t, dz, w_z)
        dssd, keep, send, parts_out = lax.optimization_barrier((dssd, keep, send, parts_out))
        parts = sum_tensor(keep, send)
        carry = scan(blocks * 3 // 4, blocks // 4, None)
        carry[2], parts, parts_out = lax.optimization_barrier((carry[2], parts, parts_out))
        early = sum_around(jnp.concatenate([parts, parts_out], axis=2), shard_rows)
        carry = scan(0, blocks * 3 // 4, carry)
        carry[0], carry[1], early = lax.optimization_barrier((carry[0], carry[1], early))
    else:
        early = scatter_plain(
            [nn(normed_t, dz).astype(b16), nn(cot_t, mixed).astype(b16)],
            ((0, 0, half, False), (1, 0, half, False)),
        )
        carry = scan(0, blocks, None)
    dxin, dbd, _, _, _, gx, gb, gh = carry
    if quick:
        keep, send, sums = pack_first(where, normed_t, dxin, dbd, w_x, w_s, sums)
        sums, keep, send = lax.optimization_barrier((sums, keep, send))
        parts_first = sum_tensor(keep, send)
        keep, send = pack_second(where, normed_t, dxin, w_x, sums, gx, gb, gh, grad_norm, gain_row)
        dxin, dz, mixed, keep, send, parts_first = lax.optimization_barrier(
            (dxin, dz, mixed, keep, send, parts_first)
        )
        parts_second = sum_tensor(keep, send)
        parts_first = sum_around(parts_first, shard_rows)
        early = early.reshape(2, 2, *early.shape[1:])
        early, near = early[:, 0], swap(early[:, 1], 4)
    grad_tokens = token_grads(dz, dxin, dbd, x, cotangent, w_z, w_x, w_s, gain_row)
    if quick:
        grad_tokens, mixed, parts_first, parts_second, early, near = lax.optimization_barrier(
            (grad_tokens, mixed, parts_first, parts_second, early, near)
        )
        second = sum_around(parts_second, shard_rows)
        early = plus(early, near)
        early = [early[0], swap(early[1], 8)]
        parts_first = parts_first.reshape(2, 2, *parts_first.shape[1:])
        first = plus(parts_first[:, 0], swap(parts_first[:, 1], 4))
        mixed, second, first = lax.optimization_barrier((mixed, second, first))
        first = [first[0], swap(first[1], 8)]
        second = along_z_parts(second)
    out = add_branch(mixed, x, w_out_t)
    if quick:
        z_out, bc_out, dt_out, cx_out, cb_out, alog, bias, skip, norm, pre_sum, w_out_grad = finish(
            where, early, first, second, pick[:half], model, half
        )
        return (
            out, grad_tokens, pre_sum, z_out, bc_out, dt_out.T,
            cx_out, cb_out, alog[0], bias[0], skip[0], norm, w_out_grad.T,
        )
    late = scatter_plain(
        [nn(normed_t, dxin).astype(b16), nn(normed_t, dbd).astype(b16)],
        ((0, 0, half, False), (1, 0, 2 * STATE + 128, True)),
    )
    dnormed = nt(dz, w_z) + nt(dxin, w_x) + nt(dbd, w_s)
    wide_x = x.astype(f32)
    scale = lax.rsqrt(jnp.mean(wide_x * wide_x, axis=1, keepdims=True) + epsilon)
    grad_pre = jnp.sum(dnormed * wide_x * scale, axis=0)
    lines = jnp.sum(gx.reshape(6, 8, inner), axis=1)
    lines, norm, convbc, rates, grad_pre = lax.psum(
        (lines, jnp.sum(grad_norm, axis=0), jnp.sum(gb.reshape(5, 8, 2 * STATE), axis=1), gh[:2], grad_pre), ("dp", "tensor")
    )

    def mine(vector, width):
        return lax.dynamic_slice_in_dim(vector, side * width, width, vector.ndim - 1)

    skip = jnp.sum(lines[5].reshape(heads_count, HEAD), axis=1)
    return (
        out,
        grad_tokens,
        grad_pre,
        jnp.stack([early[:, :half], late[:, :half]], axis=1),
        late[:, half : half + 2 * STATE],
        mine(late[:, half + 2 * STATE :], half_heads),
        mine(lines[:5], half),
        convbc,
        mine(rates[0], half_heads),
        mine(rates[1], half_heads),
        mine(skip, half_heads),
        mine(norm, half),
        early[:, half:].T,
    )


def solution(mesh):
    placed = (
        P(("dp", "tensor"), None),
        P(),
        P("dp", None, "tensor"),
        P("dp", None),
        P("dp", "tensor"),
        P(None, "tensor"),
        P(),
        P("tensor"),
        P("tensor"),
        P("tensor"),
        P("tensor"),
        P("tensor", "dp"),
        P(("dp", "tensor"), None),
    )
    return jax.shard_map(
        body,
        mesh=mesh,
        in_specs=placed,
        out_specs=(
            P(("dp", "tensor"), None),
            P(("dp", "tensor"), None),
            P(),
            P("dp", None, "tensor"),
            P("dp", None),
            P("dp", "tensor"),
            P(None, "tensor"),
            P(),
            P("tensor"),
            P("tensor"),
            P("tensor"),
            P("tensor"),
            P("tensor", "dp"),
        ),
        check_vma=False,
    )
```

```python
import functools

import jax
import jax.numpy as jnp
from jax import lax
from jax.experimental import pallas as pl
from jax.experimental.pallas import tpu as pltpu
from jax.sharding import PartitionSpec as P

LEN = 1024
LOG2E = 1.4426950408889634
Q = 128
HEAD = 64
STATE = 128
epsilon = 1e-05
f32 = jnp.float32
b16 = jnp.bfloat16
exact = lax.Precision.HIGHEST
MIB = 1024 * 1024


def nn(a, b, precision=None):
    return lax.dot_general(
        a, b, (((1,), (0,)), ((), ())), preferred_element_type=f32, precision=precision
    )


def nt(a, b, precision=None):
    return lax.dot_general(
        a, b, (((1,), (1,)), ((), ())), preferred_element_type=f32, precision=precision
    )


def tn(a, b):
    return lax.dot_general(a, b, (((0,), (0,)), ((), ())), preferred_element_type=f32)


def sigmoid(v):
    return 0.5 * jnp.tanh(0.5 * v) + 0.5


def softplus(v):
    return jnp.maximum(v, 0.0) + jnp.log1p(jnp.exp(-jnp.abs(v)))


def iota(axis):
    return lax.broadcasted_iota(jnp.int32, (Q, Q), axis)


def token(row):
    return ((row & 7) << 4) | (row >> 3)


def sublane(width):
    return lax.broadcasted_iota(jnp.int32, (24, width), 0) & 7


def with_past(here, past):
    mixed = jnp.where(
        sublane(here.shape[1]) == 0, pltpu.roll(past, 17, 0), pltpu.roll(here[Q - 24 :], 1, 0)
    )
    return jnp.concatenate([mixed, here], axis=0)


def with_future(here, future):
    mixed = jnp.where(
        sublane(here.shape[1]) == 7, pltpu.roll(future, 7, 0), pltpu.roll(here[:24], 23, 0)
    )
    return jnp.concatenate([here, mixed], axis=0)


def conv(padded, taps, lanes):
    total = taps[4:5, lanes]
    for k in range(4):
        total = total + taps[k : k + 1, lanes] * padded[8 * k : 8 * k + Q]
    return total


def fold(value):
    return jnp.sum(value.reshape(Q // 8, 8, value.shape[1]), axis=0)


def split_low(value, count):
    pieces = []
    for _ in range(count):
        piece = value.astype(b16)
        pieces.append(piece)
        value = value - piece.astype(f32)
    return jnp.concatenate(pieces, axis=1)


def head_rates(dt_raw, heads_ref, low_tri):
    step = softplus(dt_raw + heads_ref[0:1, :])
    decay = -step * heads_ref[1:2, :]
    sums = nn(low_tri, split_low(decay, 3))
    cum = (sums[:, :Q] + sums[:, Q : 2 * Q] + sums[:, 2 * Q :]) * LOG2E
    return step, decay, cum


def scan_forward_kernel(
    per_seq, pairs, base, resumed, *refs
):
    xin_ref, xhalo_ref, bd_ref, bdhalo_ref, cx_ref, cb_ref, heads_ref = refs[:7]
    y_ref, state_out_ref, pre_ref, rates_ref, state = refs[-5:]
    first = ((base + pl.program_id(0)) % per_seq) == 0

    if resumed:

        @pl.when(pl.program_id(0) == 0)
        def _():
            state[...] = refs[7][...]

    @pl.when(first)
    def _():
        state[...] = jnp.zeros_like(state)

    keep = jnp.where(first, 0.0, 1.0)
    rows, cols = token(iota(0)), token(iota(1))
    lower = rows >= cols
    low_tri = jnp.where(lower, 1.0, 0.0).astype(b16)
    left = iota(1) < HEAD
    bs = with_past(bd_ref[:, : 2 * STATE], bdhalo_ref[8:32, : 2 * STATE] * keep)
    pre_bc = conv(bs, cb_ref, slice(0, 2 * STATE))
    bc = pre_bc * sigmoid(pre_bc)
    b_low, c_low = bc[:, :STATE].astype(b16), bc[:, STATE:].astype(b16)
    gram = jnp.where(lower, nt(c_low, b_low), 0.0)
    step, decay, cum = head_rates(bd_ref[:, 2 * STATE :], heads_ref, low_tri)
    cum_rows = cum.T
    rates_ref[:, :Q] = step
    rates_ref[:, Q:] = cum
    b_turned = bc[:, :STATE].T.astype(b16)
    leaving = []
    for p in range(pairs):
        sl = slice(p * Q, (p + 1) * Q)
        if p % 2 == 0:
            two = slice(p * Q, (p + 2) * Q)
            entering = state[:, two]
            held = entering.astype(b16)
            state_out_ref[0, :, two] = held
            carried = nn(c_low, held)
            rises = []
        past = xhalo_ref[:, sl].astype(f32)[8:32] * keep
        pre = conv(with_past(xin_ref[:, sl].astype(f32), past), cx_ref, sl)
        pre_ref[:, sl] = pre.astype(b16)
        x = pre * sigmoid(pre)
        step2 = jnp.where(left, step[:, 2 * p : 2 * p + 1], step[:, 2 * p + 1 : 2 * p + 2])
        scaled = x * step2
        c0 = jnp.broadcast_to(cum[:, 2 * p : 2 * p + 1], (Q, Q))
        c1 = jnp.broadcast_to(cum[:, 2 * p + 1 : 2 * p + 2], (Q, Q))
        w0 = jnp.exp2(jnp.minimum(c0 - cum_rows[2 * p : 2 * p + 1, :], 0.0)) * gram
        w1 = jnp.exp2(jnp.minimum(c1 - cum_rows[2 * p + 1 : 2 * p + 2, :], 0.0)) * gram
        weights = jnp.concatenate([w0.astype(b16), w1.astype(b16)], axis=1)
        split = jnp.concatenate(
            [jnp.where(left, scaled, 0.0).astype(b16), jnp.where(left, 0.0, scaled).astype(b16)], axis=0
        )
        both = jnp.where(left, c0, c1)
        rise = jnp.exp2(both)
        here = carried[:, (p % 2) * Q : (p % 2 + 1) * Q]
        y = nn(weights, split) + here * rise + cx_ref[5:6, sl] * x
        y_ref[:, sl] = y.astype(b16)
        leaving.append((scaled * jnp.exp2(both[Q - 1 : Q, :] - both)).astype(b16))
        rises.append(rise[Q - 1 : Q, :])
        if p % 2 == 1:
            added = nn(b_turned, jnp.concatenate(leaving[-2:], axis=1))
            state[:, two] = entering * jnp.concatenate(rises, axis=1) + added


def scan_forward(xin, bd, cx, cb, heads, base, count, before):
    rows, inner = xin.shape
    blocks, per_seq, pairs = rows // Q, LEN // Q, inner // Q
    wide = bd.shape[1]
    kept = [] if before is None else [before[4], *before[:4]]
    return pl.pallas_call(
        functools.partial(scan_forward_kernel, per_seq, pairs, base, before is not None),
        grid=(count,),
        in_specs=[
            pl.BlockSpec((Q, inner), lambda k: (base + k, 0)),
            pl.BlockSpec((32, inner), lambda k: (jnp.maximum((base + k) * (Q // 32) - 1, 0), 0)),
            pl.BlockSpec((Q, wide), lambda k: (base + k, 0)),
            pl.BlockSpec((32, wide), lambda k: (jnp.maximum((base + k) * (Q // 32) - 1, 0), 0)),
            pl.BlockSpec(cx.shape, lambda k: (0, 0)),
            pl.BlockSpec(cb.shape, lambda k: (0, 0)),
            pl.BlockSpec(heads.shape, lambda k: (0, 0)),
        ]
        + ([pl.BlockSpec((STATE, inner), lambda k: (0, 0))] + [pl.BlockSpec(memory_space=pl.ANY)] * 4 if kept else []),
        out_specs=[
            pl.BlockSpec((Q, inner), lambda k: (base + k, 0)),
            pl.BlockSpec((1, STATE, inner), lambda k: (base + k, 0, 0)),
            pl.BlockSpec((Q, inner), lambda k: (base + k, 0)),
            pl.BlockSpec((Q, 2 * Q), lambda k: (base + k, 0)),
            pl.BlockSpec((STATE, inner), lambda k: (0, 0)),
        ],
        out_shape=[
            jax.ShapeDtypeStruct((rows, inner), b16),
            jax.ShapeDtypeStruct((blocks, STATE, inner), b16),
            jax.ShapeDtypeStruct((rows, inner), b16),
            jax.ShapeDtypeStruct((rows, 2 * Q), f32),
            jax.ShapeDtypeStruct((STATE, inner), f32),
        ],
        input_output_aliases={8: 0, 9: 1, 10: 2, 11: 3} if kept else {},
        compiler_params=pltpu.CompilerParams(vmem_limit_bytes=56 * MIB),
        cost_estimate=pl.CostEstimate(flops=count * Q * inner * 6000, bytes_accessed=count * Q * inner * 8, transcendentals=count * Q * inner * 8),
        name="scan_forward",
    )(xin, xin, bd, bd, cx, cb, heads, *kept)


def scan_backward_kernel(
    per_seq, pairs, base, count, resumed, *refs
):
    (dy_ref, xin_ref, pre_ref, bd_ref, bdhalo_ref, held_ref, rates_ref, cx_ref, cb_ref, heads_ref, pick_ref) = refs[:11]
    (
        dxin_ref, dbd_ref, adjoint, xnext, bnext, gx_ref, gb_ref, gh_ref,
        xt, dye, lam_low, products, row_sums,
    ) = refs[-13:]
    step_id = pl.program_id(0)
    block = base + count - 1 - step_id
    first = (block % per_seq) == 0
    last = (block % per_seq) == per_seq - 1

    @pl.when(step_id == 0)
    def _():
        row_sums[...] = jnp.zeros_like(row_sums)
        for here, ref in enumerate((adjoint, xnext, bnext, gx_ref, gb_ref, gh_ref)):
            ref[...] = refs[11 + here][...] if resumed else jnp.zeros_like(ref)

    @pl.when(last)
    def _():
        adjoint[...] = jnp.zeros_like(adjoint)
        xnext[...] = jnp.zeros_like(xnext)
        bnext[...] = jnp.zeros_like(bnext)

    keep = jnp.where(first, 0.0, 1.0)
    rows, cols = token(iota(0)), token(iota(1))
    upper = cols >= rows
    left = iota(1) < HEAD
    left_low = jnp.where(left, 1.0, 0.0).astype(b16)
    right_low = jnp.where(left, 0.0, 1.0).astype(b16)
    ones_low = jnp.ones((8, Q), b16)
    lane_of = lax.broadcasted_iota(jnp.int32, (2 * Q, Q), 1)
    half_of = lax.broadcasted_iota(jnp.int32, (2 * Q, Q), 0) // Q
    bs = with_past(bd_ref[:, : 2 * STATE], bdhalo_ref[8:32, : 2 * STATE] * keep)
    pre_bc = conv(bs, cb_ref, slice(0, 2 * STATE))
    sig_bc = sigmoid(pre_bc)
    bc = pre_bc * sig_bc
    b_low, c_low = bc[:, :STATE].astype(b16), bc[:, STATE:].astype(b16)
    gram = jnp.where(upper, nt(b_low, c_low), 0.0)
    gram_low = gram.astype(b16)
    raw = bd_ref[:, 2 * STATE :]
    step, cum = rates_ref[:, :Q], rates_ref[:, Q:]
    cum_rows = cum.T
    c_turned = bc[:, STATE:].T.astype(b16)
    inner_states = []
    dgram = jnp.zeros((Q, Q), f32)
    col_sums = jnp.zeros((Q, Q), f32)
    for p in range(pairs):
        sl = slice(p * Q, (p + 1) * Q)
        if p % 2 == 0:
            two = slice(p * Q, (p + 2) * Q)
            held = held_ref[0, :, two]
            lam = adjoint[:, two]
            lam_here = lam.astype(b16)
            lam_low[:, two] = lam_here
            inner_states.append(jnp.sum(lam * held.astype(f32), axis=0, keepdims=True))
            carried_two = nn(c_low, held)
            back_two = nn(b_low, lam_here)
            rises = []
        half_lanes = slice((p % 2) * Q, (p % 2 + 1) * Q)
        pre = pre_ref[:, sl].astype(f32)
        sig = sigmoid(pre)
        x = pre * sig
        step2 = jnp.where(left, step[:, 2 * p : 2 * p + 1], step[:, 2 * p + 1 : 2 * p + 2])
        scaled = x * step2
        dy_low = dy_ref[:, sl]
        dy = dy_low.astype(f32)
        split = jnp.concatenate([dy_low * left_low, dy_low * right_low], axis=0)
        dweights = nt(scaled.astype(b16), split)
        c0 = jnp.broadcast_to(cum[:, 2 * p : 2 * p + 1], (Q, Q))
        c1 = jnp.broadcast_to(cum[:, 2 * p + 1 : 2 * p + 2], (Q, Q))
        weights, crossing = [], []
        for half, column in ((0, c0), (1, c1)):
            head = 2 * p + half
            fade = jnp.exp2(jnp.minimum(cum_rows[head : head + 1, :] - column, 0.0))
            weights.append(fade.astype(b16) * gram_low)
            faded = dweights[:, half * Q : (half + 1) * Q] * fade
            dgram = dgram + faded
            crossing.append((faded * gram).astype(b16))
        crossing = jnp.concatenate(crossing, axis=1)
        over_rows = nn(ones_low, crossing)
        row_sums[2 * p : 2 * p + 1, :] = over_rows[0:1, :Q]
        row_sums[2 * p + 1 : 2 * p + 2, :] = over_rows[0:1, Q:]
        col_sums = col_sums + nn(crossing, jnp.where(lane_of == 2 * p + half_of, 1.0, 0.0).astype(b16))
        both = jnp.where(left, c0, c1)
        tail = jnp.exp2(both[Q - 1 : Q, :] - both)
        rise = jnp.exp2(both)
        dx_state = back_two[:, half_lanes] * tail
        dscaled = nn(jnp.concatenate(weights, axis=1), split) + dx_state
        dye_here = dy * rise
        products[0:Q, sl] = (dye_here * carried_two[:, half_lanes]).astype(b16)
        products[Q : 2 * Q, sl] = (scaled * dx_state).astype(b16)
        products[2 * Q :, sl] = (dscaled * x).astype(b16)
        xt[:, sl] = (scaled * tail).astype(b16)
        dye[:, sl] = dye_here.astype(b16)
        rises.append(rise[Q - 1 : Q, :])
        if p % 2 == 1:
            adjoint[:, two] = lam * jnp.concatenate(rises, axis=1) + nn(c_turned, dye[:, two])
        dx = dscaled * step2 + cx_ref[5:6, sl] * dy
        dpre = dx * (sig + x * (1.0 - sig))
        padded = with_future(dpre, xnext[:, sl])
        xnext[:, sl] = dpre[:24]
        dxin = jnp.zeros((Q, Q), f32)
        xin = xin_ref[:, sl].astype(f32)
        for k in range(4):
            ahead = padded[24 - 8 * k : 24 - 8 * k + Q]
            dxin = dxin + cx_ref[k : k + 1, sl] * ahead
            gx_ref[8 * k : 8 * k + 8, sl] += fold(ahead * xin)
        dxin_ref[:, sl] = dxin.astype(b16)
        gx_ref[32:40, sl] += fold(dpre)
        gx_ref[40:48, sl] += fold(dy * x)
    dgram_low = jnp.where(upper, dgram, 0.0)
    db = nn(dgram_low.astype(b16), c_low) + nt(xt[...], lam_low[...])
    dc = nn(dgram_low.T.astype(b16), b_low) + nt(dye[...], held_ref[0])
    total = cum[Q - 1 : Q, :]
    inner_states = jnp.concatenate(inner_states, axis=1)
    pick = pick_ref[...]
    summed = nn(products[...], pick)
    high = inner_states.astype(b16)
    low = (inner_states - high.astype(f32)).astype(b16)
    both_states = jnp.concatenate([jnp.broadcast_to(high, (8, high.shape[1])), jnp.broadcast_to(low, (8, low.shape[1]))], axis=0)
    state_sums = nn(both_states, pick)
    constant = jnp.exp2(total) * (state_sums[0:1, :] + state_sums[8:9, :])
    up_tri = jnp.where(upper, 1.0, 0.0).astype(b16)
    strict = jnp.where(rows > cols, 1.0, 0.0).astype(b16)
    moved = jnp.concatenate([summed[:Q] - col_sums + row_sums[...].T, summed[Q : 2 * Q]], axis=0)
    crossed = nn(jnp.concatenate([up_tri, strict], axis=1), split_low(moved, 3))
    ddecay = crossed[:, :Q] + crossed[:, Q : 2 * Q] + crossed[:, 2 * Q :] + constant
    summed3 = summed[2 * Q :]
    dstep = summed3 - ddecay * heads_ref[1:2, :]
    draw = dstep * sigmoid(raw + heads_ref[0:1, :])
    gh_ref[0:1, :] += jnp.sum(ddecay * step, axis=0, keepdims=True) * -heads_ref[1:2, :]
    gh_ref[1:2, :] += jnp.sum(draw, axis=0, keepdims=True)
    dbc = jnp.concatenate([db, dc], axis=1)
    dpre_bc = dbc * sig_bc * (1.0 + pre_bc * (1.0 - sig_bc))
    padded = with_future(dpre_bc, bnext[...])
    bnext[...] = dpre_bc[:24]
    dbc_in = jnp.zeros((Q, 2 * STATE), f32)
    for k in range(4):
        ahead = padded[24 - 8 * k : 24 - 8 * k + Q]
        dbc_in = dbc_in + cb_ref[k : k + 1, :] * ahead
        gb_ref[8 * k : 8 * k + 8, :] += fold(ahead * bd_ref[:, : 2 * STATE])
    gb_ref[32:40, :] += fold(dpre_bc)
    dbd_ref[:, : 2 * STATE] = dbc_in.astype(b16)
    dbd_ref[:, 2 * STATE :] = draw.astype(b16)


def scan_backward(dy, xin, pre, bd, held, rates, cx, cb, heads, pick, base, count, before):
    rows, inner = xin.shape
    blocks, per_seq, pairs = rows // Q, LEN // Q, inner // Q
    wide = bd.shape[1]
    back = lambda k: base + count - 1 - k
    fixed = lambda shape: pl.BlockSpec(shape, lambda k: (0, 0))
    carry = [(STATE, inner), (24, inner), (24, 2 * STATE), (48, inner), (40, 2 * STATE), (8, Q)]
    kept = [] if before is None else [*before[2:], before[0], before[1]]
    return pl.pallas_call(
        functools.partial(scan_backward_kernel, per_seq, pairs, base, count, before is not None),
        grid=(count,),
        in_specs=[
            pl.BlockSpec((Q, inner), lambda k: (back(k), 0)),
            pl.BlockSpec((Q, inner), lambda k: (back(k), 0)),
            pl.BlockSpec((Q, inner), lambda k: (back(k), 0)),
            pl.BlockSpec((Q, wide), lambda k: (back(k), 0)),
            pl.BlockSpec((32, wide), lambda k: (jnp.maximum(back(k) * (Q // 32) - 1, 0), 0)),
            pl.BlockSpec((1, STATE, inner), lambda k: (back(k), 0, 0)),
            pl.BlockSpec((Q, 2 * Q), lambda k: (back(k), 0)),
            fixed(cx.shape),
            fixed(cb.shape),
            fixed(heads.shape),
            fixed(pick.shape),
        ]
        + ([fixed(shape) for shape in carry] + [pl.BlockSpec(memory_space=pl.ANY)] * 2 if kept else []),
        out_specs=[
            pl.BlockSpec((Q, inner), lambda k: (back(k), 0)),
            pl.BlockSpec((Q, wide), lambda k: (back(k), 0)),
        ]
        + [fixed(shape) for shape in carry],
        out_shape=[
            jax.ShapeDtypeStruct((rows, inner), b16),
            jax.ShapeDtypeStruct((rows, wide), b16),
        ]
        + [jax.ShapeDtypeStruct(shape, f32) for shape in carry],
        input_output_aliases={17: 0, 18: 1} if kept else {},
        scratch_shapes=[
            pltpu.VMEM((Q, inner), b16),
            pltpu.VMEM((Q, inner), b16),
            pltpu.VMEM((STATE, inner), b16),
            pltpu.VMEM((3 * Q, inner), b16),
            pltpu.VMEM((Q, Q), f32),
        ],
        compiler_params=pltpu.CompilerParams(vmem_limit_bytes=56 * MIB),
        cost_estimate=pl.CostEstimate(flops=count * Q * inner * 12000, bytes_accessed=count * Q * inner * 10, transcendentals=count * Q * inner * 8),
        name="scan_backward",
    )(dy, xin, pre, bd, bd, held, rates, cx, cb, heads, pick, *kept)


def gate_kernel(y, normed, cot, w_z, w_out_t, gain, mixed, dz, dssd, grad_norm, zs, hats, dhats):
    @pl.when(pl.program_id(0) == 0)
    def _():
        grad_norm[...] = jnp.zeros_like(grad_norm)

    rows, inner = y.shape
    chunks = [slice(begin, begin + 256) for begin in range(0, inner, 256)]
    squares = jnp.zeros((rows, 128), f32)
    for sl in chunks:
        z = nn(normed[...], w_z[:, sl])
        zs[:, sl] = z
        gated = y[:, sl].astype(f32) * (z * sigmoid(z))
        hats[:, sl] = gated
        square = gated * gated
        squares = squares + square[:, :128] + square[:, 128:]
    inv = lax.rsqrt(jnp.sum(squares, axis=1, keepdims=True) / inner + epsilon)
    crosses = jnp.zeros((rows, 128), f32)
    for sl in chunks:
        hat = hats[:, sl] * inv
        hats[:, sl] = hat
        mixed[:, sl] = (hat * gain[:, sl]).astype(b16)
        dmixed = nn(cot[...], w_out_t[:, sl])
        dhat = dmixed * gain[:, sl]
        dhats[:, sl] = dhat
        product = dmixed * hat
        grad_norm[:, sl] += jnp.sum(product.reshape(rows // 8, 8, 256), axis=0)
        product = dhat * hat
        crosses = crosses + product[:, :128] + product[:, 128:]
    cross = jnp.sum(crosses, axis=1, keepdims=True) / inner
    for sl in chunks:
        dgated = inv * (dhats[:, sl] - hats[:, sl] * cross)
        z = zs[:, sl]
        sig = sigmoid(z)
        gate = z * sig
        dz[:, sl] = (dgated * y[:, sl].astype(f32) * (sig + gate * (1.0 - sig))).astype(b16)
        dssd[:, sl] = (dgated * gate).astype(b16)


def gate_both(y, normed, cot, w_z, w_out_t, gain):
    rows, inner = y.shape
    model = normed.shape[1]
    size = 256
    tall = lambda width: pl.BlockSpec((size, width), lambda k: (k, 0))
    fixed = lambda shape: pl.BlockSpec(shape, lambda k: (0, 0))
    return pl.pallas_call(
        gate_kernel,
        grid=(rows // size,),
        in_specs=[tall(inner), tall(model), tall(model), fixed(w_z.shape), fixed(w_out_t.shape), fixed(gain.shape)],
        out_specs=[tall(inner)] * 3 + [fixed((8, inner))],
        out_shape=[jax.ShapeDtypeStruct((rows, inner), b16)] * 3 + [jax.ShapeDtypeStruct((8, inner), f32)],
        scratch_shapes=[pltpu.VMEM((size, inner), f32)] * 3,
        compiler_params=pltpu.CompilerParams(vmem_limit_bytes=44 * MIB),
        cost_estimate=pl.CostEstimate(flops=rows * inner * 8000, bytes_accessed=rows * inner * 10, transcendentals=rows * inner * 2),
        name="gate_both",
    )(y, normed, cot, w_z, w_out_t, gain)


def swap(value, bit, axis="dp"):
    count = lax.axis_size(axis)
    return lax.ppermute(value, axis, [(i, i ^ bit) for i in range(count)])


def tie(value, *others):
    return lax.optimization_barrier((value, *others))[0]


def fast(rows):
    return lax.axis_size("dp") == 16 and rows % 16 == 0


def along_z(shard):
    return jnp.stack([shard] + [swap(shard, z << 2) for z in (1, 2, 3)])


def around(column):
    return [column] + [swap(column, q) for q in (1, 2, 3)]


def merge_kernel(rows, layout, where_ref, *refs):
    mine, other, outs = refs[:4], refs[4:8], refs[8:]
    me, side = where_ref[0], where_ref[1]
    for q in range(4):
        for z in range(4):
            start = pl.multiple_of((me ^ (4 * z + q)) * rows, 16)
            for piece, half in ((mine[q], side), (other[q], 1 - side)):
                for out, (begin, width) in zip(outs, layout):
                    lane = pl.multiple_of(half * width, 128)
                    out[pl.ds(start, rows), pl.ds(lane, width)] = piece[z, :, begin : begin + width]


def merge(where, mine, other, layout):
    rows = mine[0].shape[1]
    whole = pl.BlockSpec(memory_space=pltpu.VMEM)
    return pl.pallas_call(
        functools.partial(merge_kernel, rows, layout),
        in_specs=[pl.BlockSpec(memory_space=pltpu.SMEM)] + [whole] * 8,
        out_specs=[whole] * len(layout),
        out_shape=[jax.ShapeDtypeStruct((16 * rows, 2 * width), b16) for _, width in layout],
        compiler_params=pltpu.CompilerParams(vmem_limit_bytes=16 * MIB),
        name="merge_weights",
    )(where, *mine, *other)


def gather_plain(shard, layout):
    full = lax.all_gather(shard, "dp", axis=0, tiled=True)
    return [
        lax.all_gather(full[:, begin : begin + width], "tensor", axis=1, tiled=True)
        for begin, width in layout
    ]


def put(where_ref, rows, piece, keep, send, lane, width, owner):
    me, side = where_ref[0], where_ref[1]

    def store(out):
        for q in range(4):
            for z in range(4):
                start = pl.multiple_of((me ^ (4 * z + q)) * rows, 16)
                out[q, z * rows : (z + 1) * rows, pl.ds(lane, width)] = piece[pl.ds(start, rows), :width]

    if owner is None:
        store(keep)
        store(send)
    else:
        pl.when(side == owner)(lambda: store(keep))
        pl.when(side != owner)(lambda: store(send))


def product_sums(weight, grad):
    total = jnp.zeros((weight.shape[0], 128), f32)
    for begin in range(0, weight.shape[1], 128):
        lanes = slice(begin, begin + 128)
        total = total + weight[:, lanes].astype(f32) * grad[:, lanes]
    return total


TILE = 256


def pack_whole_kernel(rows, weighted, where_ref, left, right, *refs):
    step = pl.program_id(0)
    grad = nn(left[...], right[...])
    if weighted:
        weight, keep, send, sums, piece = refs

        @pl.when(step == 0)
        def _():
            sums[...] = jnp.zeros_like(sums)

        sums[...] += product_sums(weight, grad)
    else:
        keep, send, piece = refs
    piece[...] = grad.astype(b16)
    put(where_ref, rows, piece, keep, send, 0, piece.shape[1], step)


def pack_whole(where, left, right, weight=None):
    model, tokens = left.shape
    rows = model // 16
    half = right.shape[1] // 2
    fixed = lambda shape: pl.BlockSpec(shape, lambda t: (0,) * len(shape))
    packed = (4, 4 * rows, half)
    weights = [] if weight is None else [weight]
    extra = [(model, 128)] * len(weights)
    return pl.pallas_call(
        functools.partial(pack_whole_kernel, rows, bool(weights)),
        grid=(2,),
        in_specs=[
            pl.BlockSpec(memory_space=pltpu.SMEM),
            fixed((model, tokens)),
            pl.BlockSpec((tokens, half), lambda t: (0, t)),
        ]
        + [pl.BlockSpec((model, half), lambda t: (0, t))] * len(weights),
        out_specs=[fixed(packed), fixed(packed)] + [fixed(shape) for shape in extra],
        out_shape=[jax.ShapeDtypeStruct(packed, b16)] * 2 + [jax.ShapeDtypeStruct(shape, f32) for shape in extra],
        scratch_shapes=[pltpu.VMEM((model, half), b16)],
        compiler_params=pltpu.CompilerParams(vmem_limit_bytes=30 * MIB),
        cost_estimate=pl.CostEstimate(flops=8 * model * tokens * half, bytes_accessed=8 * tokens * half, transcendentals=0),
        name="pack_whole",
    )(where, left, right, *weights)


def pack_first_kernel(rows, where_ref, normed_t, dxin, dbd, w_x, w_s, sums_in, keep, send, sums, piece):
    step = pl.program_id(0)

    @pl.when(step == 0)
    def _():
        sums[...] = sums_in[...]

    @pl.when(step < 2)
    def _():
        grad = nn(normed_t[...], dxin[...])
        sums[...] += product_sums(w_x, grad)
        piece[:, :TILE] = grad.astype(b16)
        put(where_ref, rows, piece, keep, send, 0, TILE, step)

    @pl.when(step == 2)
    def _():
        grad = nn(normed_t[...], dbd[...])
        sums[...] += product_sums(w_s, grad)
        piece[...] = grad.astype(b16)
        put(where_ref, rows, piece, keep, send, TILE, piece.shape[1], None)


def pack_first(where, normed_t, dxin, dbd, w_x, w_s, sums):
    model, tokens = normed_t.shape
    rows = model // 16
    tiles = dxin.shape[1] // TILE
    shared = dbd.shape[1]
    fixed = lambda shape: pl.BlockSpec(shape, lambda t: (0,) * len(shape))
    chosen = lambda t: (0, jnp.minimum(t, 1) * (tiles // 2))
    packed = (4, 4 * rows, TILE + shared)
    return pl.pallas_call(
        functools.partial(pack_first_kernel, rows),
        grid=(3,),
        in_specs=[
            pl.BlockSpec(memory_space=pltpu.SMEM),
            fixed((model, tokens)),
            pl.BlockSpec((tokens, TILE), chosen),
            fixed(dbd.shape),
            pl.BlockSpec((model, TILE), chosen),
            fixed(w_s.shape),
            fixed((model, 128)),
        ],
        out_specs=[fixed(packed), fixed(packed), fixed((model, 128))],
        out_shape=[jax.ShapeDtypeStruct(packed, b16)] * 2 + [jax.ShapeDtypeStruct((model, 128), f32)],
        scratch_shapes=[pltpu.VMEM((model, shared), b16)],
        compiler_params=pltpu.CompilerParams(vmem_limit_bytes=20 * MIB),
        cost_estimate=pl.CostEstimate(flops=2 * model * tokens * (2 * TILE + shared), bytes_accessed=4 * tokens * TILE, transcendentals=0),
        name="pack_first",
    )(where, normed_t, dxin, dbd, w_x, w_s, sums)


def pack_second_kernel(
    rows, each, where_ref, normed_t, dxin, w_x, sums_in, gx, gb, gh, grad_norm, gain_pre, keep, send, sums, piece, flat
):
    step = pl.program_id(0)

    @pl.when(step == 0)
    def _():
        sums[...] = sums_in[...]

    grad = nn(normed_t[...], dxin[...])
    sums[...] += product_sums(w_x, grad)
    piece[...] = grad.astype(b16)
    put(where_ref, rows, piece, keep, send, pl.multiple_of((step % each) * TILE, 128), TILE, step // each)

    @pl.when(step == 2 * each - 1)
    def _():
        model = piece.shape[0]
        width = each * TILE
        lines = gx.shape[1] // width
        flat[...] = jnp.zeros_like(flat)
        for r in range(7):
            source = gx[8 * r : 8 * r + 8, :] if r < 6 else grad_norm[...]
            line = jnp.sum(source, axis=0, keepdims=True)
            for k in range(lines):
                flat[lines * r + k : lines * r + k + 1, :] = line[:, k * width : (k + 1) * width]
        for k in range(5):
            row, lane = 7 * lines + k // 2, 2 * STATE * (k % 2)
            flat[row : row + 1, lane : lane + 2 * STATE] = jnp.sum(
                gb[8 * k : 8 * k + 8, :], axis=0, keepdims=True
            )
        row = 7 * lines + 2
        flat[row : row + 1, 256:384] = gh[0:1, :]
        flat[row : row + 1, 384:512] = gh[1:2, :]
        total = sums[...]
        high = total.astype(b16)
        low = (total - high.astype(f32)).astype(b16)
        ones = jnp.ones((8, 128), b16)
        over = (nt(ones, high) + nt(ones, low))[0:1, :] / gain_pre[...]
        flat[row + 1 : row + 2, :] = over[:, :width]
        flat[row + 2 : row + 3, : model - width] = over[:, width:]
        flat_low = flat[...].astype(b16)
        for q in range(4):
            keep[q, 4 * rows :, :] = flat_low
            send[q, 4 * rows :, :] = flat_low


def pack_second(where, normed_t, dxin, w_x, sums, gx, gb, gh, grad_norm, gain_pre):
    model, tokens = normed_t.shape
    rows = model // 16
    half = dxin.shape[1] // TILE // 2
    each = half - 1
    fixed = lambda shape: pl.BlockSpec(shape, lambda t: (0,) * len(shape))
    chosen = lambda t: (0, (t // each) * half + 1 + t % each)
    packed = (4, 4 * rows + 32, each * TILE)
    return pl.pallas_call(
        functools.partial(pack_second_kernel, rows, each),
        grid=(2 * each,),
        in_specs=[
            pl.BlockSpec(memory_space=pltpu.SMEM),
            fixed((model, tokens)),
            pl.BlockSpec((tokens, TILE), chosen),
            pl.BlockSpec((model, TILE), chosen),
            fixed((model, 128)),
            fixed(gx.shape),
            fixed(gb.shape),
            fixed(gh.shape),
            fixed(grad_norm.shape),
            fixed(gain_pre.shape),
        ],
        out_specs=[fixed(packed), fixed(packed)],
        out_shape=[jax.ShapeDtypeStruct(packed, b16)] * 2,
        scratch_shapes=[
            pltpu.VMEM((model, 128), f32),
            pltpu.VMEM((model, TILE), b16),
            pltpu.VMEM((32, each * TILE), f32),
        ],
        compiler_params=pltpu.CompilerParams(vmem_limit_bytes=20 * MIB),
        cost_estimate=pl.CostEstimate(flops=4 * model * tokens * each * TILE, bytes_accessed=4 * tokens * each * TILE, transcendentals=0),
        name="pack_second",
    )(where, normed_t, dxin, w_x, sums, gx, gb, gh, grad_norm, gain_pre)


def finish_kernel(half, side_ref, *refs):
    early, first, second, pick = refs[:2], refs[2:4], refs[4:8], refs[8]
    (z_out, bc_out, dt_out, cx_out, cb_out, alog_out, bias_out, skip_out, norm_out, pre_out, w_out, lines) = refs[9:]
    side = side_ref[1]
    rows = first[0].shape[0]

    def total(parts):
        value = parts[0][...].astype(f32)
        for k in range(1, len(parts)):
            value = value + parts[k][...].astype(f32)
        return value

    one, two, three = total(early), total(first), total(second)
    width = three.shape[1]
    z_out[:, 0, :] = one[:, :half]
    z_out[:, 1, :TILE] = two[:, :TILE]
    z_out[:, 1, TILE:] = three[:rows]
    w_out[...] = one[:, half:]
    bc_out[...] = two[:, TILE : TILE + 2 * STATE]
    heads = half // HEAD

    def own(value):
        return jnp.where(side == 0, value[:, :heads], value[:, heads : 2 * heads])

    dt_out[...] = own(two[:, TILE + 2 * STATE :]).T
    flat = three[rows:]
    count = 2 * half // width
    for r in range(7):
        for k in range(count):
            lines[r : r + 1, k * width : (k + 1) * width] = flat[count * r + k : count * r + k + 1, :]
    mine = lines[:, pl.ds(pl.multiple_of(side * half, 128), half)]
    cx_out[...] = mine[:5]
    high = mine[5:6].astype(b16)
    low = (mine[5:6] - high.astype(f32)).astype(b16)
    pair = jnp.concatenate([jnp.broadcast_to(high, (8, half)), jnp.broadcast_to(low, (8, half))], axis=0)
    sums = nn(pair, pick[...])
    skip_out[...] = (sums[0:1] + sums[8:9])[:, :heads]
    norm_out[...] = mine[6]
    row = 7 * count
    for k in range(5):
        lane = 2 * STATE * (k % 2)
        cb_out[k : k + 1, :] = flat[row + k // 2 : row + k // 2 + 1, lane : lane + 2 * STATE]
    alog_out[...] = own(flat[row + 2 : row + 3, 256:384])
    bias_out[...] = own(flat[row + 2 : row + 3, 384:512])
    model = pre_out.shape[0]
    pre_out[...] = jnp.concatenate([flat[row + 3], flat[row + 4, : model - width]])


def finish(where, early, first, second, pick, model, half):
    rows = first[0].shape[0]
    heads = half // HEAD
    whole = pl.BlockSpec(memory_space=pltpu.VMEM)
    shapes = [
        (rows, 2, half), (rows, 2 * STATE), (heads, rows), (5, half), (5, 2 * STATE),
        (1, heads), (1, heads), (1, heads), (half,), (model,), (rows, half),
    ]
    return pl.pallas_call(
        functools.partial(finish_kernel, half),
        in_specs=[pl.BlockSpec(memory_space=pltpu.SMEM)] + [whole] * 9,
        out_specs=[whole] * len(shapes),
        out_shape=[jax.ShapeDtypeStruct(shape, f32) for shape in shapes],
        scratch_shapes=[pltpu.VMEM((8, 2 * half), f32)],
        compiler_params=pltpu.CompilerParams(vmem_limit_bytes=16 * MIB),
        name="finish",
    )(where, *early, *first, *second, pick)


def sum_tensor(keep, send):
    got = swap(send, 1, "tensor")
    return (keep.astype(f32) + got.astype(f32)).astype(b16)


def sum_around(parts, rows):
    total = parts[0].astype(f32)
    for value in [swap(parts[q], q) for q in (1, 2, 3)]:
        total = total + value.astype(f32)
    split = total[: 4 * rows].reshape(4, rows, total.shape[1])
    if total.shape[0] > 4 * rows:
        shared = jnp.broadcast_to(total[None, 4 * rows :], (4, *total[4 * rows :].shape))
        split = jnp.concatenate([split, shared], axis=1)
    return split.astype(b16)


def plus(a, b):
    return (a.astype(f32) + b.astype(f32)).astype(b16)


def along_z_parts(parts):
    return [parts[0]] + [swap(parts[z], z << 2) for z in (1, 2, 3)]


def scatter_plain(arrays, parts):
    halves = []
    for which, base, width, shared in parts:
        array = arrays[which][:, base : base + (width if shared else 2 * width)]
        if shared:
            array = lax.psum(array, "tensor")
        else:
            array = lax.psum_scatter(array, "tensor", scatter_dimension=1, tiled=True)
        halves.append(array)
    return lax.psum_scatter(
        jnp.concatenate(halves, axis=1).astype(f32), "dp", scatter_dimension=0, tiled=True
    )


def prepare_kernel(tokens, cot, gain, x_out, cot_out, normed_out, normed_t, cot_t):
    order = jnp.where(iota(1) == token(iota(0)), 1.0, 0.0).astype(b16)
    x = nn(order, tokens[...])
    x_out[...] = x.astype(b16)
    moved = nn(order, cot[...])
    cot_out[...] = moved.astype(b16)
    cot_t[...] = moved.T.astype(b16)
    normed = x * lax.rsqrt(jnp.mean(x * x, axis=1, keepdims=True) + epsilon) * gain[...]
    normed_out[...] = normed.astype(b16)
    normed_t[...] = normed.T.astype(b16)


def prepare(tokens, cot, gain):
    rows, model = tokens.shape
    tall = pl.BlockSpec((Q, model), lambda k: (k, 0))
    flat = pl.BlockSpec((model, Q), lambda k: (0, k))
    return pl.pallas_call(
        prepare_kernel,
        grid=(rows // Q,),
        in_specs=[tall, tall, pl.BlockSpec((1, model), lambda k: (0, 0))],
        out_specs=[tall, tall, tall, flat, flat],
        out_shape=[jax.ShapeDtypeStruct((rows, model), b16)] * 3 + [jax.ShapeDtypeStruct((model, rows), b16)] * 2,
        compiler_params=pltpu.CompilerParams(vmem_limit_bytes=56 * MIB),
        name="prepare",
    )(tokens, cot, gain)


def restore(value, out):
    order = jnp.where(iota(0) == token(iota(1)), 1.0, 0.0).astype(b16)
    value = value.astype(b16)
    for begin in range(0, value.shape[0], Q):
        out[begin : begin + Q, :] = nn(order, value[begin : begin + Q]).astype(b16)


def token_grads_kernel(dz, dxin, dbd, x, cot, w_z, w_x, w_s, gain, out):
    dn = nt(dz[...], w_z[...]) + nt(dxin[...], w_x[...]) + nt(dbd[...], w_s[...])
    dn = dn * gain[...]
    value = x[...].astype(f32)
    scale = lax.rsqrt(jnp.mean(value * value, axis=1, keepdims=True) + epsilon)
    inner = jnp.mean(dn * value, axis=1, keepdims=True)
    grad = cot[...].astype(f32) + scale * dn - value * (scale * scale * scale * inner)
    restore(grad, out)


def token_grads(dz, dxin, dbd, x, cot, w_z, w_x, w_s, gain):
    rows, model = x.shape
    tall = lambda value: pl.BlockSpec((256, value.shape[1]), lambda k: (k, 0))
    fixed = lambda value: pl.BlockSpec(value.shape, lambda k: (0, 0))
    return pl.pallas_call(
        token_grads_kernel,
        grid=(rows // 256,),
        in_specs=[tall(v) for v in (dz, dxin, dbd, x, cot)] + [fixed(v) for v in (w_z, w_x, w_s, gain)],
        out_specs=tall(x),
        out_shape=jax.ShapeDtypeStruct(x.shape, b16),
        compiler_params=pltpu.CompilerParams(vmem_limit_bytes=32 * MIB),
        cost_estimate=pl.CostEstimate(flops=rows * model * 8000, bytes_accessed=rows * model * 20, transcendentals=0),
        name="token_grads",
    )(dz, dxin, dbd, x, cot, w_z, w_x, w_s, gain)


def add_branch_kernel(mixed, x, w_out_t, out):
    restore(x[...].astype(f32) + nt(mixed[...], w_out_t[...]), out)


def add_branch(mixed, x, w_out_t):
    rows, model = x.shape
    tall = lambda value: pl.BlockSpec((256, value.shape[1]), lambda k: (k, 0))
    return pl.pallas_call(
        add_branch_kernel,
        grid=(rows // 256,),
        in_specs=[tall(mixed), tall(x), pl.BlockSpec(w_out_t.shape, lambda k: (0, 0))],
        out_specs=tall(x),
        out_shape=jax.ShapeDtypeStruct(x.shape, b16),
        compiler_params=pltpu.CompilerParams(vmem_limit_bytes=24 * MIB),
        cost_estimate=pl.CostEstimate(flops=rows * model * 4000, bytes_accessed=rows * model * 10, transcendentals=0),
        name="add_branch",
    )(mixed, x, w_out_t)


def both_sides(value, side, axis):
    other = swap(value, 1, "tensor")
    return jnp.where(
        side == 0, jnp.concatenate([value, other], axis), jnp.concatenate([other, value], axis)
    )


def body(
    tokens, pre_gain, w_zx, w_bc, w_dt, conv_x, conv_bc, a_log, dt_bias, skip_gain, norm_gain, w_out, cotangent,
):
    side = lax.axis_index("tensor")
    where = jnp.stack([lax.axis_index("dp"), side]).astype(jnp.int32)
    model, half = tokens.shape[1], conv_x.shape[1]
    inner = 2 * half
    half_heads = a_log.shape[0]
    heads_count = 2 * half_heads
    shard_rows = w_zx.shape[0]

    dt_pad = lax.dynamic_update_slice(
        jnp.zeros((shard_rows, 128), b16), w_dt, (0, side * half_heads)
    )
    bc_half = lax.dynamic_slice(w_bc, (0, side * STATE), (shard_rows, STATE))
    quick = fast(shard_rows)
    first = jnp.concatenate([w_zx[:, 1], bc_half, dt_pad], axis=1)
    second = jnp.concatenate([w_zx[:, 0], w_out.T], axis=1)
    first_layout = ((0, half), (half, STATE), (half + STATE, 128))
    second_layout = ((0, half), (half, half))
    gain_row = pre_gain.astype(f32)[None]
    pick = (jnp.arange(inner)[:, None] // HEAD == jnp.arange(Q)[None, :]).astype(b16)
    if quick:
        column = along_z(first)
        tokens, cotangent, _ = lax.optimization_barrier((tokens, cotangent, column))
    ready = prepare(tokens, cotangent, gain_row)
    if quick:
        mine_first = around(column)
        later = along_z(tie(second, column))
        mine_first[3], pick, *ready = lax.optimization_barrier((mine_first[3], pick, *ready))
        other_first = [swap(part, 1, "tensor") for part in mine_first]
        mine_second = around(tie(later, *mine_first))
        w_x, full_bc, full_dt = merge(where, mine_first, other_first, first_layout)
    else:
        w_x, full_bc, full_dt = gather_plain(first, first_layout)
        w_z, w_out_t = gather_plain(second, second_layout)
    small = jnp.concatenate(
        [
            conv_x.astype(f32),
            norm_gain.astype(f32)[None],
            jnp.pad(jnp.concatenate([a_log, dt_bias, skip_gain]), (0, half - 3 * half_heads))[None],
            jnp.zeros((1, half), f32),
        ],
        axis=0,
    )
    small = both_sides(small[None], side, 0)
    wide = jnp.concatenate([small[0, :6], small[1, :6]], axis=1)
    gain_norm = wide[5:6]
    per_head = small[:, 6, : 3 * half_heads].reshape(2, 3, half_heads).transpose(1, 0, 2)
    per_head = per_head.reshape(3, heads_count)
    cx = jnp.concatenate(
        [wide[:5], jnp.repeat(per_head[2], HEAD)[None], jnp.zeros((2, inner), f32)], axis=0
    )
    cb = jnp.pad(conv_bc.astype(f32), ((0, 3), (0, 0)))
    heads = jnp.pad(
        jnp.stack([per_head[1], jnp.exp(per_head[0])]), ((0, 6), (0, Q - heads_count))
    )

    w_s = jnp.concatenate([full_bc, full_dt[:, :128] + full_dt[:, 128:]], axis=1)
    x, cotangent, normed, normed_t, cot_t = ready
    xin = nn(normed, w_x).astype(b16)
    bd = nn(normed, w_s)
    blocks = tokens.shape[0] // Q
    started = list(scan_forward(xin, bd, cx, cb, heads, 0, blocks * 3 // 4, None))
    if quick:
        started[4], *mine_second = lax.optimization_barrier((started[4], *mine_second))
        other_second = [swap(part, 1, "tensor") for part in mine_second]
    ssd, held, pre, rates, ended = scan_forward(
        xin, bd, cx, cb, heads, blocks * 3 // 4, blocks - blocks * 3 // 4, started
    )
    if quick:
        other_second = lax.optimization_barrier((ended, *other_second))[1:]
        w_z, w_out_t = merge(where, mine_second, other_second, second_layout)
    mixed, dz, dssd, grad_norm = gate_both(ssd, normed, cotangent, w_z, w_out_t, gain_norm)
    scan = lambda base, count, before: list(
        scan_backward(dssd, xin, pre, bd, held, rates, cx, cb, heads, pick, base, count, before)
    )
    if quick:
        keep_out, send_out = pack_whole(where, cot_t, mixed)
        dz, keep_out, send_out = lax.optimization_barrier((dz, keep_out, send_out))
        parts_out = sum_tensor(keep_out, send_out)
        keep, send, sums = pack_whole(where, normed_t, dz, w_z)
        dssd, keep, send, parts_out = lax.optimization_barrier((dssd, keep, send, parts_out))
        parts = sum_tensor(keep, send)
        carry = scan(blocks * 3 // 4, blocks // 4, None)
        carry[2], parts, parts_out = lax.optimization_barrier((carry[2], parts, parts_out))
        early = sum_around(jnp.concatenate([parts, parts_out], axis=2), shard_rows)
        carry = scan(0, blocks * 3 // 4, carry)
        carry[0], carry[1], early = lax.optimization_barrier((carry[0], carry[1], early))
    else:
        early = scatter_plain(
            [nn(normed_t, dz).astype(b16), nn(cot_t, mixed).astype(b16)],
            ((0, 0, half, False), (1, 0, half, False)),
        )
        carry = scan(0, blocks, None)
    dxin, dbd, _, _, _, gx, gb, gh = carry
    if quick:
        keep, send, sums = pack_first(where, normed_t, dxin, dbd, w_x, w_s, sums)
        sums, keep, send = lax.optimization_barrier((sums, keep, send))
        parts_first = sum_tensor(keep, send)
        keep, send = pack_second(where, normed_t, dxin, w_x, sums, gx, gb, gh, grad_norm, gain_row)
        dxin, dz, mixed, keep, send, parts_first = lax.optimization_barrier(
            (dxin, dz, mixed, keep, send, parts_first)
        )
        parts_second = sum_tensor(keep, send)
        parts_first = sum_around(parts_first, shard_rows)
        early = early.reshape(2, 2, *early.shape[1:])
        early, near = early[:, 0], swap(early[:, 1], 4)
    grad_tokens = token_grads(dz, dxin, dbd, x, cotangent, w_z, w_x, w_s, gain_row)
    if quick:
        grad_tokens, mixed, parts_first, parts_second, early, near = lax.optimization_barrier(
            (grad_tokens, mixed, parts_first, parts_second, early, near)
        )
        second = sum_around(parts_second, shard_rows)
        early = plus(early, near)
        early = [early[0], swap(early[1], 8)]
        parts_first = parts_first.reshape(2, 2, *parts_first.shape[1:])
        first = plus(parts_first[:, 0], swap(parts_first[:, 1], 4))
        mixed, second, first = lax.optimization_barrier((mixed, second, first))
        first = [first[0], swap(first[1], 8)]
        second = along_z_parts(second)
    out = add_branch(mixed, x, w_out_t)
    if quick:
        z_out, bc_out, dt_out, cx_out, cb_out, alog, bias, skip, norm, pre_sum, w_out_grad = finish(
            where, early, first, second, pick[:half], model, half
        )
        return (
            out, grad_tokens, pre_sum, z_out, bc_out, dt_out.T,
            cx_out, cb_out, alog[0], bias[0], skip[0], norm, w_out_grad.T,
        )
    late = scatter_plain(
        [nn(normed_t, dxin).astype(b16), nn(normed_t, dbd).astype(b16)],
        ((0, 0, half, False), (1, 0, 2 * STATE + 128, True)),
    )
    dnormed = nt(dz, w_z) + nt(dxin, w_x) + nt(dbd, w_s)
    wide_x = x.astype(f32)
    scale = lax.rsqrt(jnp.mean(wide_x * wide_x, axis=1, keepdims=True) + epsilon)
    grad_pre = jnp.sum(dnormed * wide_x * scale, axis=0)
    lines = jnp.sum(gx.reshape(6, 8, inner), axis=1)
    lines, norm, convbc, rates, grad_pre = lax.psum(
        (lines, jnp.sum(grad_norm, axis=0), jnp.sum(gb.reshape(5, 8, 2 * STATE), axis=1), gh[:2], grad_pre), ("dp", "tensor")
    )

    def mine(vector, width):
        return lax.dynamic_slice_in_dim(vector, side * width, width, vector.ndim - 1)

    skip = jnp.sum(lines[5].reshape(heads_count, HEAD), axis=1)
    return (
        out,
        grad_tokens,
        grad_pre,
        jnp.stack([early[:, :half], late[:, :half]], axis=1),
        late[:, half : half + 2 * STATE],
        mine(late[:, half + 2 * STATE :], half_heads),
        mine(lines[:5], half),
        convbc,
        mine(rates[0], half_heads),
        mine(rates[1], half_heads),
        mine(skip, half_heads),
        mine(norm, half),
        early[:, half:].T,
    )


def solution(mesh):
    placed = (
        P(("dp", "tensor"), None),
        P(),
        P("dp", None, "tensor"),
        P("dp", None),
        P("dp", "tensor"),
        P(None, "tensor"),
        P(),
        P("tensor"),
        P("tensor"),
        P("tensor"),
        P("tensor"),
        P("tensor", "dp"),
        P(("dp", "tensor"), None),
    )
    return jax.shard_map(
        body,
        mesh=mesh,
        in_specs=placed,
        out_specs=(
            P(("dp", "tensor"), None),
            P(("dp", "tensor"), None),
            P(),
            P("dp", None, "tensor"),
            P("dp", None),
            P("dp", "tensor"),
            P(None, "tensor"),
            P(),
            P("tensor"),
            P("tensor"),
            P("tensor"),
            P("tensor"),
            P("tensor", "dp"),
        ),
        check_vma=False,
    )
```

```python
import functools

import jax
import jax.numpy as jnp
from jax import lax
from jax.experimental import pallas as pl
from jax.experimental.pallas import tpu as pltpu
from jax.sharding import PartitionSpec as P

LEN = 1024
LOG2E = 1.4426950408889634
Q = 128
HEAD = 64
STATE = 128
epsilon = 1e-05
f32 = jnp.float32
b16 = jnp.bfloat16
exact = lax.Precision.HIGHEST
MIB = 1024 * 1024


def nn(a, b, precision=None):
    return lax.dot_general(
        a, b, (((1,), (0,)), ((), ())), preferred_element_type=f32, precision=precision
    )


def nt(a, b, precision=None):
    return lax.dot_general(
        a, b, (((1,), (1,)), ((), ())), preferred_element_type=f32, precision=precision
    )


def tn(a, b):
    return lax.dot_general(a, b, (((0,), (0,)), ((), ())), preferred_element_type=f32)


def sigmoid(v):
    return 0.5 * jnp.tanh(0.5 * v) + 0.5


def softplus(v):
    return jnp.maximum(v, 0.0) + jnp.log1p(jnp.exp(-jnp.abs(v)))


def iota(axis):
    return lax.broadcasted_iota(jnp.int32, (Q, Q), axis)


def token(row):
    return ((row & 7) << 4) | (row >> 3)


def sublane(width):
    return lax.broadcasted_iota(jnp.int32, (24, width), 0) & 7


def with_past(here, past):
    mixed = jnp.where(
        sublane(here.shape[1]) == 0, pltpu.roll(past, 17, 0), pltpu.roll(here[Q - 24 :], 1, 0)
    )
    return jnp.concatenate([mixed, here], axis=0)


def with_future(here, future):
    mixed = jnp.where(
        sublane(here.shape[1]) == 7, pltpu.roll(future, 7, 0), pltpu.roll(here[:24], 23, 0)
    )
    return jnp.concatenate([here, mixed], axis=0)


def conv(padded, taps, lanes):
    total = taps[4:5, lanes]
    for k in range(4):
        total = total + taps[k : k + 1, lanes] * padded[8 * k : 8 * k + Q]
    return total


def fold(value):
    return jnp.sum(value.reshape(Q // 8, 8, value.shape[1]), axis=0)


def split_low(value, count):
    pieces = []
    for _ in range(count):
        piece = value.astype(b16)
        pieces.append(piece)
        value = value - piece.astype(f32)
    return jnp.concatenate(pieces, axis=1)


def head_rates(dt_raw, heads_ref, low_tri):
    step = softplus(dt_raw + heads_ref[0:1, :])
    decay = -step * heads_ref[1:2, :]
    sums = nn(low_tri, split_low(decay, 3))
    cum = (sums[:, :Q] + sums[:, Q : 2 * Q] + sums[:, 2 * Q :]) * LOG2E
    return step, decay, cum


def scan_forward_kernel(
    per_seq, pairs, base, resumed, *refs
):
    xin_ref, xhalo_ref, bd_ref, bdhalo_ref, cx_ref, cb_ref, heads_ref = refs[:7]
    y_ref, state_out_ref, pre_ref, rates_ref, state = refs[-5:]
    first = ((base + pl.program_id(0)) % per_seq) == 0

    if resumed:

        @pl.when(pl.program_id(0) == 0)
        def _():
            state[...] = refs[7][...]

    @pl.when(first)
    def _():
        state[...] = jnp.zeros_like(state)

    keep = jnp.where(first, 0.0, 1.0)
    rows, cols = token(iota(0)), token(iota(1))
    lower = rows >= cols
    low_tri = jnp.where(lower, 1.0, 0.0).astype(b16)
    left = iota(1) < HEAD
    bs = with_past(bd_ref[:, : 2 * STATE], bdhalo_ref[8:32, : 2 * STATE] * keep)
    pre_bc = conv(bs, cb_ref, slice(0, 2 * STATE))
    bc = pre_bc * sigmoid(pre_bc)
    b_low, c_low = bc[:, :STATE].astype(b16), bc[:, STATE:].astype(b16)
    gram = jnp.where(lower, nt(c_low, b_low), 0.0)
    step, decay, cum = head_rates(bd_ref[:, 2 * STATE :], heads_ref, low_tri)
    cum_rows = cum.T
    rates_ref[:, :Q] = step
    rates_ref[:, Q:] = cum
    b_turned = bc[:, :STATE].T.astype(b16)
    leaving = []
    for p in range(pairs):
        sl = slice(p * Q, (p + 1) * Q)
        if p % 2 == 0:
            two = slice(p * Q, (p + 2) * Q)
            entering = state[:, two]
            held = entering.astype(b16)
            state_out_ref[0, :, two] = held
            carried = nn(c_low, held)
            rises = []
        past = xhalo_ref[:, sl].astype(f32)[8:32] * keep
        pre = conv(with_past(xin_ref[:, sl].astype(f32), past), cx_ref, sl)
        pre_ref[:, sl] = pre.astype(b16)
        x = pre * sigmoid(pre)
        step2 = jnp.where(left, step[:, 2 * p : 2 * p + 1], step[:, 2 * p + 1 : 2 * p + 2])
        scaled = x * step2
        c0 = jnp.broadcast_to(cum[:, 2 * p : 2 * p + 1], (Q, Q))
        c1 = jnp.broadcast_to(cum[:, 2 * p + 1 : 2 * p + 2], (Q, Q))
        w0 = jnp.exp2(jnp.minimum(c0 - cum_rows[2 * p : 2 * p + 1, :], 0.0)) * gram
        w1 = jnp.exp2(jnp.minimum(c1 - cum_rows[2 * p + 1 : 2 * p + 2, :], 0.0)) * gram
        weights = jnp.concatenate([w0.astype(b16), w1.astype(b16)], axis=1)
        split = jnp.concatenate(
            [jnp.where(left, scaled, 0.0).astype(b16), jnp.where(left, 0.0, scaled).astype(b16)], axis=0
        )
        both = jnp.where(left, c0, c1)
        rise = jnp.exp2(both)
        here = carried[:, (p % 2) * Q : (p % 2 + 1) * Q]
        y = nn(weights, split) + here * rise + cx_ref[5:6, sl] * x
        y_ref[:, sl] = y.astype(b16)
        leaving.append((scaled * jnp.exp2(both[Q - 1 : Q, :] - both)).astype(b16))
        rises.append(rise[Q - 1 : Q, :])
        if p % 2 == 1:
            added = nn(b_turned, jnp.concatenate(leaving[-2:], axis=1))
            state[:, two] = entering * jnp.concatenate(rises, axis=1) + added


def scan_forward(xin, bd, cx, cb, heads, base, count, before):
    rows, inner = xin.shape
    blocks, per_seq, pairs = rows // Q, LEN // Q, inner // Q
    wide = bd.shape[1]
    kept = [] if before is None else [before[4], *before[:4]]
    return pl.pallas_call(
        functools.partial(scan_forward_kernel, per_seq, pairs, base, before is not None),
        grid=(count,),
        in_specs=[
            pl.BlockSpec((Q, inner), lambda k: (base + k, 0)),
            pl.BlockSpec((32, inner), lambda k: (jnp.maximum((base + k) * (Q // 32) - 1, 0), 0)),
            pl.BlockSpec((Q, wide), lambda k: (base + k, 0)),
            pl.BlockSpec((32, wide), lambda k: (jnp.maximum((base + k) * (Q // 32) - 1, 0), 0)),
            pl.BlockSpec(cx.shape, lambda k: (0, 0)),
            pl.BlockSpec(cb.shape, lambda k: (0, 0)),
            pl.BlockSpec(heads.shape, lambda k: (0, 0)),
        ]
        + ([pl.BlockSpec((STATE, inner), lambda k: (0, 0))] + [pl.BlockSpec(memory_space=pl.ANY)] * 4 if kept else []),
        out_specs=[
            pl.BlockSpec((Q, inner), lambda k: (base + k, 0)),
            pl.BlockSpec((1, STATE, inner), lambda k: (base + k, 0, 0)),
            pl.BlockSpec((Q, inner), lambda k: (base + k, 0)),
            pl.BlockSpec((Q, 2 * Q), lambda k: (base + k, 0)),
            pl.BlockSpec((STATE, inner), lambda k: (0, 0)),
        ],
        out_shape=[
            jax.ShapeDtypeStruct((rows, inner), b16),
            jax.ShapeDtypeStruct((blocks, STATE, inner), b16),
            jax.ShapeDtypeStruct((rows, inner), b16),
            jax.ShapeDtypeStruct((rows, 2 * Q), f32),
            jax.ShapeDtypeStruct((STATE, inner), f32),
        ],
        input_output_aliases={8: 0, 9: 1, 10: 2, 11: 3} if kept else {},
        compiler_params=pltpu.CompilerParams(vmem_limit_bytes=56 * MIB),
        cost_estimate=pl.CostEstimate(flops=count * Q * inner * 6000, bytes_accessed=count * Q * inner * 8, transcendentals=count * Q * inner * 8),
        name="scan_forward",
    )(xin, xin, bd, bd, cx, cb, heads, *kept)


def scan_backward_kernel(
    per_seq, pairs, base, count, resumed, *refs
):
    (dy_ref, xin_ref, pre_ref, bd_ref, bdhalo_ref, held_ref, rates_ref, cx_ref, cb_ref, heads_ref, pick_ref) = refs[:11]
    (
        dxin_ref, dbd_ref, adjoint, xnext, bnext, gx_ref, gb_ref, gh_ref,
        xt, dye, lam_low, products, row_sums,
    ) = refs[-13:]
    step_id = pl.program_id(0)
    block = base + count - 1 - step_id
    first = (block % per_seq) == 0
    last = (block % per_seq) == per_seq - 1

    @pl.when(step_id == 0)
    def _():
        row_sums[...] = jnp.zeros_like(row_sums)
        for here, ref in enumerate((adjoint, xnext, bnext, gx_ref, gb_ref, gh_ref)):
            ref[...] = refs[11 + here][...] if resumed else jnp.zeros_like(ref)

    @pl.when(last)
    def _():
        adjoint[...] = jnp.zeros_like(adjoint)
        xnext[...] = jnp.zeros_like(xnext)
        bnext[...] = jnp.zeros_like(bnext)

    keep = jnp.where(first, 0.0, 1.0)
    rows, cols = token(iota(0)), token(iota(1))
    upper = cols >= rows
    left = iota(1) < HEAD
    left_low = jnp.where(left, 1.0, 0.0).astype(b16)
    right_low = jnp.where(left, 0.0, 1.0).astype(b16)
    ones_low = jnp.ones((8, Q), b16)
    lane_of = lax.broadcasted_iota(jnp.int32, (2 * Q, Q), 1)
    half_of = lax.broadcasted_iota(jnp.int32, (2 * Q, Q), 0) // Q
    bs = with_past(bd_ref[:, : 2 * STATE], bdhalo_ref[8:32, : 2 * STATE] * keep)
    pre_bc = conv(bs, cb_ref, slice(0, 2 * STATE))
    sig_bc = sigmoid(pre_bc)
    bc = pre_bc * sig_bc
    b_low, c_low = bc[:, :STATE].astype(b16), bc[:, STATE:].astype(b16)
    gram = jnp.where(upper, nt(b_low, c_low), 0.0)
    gram_low = gram.astype(b16)
    raw = bd_ref[:, 2 * STATE :]
    step, cum = rates_ref[:, :Q], rates_ref[:, Q:]
    cum_rows = cum.T
    c_turned = bc[:, STATE:].T.astype(b16)
    inner_states = []
    dgram = jnp.zeros((Q, Q), f32)
    col_sums = jnp.zeros((Q, Q), f32)
    for p in range(pairs):
        sl = slice(p * Q, (p + 1) * Q)
        if p % 2 == 0:
            two = slice(p * Q, (p + 2) * Q)
            held = held_ref[0, :, two]
            lam = adjoint[:, two]
            lam_here = lam.astype(b16)
            lam_low[:, two] = lam_here
            inner_states.append(jnp.sum(lam * held.astype(f32), axis=0, keepdims=True))
            carried_two = nn(c_low, held)
            back_two = nn(b_low, lam_here)
            rises = []
        half_lanes = slice((p % 2) * Q, (p % 2 + 1) * Q)
        pre = pre_ref[:, sl].astype(f32)
        sig = sigmoid(pre)
        x = pre * sig
        step2 = jnp.where(left, step[:, 2 * p : 2 * p + 1], step[:, 2 * p + 1 : 2 * p + 2])
        scaled = x * step2
        dy_low = dy_ref[:, sl]
        dy = dy_low.astype(f32)
        split = jnp.concatenate([dy_low * left_low, dy_low * right_low], axis=0)
        dweights = nt(scaled.astype(b16), split)
        c0 = jnp.broadcast_to(cum[:, 2 * p : 2 * p + 1], (Q, Q))
        c1 = jnp.broadcast_to(cum[:, 2 * p + 1 : 2 * p + 2], (Q, Q))
        weights, crossing = [], []
        for half, column in ((0, c0), (1, c1)):
            head = 2 * p + half
            fade = jnp.exp2(jnp.minimum(cum_rows[head : head + 1, :] - column, 0.0))
            weights.append(fade.astype(b16) * gram_low)
            faded = dweights[:, half * Q : (half + 1) * Q] * fade
            dgram = dgram + faded
            crossing.append((faded * gram).astype(b16))
        crossing = jnp.concatenate(crossing, axis=1)
        over_rows = nn(ones_low, crossing)
        row_sums[2 * p : 2 * p + 1, :] = over_rows[0:1, :Q]
        row_sums[2 * p + 1 : 2 * p + 2, :] = over_rows[0:1, Q:]
        col_sums = col_sums + nn(crossing, jnp.where(lane_of == 2 * p + half_of, 1.0, 0.0).astype(b16))
        both = jnp.where(left, c0, c1)
        tail = jnp.exp2(both[Q - 1 : Q, :] - both)
        rise = jnp.exp2(both)
        dx_state = back_two[:, half_lanes] * tail
        dscaled = nn(jnp.concatenate(weights, axis=1), split) + dx_state
        dye_here = dy * rise
        products[0:Q, sl] = (dye_here * carried_two[:, half_lanes]).astype(b16)
        products[Q : 2 * Q, sl] = (scaled * dx_state).astype(b16)
        products[2 * Q :, sl] = (dscaled * x).astype(b16)
        xt[:, sl] = (scaled * tail).astype(b16)
        dye[:, sl] = dye_here.astype(b16)
        rises.append(rise[Q - 1 : Q, :])
        if p % 2 == 1:
            adjoint[:, two] = lam * jnp.concatenate(rises, axis=1) + nn(c_turned, dye[:, two])
        dx = dscaled * step2 + cx_ref[5:6, sl] * dy
        dpre = dx * (sig + x * (1.0 - sig))
        padded = with_future(dpre, xnext[:, sl])
        xnext[:, sl] = dpre[:24]
        dxin = jnp.zeros((Q, Q), f32)
        xin = xin_ref[:, sl].astype(f32)
        for k in range(4):
            ahead = padded[24 - 8 * k : 24 - 8 * k + Q]
            dxin = dxin + cx_ref[k : k + 1, sl] * ahead
            gx_ref[8 * k : 8 * k + 8, sl] += fold(ahead * xin)
        dxin_ref[:, sl] = dxin.astype(b16)
        gx_ref[32:40, sl] += fold(dpre)
        gx_ref[40:48, sl] += fold(dy * x)
    dgram_low = jnp.where(upper, dgram, 0.0)
    db = nn(dgram_low.astype(b16), c_low) + nt(xt[...], lam_low[...])
    dc = nn(dgram_low.T.astype(b16), b_low) + nt(dye[...], held_ref[0])
    total = cum[Q - 1 : Q, :]
    inner_states = jnp.concatenate(inner_states, axis=1)
    pick = pick_ref[...]
    summed = nn(products[...], pick)
    high = inner_states.astype(b16)
    low = (inner_states - high.astype(f32)).astype(b16)
    both_states = jnp.concatenate([jnp.broadcast_to(high, (8, high.shape[1])), jnp.broadcast_to(low, (8, low.shape[1]))], axis=0)
    state_sums = nn(both_states, pick)
    constant = jnp.exp2(total) * (state_sums[0:1, :] + state_sums[8:9, :])
    up_tri = jnp.where(upper, 1.0, 0.0).astype(b16)
    strict = jnp.where(rows > cols, 1.0, 0.0).astype(b16)
    moved = jnp.concatenate([summed[:Q] - col_sums + row_sums[...].T, summed[Q : 2 * Q]], axis=0)
    crossed = nn(jnp.concatenate([up_tri, strict], axis=1), split_low(moved, 3))
    ddecay = crossed[:, :Q] + crossed[:, Q : 2 * Q] + crossed[:, 2 * Q :] + constant
    summed3 = summed[2 * Q :]
    dstep = summed3 - ddecay * heads_ref[1:2, :]
    draw = dstep * sigmoid(raw + heads_ref[0:1, :])
    gh_ref[0:1, :] += jnp.sum(ddecay * step, axis=0, keepdims=True) * -heads_ref[1:2, :]
    gh_ref[1:2, :] += jnp.sum(draw, axis=0, keepdims=True)
    dbc = jnp.concatenate([db, dc], axis=1)
    dpre_bc = dbc * sig_bc * (1.0 + pre_bc * (1.0 - sig_bc))
    padded = with_future(dpre_bc, bnext[...])
    bnext[...] = dpre_bc[:24]
    dbc_in = jnp.zeros((Q, 2 * STATE), f32)
    for k in range(4):
        ahead = padded[24 - 8 * k : 24 - 8 * k + Q]
        dbc_in = dbc_in + cb_ref[k : k + 1, :] * ahead
        gb_ref[8 * k : 8 * k + 8, :] += fold(ahead * bd_ref[:, : 2 * STATE])
    gb_ref[32:40, :] += fold(dpre_bc)
    dbd_ref[:, : 2 * STATE] = dbc_in.astype(b16)
    dbd_ref[:, 2 * STATE :] = draw.astype(b16)


def scan_backward(dy, xin, pre, bd, held, rates, cx, cb, heads, pick, base, count, before):
    rows, inner = xin.shape
    blocks, per_seq, pairs = rows // Q, LEN // Q, inner // Q
    wide = bd.shape[1]
    back = lambda k: base + count - 1 - k
    fixed = lambda shape: pl.BlockSpec(shape, lambda k: (0, 0))
    carry = [(STATE, inner), (24, inner), (24, 2 * STATE), (48, inner), (40, 2 * STATE), (8, Q)]
    kept = [] if before is None else [*before[2:], before[0], before[1]]
    return pl.pallas_call(
        functools.partial(scan_backward_kernel, per_seq, pairs, base, count, before is not None),
        grid=(count,),
        in_specs=[
            pl.BlockSpec((Q, inner), lambda k: (back(k), 0)),
            pl.BlockSpec((Q, inner), lambda k: (back(k), 0)),
            pl.BlockSpec((Q, inner), lambda k: (back(k), 0)),
            pl.BlockSpec((Q, wide), lambda k: (back(k), 0)),
            pl.BlockSpec((32, wide), lambda k: (jnp.maximum(back(k) * (Q // 32) - 1, 0), 0)),
            pl.BlockSpec((1, STATE, inner), lambda k: (back(k), 0, 0)),
            pl.BlockSpec((Q, 2 * Q), lambda k: (back(k), 0)),
            fixed(cx.shape),
            fixed(cb.shape),
            fixed(heads.shape),
            fixed(pick.shape),
        ]
        + ([fixed(shape) for shape in carry] + [pl.BlockSpec(memory_space=pl.ANY)] * 2 if kept else []),
        out_specs=[
            pl.BlockSpec((Q, inner), lambda k: (back(k), 0)),
            pl.BlockSpec((Q, wide), lambda k: (back(k), 0)),
        ]
        + [fixed(shape) for shape in carry],
        out_shape=[
            jax.ShapeDtypeStruct((rows, inner), b16),
            jax.ShapeDtypeStruct((rows, wide), b16),
        ]
        + [jax.ShapeDtypeStruct(shape, f32) for shape in carry],
        input_output_aliases={17: 0, 18: 1} if kept else {},
        scratch_shapes=[
            pltpu.VMEM((Q, inner), b16),
            pltpu.VMEM((Q, inner), b16),
            pltpu.VMEM((STATE, inner), b16),
            pltpu.VMEM((3 * Q, inner), b16),
            pltpu.VMEM((Q, Q), f32),
        ],
        compiler_params=pltpu.CompilerParams(vmem_limit_bytes=46 * MIB),
        cost_estimate=pl.CostEstimate(flops=count * Q * inner * 12000, bytes_accessed=count * Q * inner * 10, transcendentals=count * Q * inner * 8),
        name="scan_backward",
    )(dy, xin, pre, bd, bd, held, rates, cx, cb, heads, pick, *kept)


def gate_kernel(y, normed, cot, w_z, w_out_t, gain, mixed, dz, dssd, grad_norm, zs, hats, dhats):
    @pl.when(pl.program_id(0) == 0)
    def _():
        grad_norm[...] = jnp.zeros_like(grad_norm)

    rows, inner = y.shape
    chunks = [slice(begin, begin + 256) for begin in range(0, inner, 256)]
    squares = jnp.zeros((rows, 128), f32)
    for sl in chunks:
        z = nn(normed[...], w_z[:, sl])
        zs[:, sl] = z
        gated = y[:, sl].astype(f32) * (z * sigmoid(z))
        hats[:, sl] = gated
        square = gated * gated
        squares = squares + square[:, :128] + square[:, 128:]
    inv = lax.rsqrt(jnp.sum(squares, axis=1, keepdims=True) / inner + epsilon)
    crosses = jnp.zeros((rows, 128), f32)
    for sl in chunks:
        hat = hats[:, sl] * inv
        hats[:, sl] = hat
        mixed[:, sl] = (hat * gain[:, sl]).astype(b16)
        dmixed = nn(cot[...], w_out_t[:, sl])
        dhat = dmixed * gain[:, sl]
        dhats[:, sl] = dhat
        product = dmixed * hat
        grad_norm[:, sl] += jnp.sum(product.reshape(rows // 8, 8, 256), axis=0)
        product = dhat * hat
        crosses = crosses + product[:, :128] + product[:, 128:]
    cross = jnp.sum(crosses, axis=1, keepdims=True) / inner
    for sl in chunks:
        dgated = inv * (dhats[:, sl] - hats[:, sl] * cross)
        z = zs[:, sl]
        sig = sigmoid(z)
        gate = z * sig
        dz[:, sl] = (dgated * y[:, sl].astype(f32) * (sig + gate * (1.0 - sig))).astype(b16)
        dssd[:, sl] = (dgated * gate).astype(b16)


def gate_both(y, normed, cot, w_z, w_out_t, gain):
    rows, inner = y.shape
    model = normed.shape[1]
    size = 256
    tall = lambda width: pl.BlockSpec((size, width), lambda k: (k, 0))
    fixed = lambda shape: pl.BlockSpec(shape, lambda k: (0, 0))
    return pl.pallas_call(
        gate_kernel,
        grid=(rows // size,),
        in_specs=[tall(inner), tall(model), tall(model), fixed(w_z.shape), fixed(w_out_t.shape), fixed(gain.shape)],
        out_specs=[tall(inner)] * 3 + [fixed((8, inner))],
        out_shape=[jax.ShapeDtypeStruct((rows, inner), b16)] * 3 + [jax.ShapeDtypeStruct((8, inner), f32)],
        scratch_shapes=[pltpu.VMEM((size, inner), f32)] * 3,
        compiler_params=pltpu.CompilerParams(vmem_limit_bytes=44 * MIB),
        cost_estimate=pl.CostEstimate(flops=rows * inner * 8000, bytes_accessed=rows * inner * 10, transcendentals=rows * inner * 2),
        name="gate_both",
    )(y, normed, cot, w_z, w_out_t, gain)


def swap(value, bit, axis="dp"):
    count = lax.axis_size(axis)
    return lax.ppermute(value, axis, [(i, i ^ bit) for i in range(count)])


def tie(value, *others):
    return lax.optimization_barrier((value, *others))[0]


def fast(rows):
    return lax.axis_size("dp") == 16 and rows % 16 == 0


def along_z(shard):
    return jnp.stack([shard] + [swap(shard, z << 2) for z in (1, 2, 3)])


def around(column):
    return [column] + [swap(column, q) for q in (1, 2, 3)]


def merge_kernel(rows, layout, where_ref, *refs):
    mine, other, outs = refs[:4], refs[4:8], refs[8:]
    me, side = where_ref[0], where_ref[1]
    for q in range(4):
        for z in range(4):
            start = pl.multiple_of((me ^ (4 * z + q)) * rows, 16)
            for piece, half in ((mine[q], side), (other[q], 1 - side)):
                for out, (begin, width) in zip(outs, layout):
                    lane = pl.multiple_of(half * width, 128)
                    out[pl.ds(start, rows), pl.ds(lane, width)] = piece[z, :, begin : begin + width]


def merge(where, mine, other, layout):
    rows = mine[0].shape[1]
    whole = pl.BlockSpec(memory_space=pltpu.VMEM)
    return pl.pallas_call(
        functools.partial(merge_kernel, rows, layout),
        in_specs=[pl.BlockSpec(memory_space=pltpu.SMEM)] + [whole] * 8,
        out_specs=[whole] * len(layout),
        out_shape=[jax.ShapeDtypeStruct((16 * rows, 2 * width), b16) for _, width in layout],
        compiler_params=pltpu.CompilerParams(vmem_limit_bytes=16 * MIB),
        name="merge_weights",
    )(where, *mine, *other)


def gather_plain(shard, layout):
    full = lax.all_gather(shard, "dp", axis=0, tiled=True)
    return [
        lax.all_gather(full[:, begin : begin + width], "tensor", axis=1, tiled=True)
        for begin, width in layout
    ]


def put(where_ref, rows, piece, keep, send, lane, width, owner):
    me, side = where_ref[0], where_ref[1]

    def store(out):
        for q in range(4):
            for z in range(4):
                start = pl.multiple_of((me ^ (4 * z + q)) * rows, 16)
                out[q, z * rows : (z + 1) * rows, pl.ds(lane, width)] = piece[pl.ds(start, rows), :width]

    if owner is None:
        store(keep)
        store(send)
    else:
        pl.when(side == owner)(lambda: store(keep))
        pl.when(side != owner)(lambda: store(send))


def product_sums(weight, grad):
    total = jnp.zeros((weight.shape[0], 128), f32)
    for begin in range(0, weight.shape[1], 128):
        lanes = slice(begin, begin + 128)
        total = total + weight[:, lanes].astype(f32) * grad[:, lanes]
    return total


TILE = 256


def pack_whole_kernel(rows, weighted, where_ref, left, right, *refs):
    step = pl.program_id(0)
    grad = nn(left[...], right[...])
    if weighted:
        weight, keep, send, sums, piece = refs

        @pl.when(step == 0)
        def _():
            sums[...] = jnp.zeros_like(sums)

        sums[...] += product_sums(weight, grad)
    else:
        keep, send, piece = refs
    piece[...] = grad.astype(b16)
    put(where_ref, rows, piece, keep, send, 0, piece.shape[1], step)


def pack_whole(where, left, right, weight=None):
    model, tokens = left.shape
    rows = model // 16
    half = right.shape[1] // 2
    fixed = lambda shape: pl.BlockSpec(shape, lambda t: (0,) * len(shape))
    packed = (4, 4 * rows, half)
    weights = [] if weight is None else [weight]
    extra = [(model, 128)] * len(weights)
    return pl.pallas_call(
        functools.partial(pack_whole_kernel, rows, bool(weights)),
        grid=(2,),
        in_specs=[
            pl.BlockSpec(memory_space=pltpu.SMEM),
            fixed((model, tokens)),
            pl.BlockSpec((tokens, half), lambda t: (0, t)),
        ]
        + [pl.BlockSpec((model, half), lambda t: (0, t))] * len(weights),
        out_specs=[fixed(packed), fixed(packed)] + [fixed(shape) for shape in extra],
        out_shape=[jax.ShapeDtypeStruct(packed, b16)] * 2 + [jax.ShapeDtypeStruct(shape, f32) for shape in extra],
        scratch_shapes=[pltpu.VMEM((model, half), b16)],
        compiler_params=pltpu.CompilerParams(vmem_limit_bytes=30 * MIB),
        cost_estimate=pl.CostEstimate(flops=8 * model * tokens * half, bytes_accessed=8 * tokens * half, transcendentals=0),
        name="pack_whole",
    )(where, left, right, *weights)


def pack_first_kernel(rows, where_ref, normed_t, dxin, dbd, w_x, w_s, sums_in, keep, send, sums, piece):
    step = pl.program_id(0)

    @pl.when(step == 0)
    def _():
        sums[...] = sums_in[...]

    @pl.when(step < 2)
    def _():
        grad = nn(normed_t[...], dxin[...])
        sums[...] += product_sums(w_x, grad)
        piece[:, :TILE] = grad.astype(b16)
        put(where_ref, rows, piece, keep, send, 0, TILE, step)

    @pl.when(step == 2)
    def _():
        grad = nn(normed_t[...], dbd[...])
        sums[...] += product_sums(w_s, grad)
        piece[...] = grad.astype(b16)
        put(where_ref, rows, piece, keep, send, TILE, piece.shape[1], None)


def pack_first(where, normed_t, dxin, dbd, w_x, w_s, sums):
    model, tokens = normed_t.shape
    rows = model // 16
    tiles = dxin.shape[1] // TILE
    shared = dbd.shape[1]
    fixed = lambda shape: pl.BlockSpec(shape, lambda t: (0,) * len(shape))
    chosen = lambda t: (0, jnp.minimum(t, 1) * (tiles // 2))
    packed = (4, 4 * rows, TILE + shared)
    return pl.pallas_call(
        functools.partial(pack_first_kernel, rows),
        grid=(3,),
        in_specs=[
            pl.BlockSpec(memory_space=pltpu.SMEM),
            fixed((model, tokens)),
            pl.BlockSpec((tokens, TILE), chosen),
            fixed(dbd.shape),
            pl.BlockSpec((model, TILE), chosen),
            fixed(w_s.shape),
            fixed((model, 128)),
        ],
        out_specs=[fixed(packed), fixed(packed), fixed((model, 128))],
        out_shape=[jax.ShapeDtypeStruct(packed, b16)] * 2 + [jax.ShapeDtypeStruct((model, 128), f32)],
        scratch_shapes=[pltpu.VMEM((model, shared), b16)],
        compiler_params=pltpu.CompilerParams(vmem_limit_bytes=20 * MIB),
        cost_estimate=pl.CostEstimate(flops=2 * model * tokens * (2 * TILE + shared), bytes_accessed=4 * tokens * TILE, transcendentals=0),
        name="pack_first",
    )(where, normed_t, dxin, dbd, w_x, w_s, sums)


def pack_second_kernel(
    rows, each, where_ref, normed_t, dxin, w_x, sums_in, gx, gb, gh, grad_norm, gain_pre, keep, send, sums, piece, flat
):
    step = pl.program_id(0)

    @pl.when(step == 0)
    def _():
        sums[...] = sums_in[...]

    grad = nn(normed_t[...], dxin[...])
    sums[...] += product_sums(w_x, grad)
    piece[...] = grad.astype(b16)
    put(where_ref, rows, piece, keep, send, pl.multiple_of((step % each) * TILE, 128), TILE, step // each)

    @pl.when(step == 2 * each - 1)
    def _():
        model = piece.shape[0]
        width = each * TILE
        lines = gx.shape[1] // width
        flat[...] = jnp.zeros_like(flat)
        for r in range(7):
            source = gx[8 * r : 8 * r + 8, :] if r < 6 else grad_norm[...]
            line = jnp.sum(source, axis=0, keepdims=True)
            for k in range(lines):
                flat[lines * r + k : lines * r + k + 1, :] = line[:, k * width : (k + 1) * width]
        for k in range(5):
            row, lane = 7 * lines + k // 2, 2 * STATE * (k % 2)
            flat[row : row + 1, lane : lane + 2 * STATE] = jnp.sum(
                gb[8 * k : 8 * k + 8, :], axis=0, keepdims=True
            )
        row = 7 * lines + 2
        flat[row : row + 1, 256:384] = gh[0:1, :]
        flat[row : row + 1, 384:512] = gh[1:2, :]
        total = sums[...]
        high = total.astype(b16)
        low = (total - high.astype(f32)).astype(b16)
        ones = jnp.ones((8, 128), b16)
        over = (nt(ones, high) + nt(ones, low))[0:1, :] / gain_pre[...]
        flat[row + 1 : row + 2, :] = over[:, :width]
        flat[row + 2 : row + 3, : model - width] = over[:, width:]
        flat_low = flat[...].astype(b16)
        for q in range(4):
            keep[q, 4 * rows :, :] = flat_low
            send[q, 4 * rows :, :] = flat_low


def pack_second(where, normed_t, dxin, w_x, sums, gx, gb, gh, grad_norm, gain_pre):
    model, tokens = normed_t.shape
    rows = model // 16
    half = dxin.shape[1] // TILE // 2
    each = half - 1
    fixed = lambda shape: pl.BlockSpec(shape, lambda t: (0,) * len(shape))
    chosen = lambda t: (0, (t // each) * half + 1 + t % each)
    packed = (4, 4 * rows + 32, each * TILE)
    return pl.pallas_call(
        functools.partial(pack_second_kernel, rows, each),
        grid=(2 * each,),
        in_specs=[
            pl.BlockSpec(memory_space=pltpu.SMEM),
            fixed((model, tokens)),
            pl.BlockSpec((tokens, TILE), chosen),
            pl.BlockSpec((model, TILE), chosen),
            fixed((model, 128)),
            fixed(gx.shape),
            fixed(gb.shape),
            fixed(gh.shape),
            fixed(grad_norm.shape),
            fixed(gain_pre.shape),
        ],
        out_specs=[fixed(packed), fixed(packed)],
        out_shape=[jax.ShapeDtypeStruct(packed, b16)] * 2,
        scratch_shapes=[
            pltpu.VMEM((model, 128), f32),
            pltpu.VMEM((model, TILE), b16),
            pltpu.VMEM((32, each * TILE), f32),
        ],
        compiler_params=pltpu.CompilerParams(vmem_limit_bytes=20 * MIB),
        cost_estimate=pl.CostEstimate(flops=4 * model * tokens * each * TILE, bytes_accessed=4 * tokens * each * TILE, transcendentals=0),
        name="pack_second",
    )(where, normed_t, dxin, w_x, sums, gx, gb, gh, grad_norm, gain_pre)


def finish_kernel(half, side_ref, *refs):
    early, first, second, pick = refs[:2], refs[2:4], refs[4:8], refs[8]
    (z_out, bc_out, dt_out, cx_out, cb_out, alog_out, bias_out, skip_out, norm_out, pre_out, w_out, lines) = refs[9:]
    side = side_ref[1]
    rows = first[0].shape[0]

    def total(parts):
        value = parts[0][...].astype(f32)
        for k in range(1, len(parts)):
            value = value + parts[k][...].astype(f32)
        return value

    one, two, three = total(early), total(first), total(second)
    width = three.shape[1]
    z_out[:, 0, :] = one[:, :half]
    z_out[:, 1, :TILE] = two[:, :TILE]
    z_out[:, 1, TILE:] = three[:rows]
    w_out[...] = one[:, half:]
    bc_out[...] = two[:, TILE : TILE + 2 * STATE]
    heads = half // HEAD

    def own(value):
        return jnp.where(side == 0, value[:, :heads], value[:, heads : 2 * heads])

    dt_out[...] = own(two[:, TILE + 2 * STATE :]).T
    flat = three[rows:]
    count = 2 * half // width
    for r in range(7):
        for k in range(count):
            lines[r : r + 1, k * width : (k + 1) * width] = flat[count * r + k : count * r + k + 1, :]
    mine = lines[:, pl.ds(pl.multiple_of(side * half, 128), half)]
    cx_out[...] = mine[:5]
    high = mine[5:6].astype(b16)
    low = (mine[5:6] - high.astype(f32)).astype(b16)
    pair = jnp.concatenate([jnp.broadcast_to(high, (8, half)), jnp.broadcast_to(low, (8, half))], axis=0)
    sums = nn(pair, pick[...])
    skip_out[...] = (sums[0:1] + sums[8:9])[:, :heads]
    norm_out[...] = mine[6]
    row = 7 * count
    for k in range(5):
        lane = 2 * STATE * (k % 2)
        cb_out[k : k + 1, :] = flat[row + k // 2 : row + k // 2 + 1, lane : lane + 2 * STATE]
    alog_out[...] = own(flat[row + 2 : row + 3, 256:384])
    bias_out[...] = own(flat[row + 2 : row + 3, 384:512])
    model = pre_out.shape[0]
    pre_out[...] = jnp.concatenate([flat[row + 3], flat[row + 4, : model - width]])


def finish(where, early, first, second, pick, model, half):
    rows = first[0].shape[0]
    heads = half // HEAD
    whole = pl.BlockSpec(memory_space=pltpu.VMEM)
    shapes = [
        (rows, 2, half), (rows, 2 * STATE), (heads, rows), (5, half), (5, 2 * STATE),
        (1, heads), (1, heads), (1, heads), (half,), (model,), (rows, half),
    ]
    return pl.pallas_call(
        functools.partial(finish_kernel, half),
        in_specs=[pl.BlockSpec(memory_space=pltpu.SMEM)] + [whole] * 9,
        out_specs=[whole] * len(shapes),
        out_shape=[jax.ShapeDtypeStruct(shape, f32) for shape in shapes],
        scratch_shapes=[pltpu.VMEM((8, 2 * half), f32)],
        compiler_params=pltpu.CompilerParams(vmem_limit_bytes=16 * MIB),
        name="finish",
    )(where, *early, *first, *second, pick)


def sum_tensor(keep, send):
    got = swap(send, 1, "tensor")
    return (keep.astype(f32) + got.astype(f32)).astype(b16)


def sum_around(parts, rows):
    total = parts[0].astype(f32)
    for value in [swap(parts[q], q) for q in (1, 2, 3)]:
        total = total + value.astype(f32)
    split = total[: 4 * rows].reshape(4, rows, total.shape[1])
    if total.shape[0] > 4 * rows:
        shared = jnp.broadcast_to(total[None, 4 * rows :], (4, *total[4 * rows :].shape))
        split = jnp.concatenate([split, shared], axis=1)
    return split.astype(b16)


def plus(a, b):
    return (a.astype(f32) + b.astype(f32)).astype(b16)


def along_z_parts(parts):
    return [parts[0]] + [swap(parts[z], z << 2) for z in (1, 2, 3)]


def scatter_plain(arrays, parts):
    halves = []
    for which, base, width, shared in parts:
        array = arrays[which][:, base : base + (width if shared else 2 * width)]
        if shared:
            array = lax.psum(array, "tensor")
        else:
            array = lax.psum_scatter(array, "tensor", scatter_dimension=1, tiled=True)
        halves.append(array)
    return lax.psum_scatter(
        jnp.concatenate(halves, axis=1).astype(f32), "dp", scatter_dimension=0, tiled=True
    )


def prepare_kernel(tokens, cot, gain, x_out, cot_out, normed_out, normed_t, cot_t):
    order = jnp.where(iota(1) == token(iota(0)), 1.0, 0.0).astype(b16)
    x = nn(order, tokens[...])
    x_out[...] = x.astype(b16)
    moved = nn(order, cot[...])
    cot_out[...] = moved.astype(b16)
    cot_t[...] = moved.T.astype(b16)
    normed = x * lax.rsqrt(jnp.mean(x * x, axis=1, keepdims=True) + epsilon) * gain[...]
    normed_out[...] = normed.astype(b16)
    normed_t[...] = normed.T.astype(b16)


def prepare(tokens, cot, gain):
    rows, model = tokens.shape
    tall = pl.BlockSpec((Q, model), lambda k: (k, 0))
    flat = pl.BlockSpec((model, Q), lambda k: (0, k))
    return pl.pallas_call(
        prepare_kernel,
        grid=(rows // Q,),
        in_specs=[tall, tall, pl.BlockSpec((1, model), lambda k: (0, 0))],
        out_specs=[tall, tall, tall, flat, flat],
        out_shape=[jax.ShapeDtypeStruct((rows, model), b16)] * 3 + [jax.ShapeDtypeStruct((model, rows), b16)] * 2,
        compiler_params=pltpu.CompilerParams(vmem_limit_bytes=56 * MIB),
        name="prepare",
    )(tokens, cot, gain)


def restore(value, out):
    order = jnp.where(iota(0) == token(iota(1)), 1.0, 0.0).astype(b16)
    value = value.astype(b16)
    for begin in range(0, value.shape[0], Q):
        out[begin : begin + Q, :] = nn(order, value[begin : begin + Q]).astype(b16)


def token_grads_kernel(dz, dxin, dbd, x, cot, w_z, w_x, w_s, gain, out):
    dn = nt(dz[...], w_z[...]) + nt(dxin[...], w_x[...]) + nt(dbd[...], w_s[...])
    dn = dn * gain[...]
    value = x[...].astype(f32)
    scale = lax.rsqrt(jnp.mean(value * value, axis=1, keepdims=True) + epsilon)
    inner = jnp.mean(dn * value, axis=1, keepdims=True)
    grad = cot[...].astype(f32) + scale * dn - value * (scale * scale * scale * inner)
    restore(grad, out)


def token_grads(dz, dxin, dbd, x, cot, w_z, w_x, w_s, gain):
    rows, model = x.shape
    tall = lambda value: pl.BlockSpec((256, value.shape[1]), lambda k: (k, 0))
    fixed = lambda value: pl.BlockSpec(value.shape, lambda k: (0, 0))
    return pl.pallas_call(
        token_grads_kernel,
        grid=(rows // 256,),
        in_specs=[tall(v) for v in (dz, dxin, dbd, x, cot)] + [fixed(v) for v in (w_z, w_x, w_s, gain)],
        out_specs=tall(x),
        out_shape=jax.ShapeDtypeStruct(x.shape, b16),
        compiler_params=pltpu.CompilerParams(vmem_limit_bytes=32 * MIB),
        cost_estimate=pl.CostEstimate(flops=rows * model * 8000, bytes_accessed=rows * model * 20, transcendentals=0),
        name="token_grads",
    )(dz, dxin, dbd, x, cot, w_z, w_x, w_s, gain)


def add_branch_kernel(mixed, x, w_out_t, out):
    restore(x[...].astype(f32) + nt(mixed[...], w_out_t[...]), out)


def add_branch(mixed, x, w_out_t):
    rows, model = x.shape
    tall = lambda value: pl.BlockSpec((256, value.shape[1]), lambda k: (k, 0))
    return pl.pallas_call(
        add_branch_kernel,
        grid=(rows // 256,),
        in_specs=[tall(mixed), tall(x), pl.BlockSpec(w_out_t.shape, lambda k: (0, 0))],
        out_specs=tall(x),
        out_shape=jax.ShapeDtypeStruct(x.shape, b16),
        compiler_params=pltpu.CompilerParams(vmem_limit_bytes=24 * MIB),
        cost_estimate=pl.CostEstimate(flops=rows * model * 4000, bytes_accessed=rows * model * 10, transcendentals=0),
        name="add_branch",
    )(mixed, x, w_out_t)


def both_sides(value, side, axis):
    other = swap(value, 1, "tensor")
    return jnp.where(
        side == 0, jnp.concatenate([value, other], axis), jnp.concatenate([other, value], axis)
    )


def body(
    tokens, pre_gain, w_zx, w_bc, w_dt, conv_x, conv_bc, a_log, dt_bias, skip_gain, norm_gain, w_out, cotangent,
):
    side = lax.axis_index("tensor")
    where = jnp.stack([lax.axis_index("dp"), side]).astype(jnp.int32)
    model, half = tokens.shape[1], conv_x.shape[1]
    inner = 2 * half
    half_heads = a_log.shape[0]
    heads_count = 2 * half_heads
    shard_rows = w_zx.shape[0]

    dt_pad = lax.dynamic_update_slice(
        jnp.zeros((shard_rows, 128), b16), w_dt, (0, side * half_heads)
    )
    bc_half = lax.dynamic_slice(w_bc, (0, side * STATE), (shard_rows, STATE))
    quick = fast(shard_rows)
    first = jnp.concatenate([w_zx[:, 1], bc_half, dt_pad], axis=1)
    second = jnp.concatenate([w_zx[:, 0], w_out.T], axis=1)
    first_layout = ((0, half), (half, STATE), (half + STATE, 128))
    second_layout = ((0, half), (half, half))
    gain_row = pre_gain.astype(f32)[None]
    pick = (jnp.arange(inner)[:, None] // HEAD == jnp.arange(Q)[None, :]).astype(b16)
    if quick:
        column = along_z(first)
        tokens, cotangent, _ = lax.optimization_barrier((tokens, cotangent, column))
    ready = prepare(tokens, cotangent, gain_row)
    if quick:
        mine_first = around(column)
        later = along_z(tie(second, column))
        mine_first[3], pick, *ready = lax.optimization_barrier((mine_first[3], pick, *ready))
        other_first = [swap(part, 1, "tensor") for part in mine_first]
        mine_second = around(tie(later, *mine_first))
        w_x, full_bc, full_dt = merge(where, mine_first, other_first, first_layout)
    else:
        w_x, full_bc, full_dt = gather_plain(first, first_layout)
        w_z, w_out_t = gather_plain(second, second_layout)
    small = jnp.concatenate(
        [
            conv_x.astype(f32),
            norm_gain.astype(f32)[None],
            jnp.pad(jnp.concatenate([a_log, dt_bias, skip_gain]), (0, half - 3 * half_heads))[None],
            jnp.zeros((1, half), f32),
        ],
        axis=0,
    )
    small = both_sides(small[None], side, 0)
    wide = jnp.concatenate([small[0, :6], small[1, :6]], axis=1)
    gain_norm = wide[5:6]
    per_head = small[:, 6, : 3 * half_heads].reshape(2, 3, half_heads).transpose(1, 0, 2)
    per_head = per_head.reshape(3, heads_count)
    cx = jnp.concatenate(
        [wide[:5], jnp.repeat(per_head[2], HEAD)[None], jnp.zeros((2, inner), f32)], axis=0
    )
    cb = jnp.pad(conv_bc.astype(f32), ((0, 3), (0, 0)))
    heads = jnp.pad(
        jnp.stack([per_head[1], jnp.exp(per_head[0])]), ((0, 6), (0, Q - heads_count))
    )

    w_s = jnp.concatenate([full_bc, full_dt[:, :128] + full_dt[:, 128:]], axis=1)
    x, cotangent, normed, normed_t, cot_t = ready
    xin = nn(normed, w_x).astype(b16)
    bd = nn(normed, w_s)
    blocks = tokens.shape[0] // Q
    started = list(scan_forward(xin, bd, cx, cb, heads, 0, blocks * 3 // 4, None))
    if quick:
        started[4], *mine_second = lax.optimization_barrier((started[4], *mine_second))
        other_second = [swap(part, 1, "tensor") for part in mine_second]
    ssd, held, pre, rates, ended = scan_forward(
        xin, bd, cx, cb, heads, blocks * 3 // 4, blocks - blocks * 3 // 4, started
    )
    if quick:
        other_second = lax.optimization_barrier((ended, *other_second))[1:]
        w_z, w_out_t = merge(where, mine_second, other_second, second_layout)
    mixed, dz, dssd, grad_norm = gate_both(ssd, normed, cotangent, w_z, w_out_t, gain_norm)
    scan = lambda base, count, before: list(
        scan_backward(dssd, xin, pre, bd, held, rates, cx, cb, heads, pick, base, count, before)
    )
    if quick:
        keep_out, send_out = pack_whole(where, cot_t, mixed)
        dz, keep_out, send_out = lax.optimization_barrier((dz, keep_out, send_out))
        parts_out = sum_tensor(keep_out, send_out)
        keep, send, sums = pack_whole(where, normed_t, dz, w_z)
        dssd, keep, send, parts_out = lax.optimization_barrier((dssd, keep, send, parts_out))
        parts = sum_tensor(keep, send)
        carry = scan(blocks * 3 // 4, blocks // 4, None)
        carry[2], parts, parts_out = lax.optimization_barrier((carry[2], parts, parts_out))
        early = sum_around(jnp.concatenate([parts, parts_out], axis=2), shard_rows)
        carry = scan(0, blocks * 3 // 4, carry)
        carry[0], carry[1], early = lax.optimization_barrier((carry[0], carry[1], early))
    else:
        early = scatter_plain(
            [nn(normed_t, dz).astype(b16), nn(cot_t, mixed).astype(b16)],
            ((0, 0, half, False), (1, 0, half, False)),
        )
        carry = scan(0, blocks, None)
    dxin, dbd, _, _, _, gx, gb, gh = carry
    if quick:
        keep, send, sums = pack_first(where, normed_t, dxin, dbd, w_x, w_s, sums)
        sums, keep, send = lax.optimization_barrier((sums, keep, send))
        parts_first = sum_tensor(keep, send)
        keep, send = pack_second(where, normed_t, dxin, w_x, sums, gx, gb, gh, grad_norm, gain_row)
        dxin, dz, mixed, keep, send, parts_first = lax.optimization_barrier(
            (dxin, dz, mixed, keep, send, parts_first)
        )
        parts_second = sum_tensor(keep, send)
        parts_first = sum_around(parts_first, shard_rows)
        early = early.reshape(2, 2, *early.shape[1:])
        early, near = early[:, 0], swap(early[:, 1], 4)
    grad_tokens = token_grads(dz, dxin, dbd, x, cotangent, w_z, w_x, w_s, gain_row)
    if quick:
        grad_tokens, mixed, parts_first, parts_second, early, near = lax.optimization_barrier(
            (grad_tokens, mixed, parts_first, parts_second, early, near)
        )
        second = sum_around(parts_second, shard_rows)
        early = plus(early, near)
        early = [early[0], swap(early[1], 8)]
        parts_first = parts_first.reshape(2, 2, *parts_first.shape[1:])
        first = plus(parts_first[:, 0], swap(parts_first[:, 1], 4))
        mixed, second, first = lax.optimization_barrier((mixed, second, first))
        first = [first[0], swap(first[1], 8)]
        second = along_z_parts(second)
    out = add_branch(mixed, x, w_out_t)
    if quick:
        z_out, bc_out, dt_out, cx_out, cb_out, alog, bias, skip, norm, pre_sum, w_out_grad = finish(
            where, early, first, second, pick[:half], model, half
        )
        return (
            out, grad_tokens, pre_sum, z_out, bc_out, dt_out.T,
            cx_out, cb_out, alog[0], bias[0], skip[0], norm, w_out_grad.T,
        )
    late = scatter_plain(
        [nn(normed_t, dxin).astype(b16), nn(normed_t, dbd).astype(b16)],
        ((0, 0, half, False), (1, 0, 2 * STATE + 128, True)),
    )
    dnormed = nt(dz, w_z) + nt(dxin, w_x) + nt(dbd, w_s)
    wide_x = x.astype(f32)
    scale = lax.rsqrt(jnp.mean(wide_x * wide_x, axis=1, keepdims=True) + epsilon)
    grad_pre = jnp.sum(dnormed * wide_x * scale, axis=0)
    lines = jnp.sum(gx.reshape(6, 8, inner), axis=1)
    lines, norm, convbc, rates, grad_pre = lax.psum(
        (lines, jnp.sum(grad_norm, axis=0), jnp.sum(gb.reshape(5, 8, 2 * STATE), axis=1), gh[:2], grad_pre), ("dp", "tensor")
    )

    def mine(vector, width):
        return lax.dynamic_slice_in_dim(vector, side * width, width, vector.ndim - 1)

    skip = jnp.sum(lines[5].reshape(heads_count, HEAD), axis=1)
    return (
        out,
        grad_tokens,
        grad_pre,
        jnp.stack([early[:, :half], late[:, :half]], axis=1),
        late[:, half : half + 2 * STATE],
        mine(late[:, half + 2 * STATE :], half_heads),
        mine(lines[:5], half),
        convbc,
        mine(rates[0], half_heads),
        mine(rates[1], half_heads),
        mine(skip, half_heads),
        mine(norm, half),
        early[:, half:].T,
    )


def solution(mesh):
    placed = (
        P(("dp", "tensor"), None),
        P(),
        P("dp", None, "tensor"),
        P("dp", None),
        P("dp", "tensor"),
        P(None, "tensor"),
        P(),
        P("tensor"),
        P("tensor"),
        P("tensor"),
        P("tensor"),
        P("tensor", "dp"),
        P(("dp", "tensor"), None),
    )
    return jax.shard_map(
        body,
        mesh=mesh,
        in_specs=placed,
        out_specs=(
            P(("dp", "tensor"), None),
            P(("dp", "tensor"), None),
            P(),
            P("dp", None, "tensor"),
            P("dp", None),
            P("dp", "tensor"),
            P(None, "tensor"),
            P(),
            P("tensor"),
            P("tensor"),
            P("tensor"),
            P("tensor"),
            P("tensor", "dp"),
        ),
        check_vma=False,
    )
```
